32 devices in a mesh: groups: 2 (over y), dp: 4 (over z), tensor: 4 (over x, core).
Axes of the slice: x: 2, y: 2, z: 4, core: 2. Of those that a mesh axis runs over, the one named last changes fastest.
Arguments:
- activations: bfloat16 [4096, 4096], P(('groups', 'dp'), 'tensor'), parts along dimension 0, may hold values from -6 to 6
- out_grads: bfloat16 [4096, 14336], P(('groups', 'dp'), 'tensor'), parts along dimension 0, may hold values from -6 to 6
- proj_in: bfloat16 [4096, 64], P('tensor'), may hold values from -0.09375 to 0.09375
- proj_out: bfloat16 [14336, 64], P('tensor'), may hold values from -0.046875 to 0.046875
- doc_lengths: int32 [8, 32], P(('groups', 'dp')), parts along dimension 0, may hold values from 1 to 48, 512 in all within a row
- doc_owner: int32 [256, 1], P(('groups', 'dp')), parts along dimension 0, may hold values from 0 to 3; in each aligned block of 32 rows (0 to 31, 32 to 63, ...) at most 16 rows name the same one
- query_grads: float32 [256, 4096], P(('groups', 'dp'), 'tensor'), parts along dimension 0, may hold values from -24 to 24
- query_ids: int32 [256], P('groups'), parts along dimension 0, may hold values from 0 to 127
Outputs:
- store: float32 [512, 4096], P(('groups', 'dp'), 'tensor'), parts along dimension 0
- scores: float32 [512, 128], P(('groups', 'dp')), parts along dimension 0
The draws below stay inside these ranges and needn't reach their ends.
There are 2 independent parts, one for each index of `groups`. The reference program is written for one: setup_inputs(seed, part) draws one part's arguments, and reference() takes and returns one part's arrays. A program takes and returns all parts, laid end to end along the dimension named above; an argument that names none is the same for every part. Nothing has to cross between parts.
Inputs may be any that keep to these rules, and one draw needn't show every extreme that they name: `doc_owner`: among the 32 documents of one index of dp no owner appears more than 16 times. `doc_lengths`: each row sums to 512; its largest entry is 48.
All inputs are finite; a program needn't handle non-finite values.
Results may differ from the reference program's by a relative error of at most 0.0003.
Values sent between devices are 32-bit elements; how exact they have to be, the bound alone decides.
No kernel may reach another device: no remote copies, remote signals or barrier semaphores. Data moves between devices by JAX's collectives and lax.ppermute only.
A program may use at most 64 MiB of HBM per device.

```python
import math
import jax
import jax.numpy as jnp
import numpy as np
from jax import lax

D = 4096
FF = 14336
K = 64
TOK_DEV = 512
DOCS_DEV = 32
QUERIES = 128
MOST_LEN = 48
CAP = 16
SHARDS = 4
TOKENS = 2048
DOCS = 128
QPOOL = 128
SLOTS = 256
N_DP = 4


def with_ends(result, own_key, least, high):
    longest = result.shape.index(max(result.shape))
    spots = []
    for shift in (0, 1):
        where = [jax.random.randint(jax.random.fold_in(own_key, axis), (), 0, length) for axis, length in enumerate(result.shape)]
        where[longest] = (where[longest] + shift) % result.shape[longest]
        spots.append(tuple(where))
    return result.at[spots[0]].set(least).at[spots[1]].set(high)


def steps_of(key, dims, split, least, top_value):
    loudness = 1.0
    for axis_at, shards_of in split:
        heights = jax.random.uniform(jax.random.fold_in(jax.random.fold_in(key, 6), axis_at), (shards_of,), jnp.float32, least / len(split), top_value / len(split))
        loudness = loudness * jnp.repeat(jnp.exp(heights), dims[axis_at] // shards_of).reshape((-1,) + (1,) * (len(dims) - 1 - axis_at))
    return loudness


def split_up(number_of, total, most, slope):
    loads = [(1 << 20) // math.isqrt(standing ** slope) + 1 for standing in range(2, number_of + 1)]
    rest, counts = total - most - (number_of - 1), [1] * (number_of - 1)
    while rest > 0:
        candidates = [i for i in range(number_of - 1) if counts[i] < most]
        whole, left = sum([loads[i] for i in candidates]), rest
        for i in candidates:
            more = min(most - counts[i], max(1, left * loads[i] // whole), rest)
            counts[i] = counts[i] + more
            rest = rest - more
    return np.array([most] + counts)


def ragged_sizes(stream_key, count, total, limit, lean):
    if count == 2:
        one = jax.random.randint(stream_key, (), max(1, total - limit), min(limit, total - 1) + 1)
        return jnp.stack([one, total - one])
    lengths = jnp.asarray(split_up(count, total, limit, lean), jnp.int32)
    pairs = (count - 1) // 2
    donor, sink = lengths[1:1 + 2 * pairs:2], lengths[2:2 + 2 * pairs:2]
    room = jnp.minimum(donor - 1, limit - sink)
    passed = jax.random.randint(jax.random.fold_in(stream_key, 1), (pairs,), 0, 1 << 20) % (room + 1)
    lengths = lengths.at[1:1 + 2 * pairs:2].set(donor - passed).at[2:2 + 2 * pairs:2].set(sink + passed)
    return lengths[jax.random.permutation(jax.random.fold_in(stream_key, 2), count)]


def assign_block(stream_key, own, number, rows, amount, top, most, slope):
    sequence = jax.random.permutation(stream_key, amount)
    crowded, ordinary = shares(amount, rows * top, most, slope, True), shares(amount, rows * top, most, slope, False)
    places = jnp.arange(amount)

    def named(sizes, turn):
        used = int((sizes > 0).sum())
        fixed = max(1, used // 4)
        moved = fixed + (places - fixed + turn * (used - fixed)) % max(1, amount - fixed)
        return jnp.zeros((amount,), jnp.int32).at[sequence[jnp.where(places < fixed, places, moved)]].set(jnp.asarray(sizes, jnp.int32))

    sizes = jnp.where(number % 4 == 0, named(crowded, number // 4), named(ordinary, number - number // 4 - 1))
    mixed = jax.random.permutation(jax.random.fold_in(own, 3), amount)
    donor, taker = mixed[0:amount // 2 * 2:2], mixed[1:amount // 2 * 2:2]
    margin = jnp.minimum(sizes[donor] - 1, most - sizes[taker]) // 2
    margin = jnp.where((donor == sequence[0]) | (taker == sequence[0]) | (sizes[taker] == 0), 0, jnp.maximum(margin, 0))
    moved = jax.random.randint(jax.random.fold_in(own, 4), (amount // 2,), 0, 1 << 20) % (margin + 1)
    sizes = sizes.at[donor].add(-moved).at[taker].add(moved)
    labels = jnp.searchsorted(jnp.cumsum(sizes), jnp.arange(rows * top), side="right").astype(jnp.int32)
    grid = labels.reshape(top, rows).T
    grid = grid[jax.random.permutation(jax.random.fold_in(own, 1), rows)]
    turn = jax.random.randint(jax.random.fold_in(own, 2), (rows, 1), 0, top)
    return jnp.take_along_axis(grid, (jnp.arange(top)[None, :] + turn) % top, axis=1)


def shares(number_of, total, most, skew, full):
    portions = [(1 << 20) // math.isqrt(standing ** skew) + 1 for standing in range(1, number_of + 1)]
    largest = most if full else min(most, max(-(-total // number_of), total * portions[0] // sum(portions)))
    least = 1 if total - largest >= number_of - 1 else 0
    holding, spare = [largest] + [least] * (number_of - 1), total - largest - least * (number_of - 1)
    while spare > 0:
        free = [i for i in range(1, number_of) if holding[i] < largest] or [i for i in range(1, number_of) if holding[i] < most]
        mass, budget = sum([portions[i] for i in free]), spare
        for i in free:
            addition = min(most - holding[i], max(1, budget * portions[i] // mass), spare)
            holding[i] = holding[i] + addition
            spare = spare - addition
    return np.array(holding)


def scatter_about(own_key, shape, width, most, pieces=(), kind=jnp.bfloat16):
    loudness = steps_of(own_key, shape, pieces, -0.22, 0.18) if pieces else 1.0
    array = jax.random.normal(own_key, shape, jnp.float32) * width * loudness
    return jnp.minimum(jnp.maximum(array, -most), most).astype(kind)


def setup_inputs(seed: int = 0, part: int = 0) -> dict:
    splits = jax.random.split(jax.random.key(seed), 9)
    own_keys = jax.random.split(jax.random.fold_in(splits[8], part), 9)
    activations = scatter_about(own_keys[0], (TOKENS, D), 1.0, 6.0, ((0, 4), (1, 4)))
    out_grads = scatter_about(own_keys[1], (TOKENS, FF), 1.0, 6.0, ((0, 4), (1, 4)))
    proj_in = scatter_about(splits[2], (D, K), D ** -0.5, 0.09375, ((0, 4),))
    proj_out = scatter_about(splits[3], (FF, K), FF ** -0.5, 0.046875, ((0, 4),))
    doc_lengths = jax.vmap(lambda own: ragged_sizes(own, DOCS_DEV, TOK_DEV, MOST_LEN, 2))(jax.random.split(own_keys[4], SHARDS)).reshape((SHARDS, DOCS_DEV)).astype(jnp.int32)
    doc_owner_keys = jax.random.split(jax.random.fold_in(own_keys[5], 1), DOCS // DOCS_DEV)
    doc_owner_turns = jax.random.permutation(jax.random.fold_in(own_keys[5], 3), DOCS // DOCS_DEV)
    doc_owner = jax.vmap(lambda own, number: assign_block(jax.random.fold_in(own_keys[5], 2), own, number, DOCS_DEV, N_DP, 1, CAP, 2))(doc_owner_keys, doc_owner_turns).reshape((DOCS, 1))
    query_grads = scatter_about(own_keys[6], (QPOOL, K * K), 4.0, 24.0, ((0, 4), (1, 4)), jnp.float32)
    query_ids = with_ends(jax.random.randint(own_keys[7], (QUERIES,), 0, QPOOL), jax.random.fold_in(own_keys[7], 1), 0, QPOOL - 1).astype(jnp.int32)
    return dict(activations=activations, out_grads=out_grads, proj_in=proj_in, proj_out=proj_out, doc_lengths=doc_lengths, doc_owner=doc_owner, query_grads=query_grads, query_ids=query_ids)


def token_docs(lengths_row, row_count, offset):
    doc_ends = jnp.cumsum(lengths_row, dtype=jnp.int32)
    position = offset + lax.iota(jnp.int32, row_count)
    doc_index = jnp.sum((position[:, None] >= doc_ends[None, :]).astype(jnp.int32), axis=1, dtype=jnp.int32)
    return (doc_index[:, None] == lax.iota(jnp.int32, doc_ends.shape[0])[None, :]).astype(jnp.float32)


def doc_outer(member, left_cols, right_cols):
    spread = (member[:, :, None] * left_cols[:, None, :]).reshape(member.shape[0], -1)
    product = lax.dot_general(spread, right_cols, (((0,), (0,)), ((), ())),
                              precision=lax.Precision.HIGHEST, preferred_element_type=jnp.float32)
    return product.reshape(member.shape[1], -1)


def reference(activations, out_grads, proj_in, proj_out, doc_lengths, doc_owner, query_grads, query_ids):
    x_proj = jnp.dot(activations, proj_in, preferred_element_type=jnp.float32)
    g_proj = jnp.dot(out_grads, proj_out, preferred_element_type=jnp.float32)

    def shard_grads(inputs):
        x_rows, g_rows, lengths_row = inputs
        member = token_docs(lengths_row, TOK_DEV, 0)
        return doc_outer(member, g_rows, x_rows)

    doc_grads = lax.map(shard_grads, (x_proj.reshape(SHARDS, TOK_DEV, K),
                                      g_proj.reshape(SHARDS, TOK_DEV, K), doc_lengths))
    doc_grads = doc_grads.reshape(DOCS, K * K)
    owner_grid = doc_owner.reshape(SHARDS, DOCS_DEV)
    owner_hot = (owner_grid[:, :, None] == lax.iota(jnp.int32, N_DP)[None, None, :]).astype(jnp.int32)
    before = jnp.cumsum(owner_hot, axis=1, dtype=jnp.int32) - owner_hot
    doc_rank = jnp.sum(before * owner_hot, axis=2, dtype=jnp.int32)
    source = lax.iota(jnp.int32, SHARDS)[:, None]
    doc_slot = (owner_grid * (N_DP * CAP) + source * CAP + doc_rank).reshape(DOCS).astype(jnp.int32)
    store = jnp.zeros((SLOTS, K * K), jnp.float32).at[doc_slot].set(doc_grads)
    queries = jnp.take(query_grads, query_ids, axis=0)
    scores = jnp.dot(store, queries.T, precision=lax.Precision.HIGHEST,
                     preferred_element_type=jnp.float32) * (1.0 / (K * K))
    return store, scores
```

```python
import functools

import jax
import jax.numpy as jnp
from jax import lax
from jax.experimental import pallas as pl
from jax.experimental.pallas import tpu as pltpu
from jax.sharding import PartitionSpec as P

F32 = jnp.float32
BF16 = jnp.bfloat16
MIB = 1024 * 1024
NT = (((1,), (1,)), ((), ()))
MOST_SHIFTS = 8


def params(mib):
    return pltpu.CompilerParams(vmem_limit_bytes=mib * MIB)


def cost(flops, nbytes):
    return pl.CostEstimate(flops=flops, bytes_accessed=nbytes, transcendentals=0)


def halves(x):
    high = x.astype(BF16)
    return high, (x - high.astype(F32)).astype(BF16)


def mm(a, b, dims=(((1,), (0,)), ((), ()))):
    return lax.dot_general(a, b, dims, preferred_element_type=F32)


def pick(parity, even, odd):
    return jnp.where(parity == 0, even, odd)


def x_kernel(act_ref, proj_ref, keep_ref, send_ref):
    parity = lax.rem(lax.axis_index("tensor"), 2)
    full = mm(act_ref[...], proj_ref[...], NT).T
    half = full.shape[0] // 2
    keep_ref[...] = pick(parity, full[:half], full[half:])
    send_ref[...] = pick(parity, full[half:], full[:half])


def g_kernel(width, act_ref, proj_ref, keep_ref, send_ref):
    parity = lax.rem(lax.axis_index("tensor"), 2)
    full = mm(act_ref[...], proj_ref[...], NT).T
    for i in range(full.shape[0] // (2 * width)):
        even = full[2 * i * width : (2 * i + 1) * width]
        odd = full[(2 * i + 1) * width : (2 * i + 2) * width]
        keep_ref[i * width : (i + 1) * width, :] = pick(parity, even, odd)
        send_ref[i * width : (i + 1) * width, :] = pick(parity, odd, even)


def project(kernel, act, proj_t, tile):
    tokens, depth = act.shape
    rank = proj_t.shape[0]
    out = jax.ShapeDtypeStruct((rank // 2, tokens), F32)
    spec = pl.BlockSpec((rank // 2, tile), lambda i: (0, i))
    return pl.pallas_call(
        kernel,
        grid=(tokens // tile,),
        in_specs=[
            pl.BlockSpec((tile, depth), lambda i: (i, 0)),
            pl.BlockSpec((rank, depth), lambda i: (0, 0)),
        ],
        out_specs=[spec, spec],
        out_shape=[out, out],
        compiler_params=params(24),
        cost_estimate=cost(8 * tokens * depth * rank, 2 * depth * (tokens + rank)),
    )(act, proj_t)


def mask_kernel(owners, relative, cap, lengths_ref, owner_ref, mask_ref):
    docs = lengths_ref.shape[1]
    slots, tokens = mask_ref.shape
    me = lax.axis_index("dp") if relative else 0
    row = lax.broadcasted_iota(jnp.int32, (docs, docs), 0)
    col = lax.broadcasted_iota(jnp.int32, (docs, docs), 1)
    len_row = lengths_ref[...].astype(F32)
    own_row = lax.rem(owner_ref[...] - me + owners, owners).astype(F32)

    def column(values):
        return jnp.sum(jnp.where(row == col, values, 0.0), axis=1, keepdims=True)

    ends = jnp.sum(jnp.where(row <= col, column(len_row), 0.0), axis=0, keepdims=True)
    rank = jnp.sum(
        jnp.where((row < col) & (column(own_row) == own_row), 1.0, 0.0), axis=0, keepdims=True
    )
    slot_row = own_row * cap + rank
    slot = lax.broadcasted_iota(jnp.int32, (slots, docs), 0).astype(F32)
    hot = slot == slot_row
    first = jnp.sum(jnp.where(hot, ends - len_row, 0.0), axis=1, keepdims=True)
    last = jnp.sum(jnp.where(hot, ends, 0.0), axis=1, keepdims=True)
    token = lax.broadcasted_iota(jnp.int32, (slots, tokens), 1).astype(F32)
    mask_ref[...] = jnp.where((token >= first) & (token < last), 1.0, 0.0)


def slot_mask(lengths, owner_row, tokens, owners, cap, relative):
    return pl.pallas_call(
        functools.partial(mask_kernel, owners, relative, cap),
        out_shape=jax.ShapeDtypeStruct((owners * cap, tokens), F32),
        cost_estimate=cost(0, 4 * owners * cap * tokens),
    )(lengths, owner_row)


def query_kernel(shards, *refs):
    ids_ref, pieces, out_ref = refs[0], refs[1:-1], refs[-1]
    queries = ids_ref.shape[1]
    me = lax.axis_index("dp")
    row = lax.broadcasted_iota(jnp.int32, (queries, queries), 0)
    col = lax.broadcasted_iota(jnp.int32, (queries, queries), 1)
    ids = jnp.sum(
        jnp.where(row == col, ids_ref[...].astype(F32), 0.0), axis=1, keepdims=True
    )
    high_sum, low_sum = None, None
    for k, piece in enumerate(pieces):
        rows = piece.shape[0]
        base = lax.rem(me - k + shards, shards) * rows if len(pieces) > 1 else 0
        place = (lax.broadcasted_iota(jnp.int32, (queries, rows), 1) + base).astype(F32)
        hot = jnp.where(ids == place, 1.0, 0.0).astype(BF16)
        high, low = halves(piece[...])
        high_part, low_part = mm(hot, high), mm(hot, low)
        high_sum = high_part if high_sum is None else high_sum + high_part
        low_sum = low_part if low_sum is None else low_sum + low_part
    out_ref[:queries, :] = high_sum.astype(BF16)
    out_ref[queries:, :] = low_sum.astype(BF16)


def pick_queries(ids_row, pieces, shards):
    queries, feats = ids_row.shape[1], pieces[0].shape[1]
    pool = pieces[0].shape[0] * len(pieces)
    return pl.pallas_call(
        functools.partial(query_kernel, shards),
        out_shape=jax.ShapeDtypeStruct((2 * queries, feats), BF16),
        compiler_params=params(24),
        cost_estimate=cost(4 * queries * pool * feats, 4 * pool * feats),
    )(ids_row, *pieces)


def outer_kernel(x_ref, g_ref, mask_ref, query_ref, *outs):
    *blocks, scores_ref = outs
    width = g_ref.shape[0]
    rank = x_ref.shape[0]
    slots = mask_ref.shape[0]
    queries = query_ref.shape[0] // 2
    x_high, x_low = halves(x_ref[...])
    x_both = jnp.concatenate([x_high, x_low], axis=0)
    g_high = g_ref[...].astype(BF16).astype(F32)
    g_low = g_ref[...] - g_high
    mask = mask_ref[...]

    def part(g, i):
        return (mask * g[i : i + 1, :]).astype(BF16)

    columns = []
    for i in range(width):
        both = mm(part(g_high, i), x_both, NT) + mm(part(g_low, i), x_both, NT)
        columns.append(both[:, :rank] + both[:, rank:])
    grads = jnp.concatenate(columns, axis=1)
    cap = blocks[0].shape[0]
    for k, block in enumerate(blocks):
        block[...] = grads[k * cap : (k + 1) * cap, :]
    high, low = halves(grads)
    query = query_ref[...]
    products = mm(jnp.concatenate([high, low], axis=0), query, NT)
    scores_ref[...] = (
        products[:slots, :queries] + products[:slots, queries:] + products[slots:, :queries]
    )


def outer(x_t, g_t, mask, query, owners):
    slots, tokens = mask.shape
    width, rank = g_t.shape[0], x_t.shape[0]
    queries = query.shape[0] // 2
    cap = slots // owners
    return pl.pallas_call(
        outer_kernel,
        out_shape=[jax.ShapeDtypeStruct((cap, width * rank), F32)] * owners
        + [jax.ShapeDtypeStruct((slots, queries), F32)],
        compiler_params=params(24),
        cost_estimate=cost(16 * slots * width * tokens * rank, 4 * slots * width * rank),
    )(x_t, g_t, mask, query)


def place_kernel(scale, *refs):
    ins, (store_ref, scores_ref) = refs[:-2], refs[-2:]
    count = len(ins) // 2
    me = lax.axis_index("dp")
    cap = ins[0].shape[0]
    for k in range(count):
        spot = pl.ds(pl.multiple_of(lax.rem(me - k + count, count) * cap, cap), cap)
        store_ref[spot, :] = ins[k][...]
        scores_ref[spot, :] = ins[count + k][...] * scale


def place(rows, scores, scale):
    slots = rows[0].shape[0] * len(rows)
    return pl.pallas_call(
        functools.partial(place_kernel, scale),
        out_shape=[
            jax.ShapeDtypeStruct((slots, rows[0].shape[1]), F32),
            jax.ShapeDtypeStruct((slots, scores[0].shape[1]), F32),
        ],
        compiler_params=params(16),
        cost_estimate=cost(0, 8 * slots * rows[0].shape[1]),
    )(*rows, *scores)


def flip(x, bit, size):
    return lax.ppermute(x, "tensor", [(i, i ^ bit) for i in range(size)])


def shift(x, by, size):
    return lax.ppermute(x, "dp", [(i, (i + by) % size) for i in range(size)])


def local(
    activations, out_grads, proj_in, proj_out, doc_lengths, doc_owner, query_grads, query_ids
):
    tensor_size = lax.axis_size("tensor")
    data_size = lax.axis_size("dp")
    tensor_pos = lax.axis_index("tensor")
    tokens = activations.shape[0]
    rank = proj_in.shape[1]
    width = rank // tensor_size
    docs = doc_owner.shape[0]
    cap = max(2, 2 * docs // data_size)
    direct = data_size <= MOST_SHIFTS

    if direct:
        pieces = [query_grads] + [shift(query_grads, k, data_size) for k in range(1, data_size)]
    else:
        pieces = [lax.all_gather(query_grads, "dp", axis=0, tiled=True)]

    x_keep, x_send = project(x_kernel, activations, proj_in.T, tokens)
    x_got = flip(x_send, 1, tensor_size)
    g_keep, g_send = project(
        functools.partial(g_kernel, width), out_grads, proj_out.T, tokens // 4
    )
    g_got = flip(g_send, 1, tensor_size)
    x_half = x_keep + x_got
    g_part = (g_keep + g_got).reshape(-1, width, tokens)
    bit = 2
    while bit < tensor_size:
        x_got = flip(x_half, bit, tensor_size)
        pairs = g_part.reshape(-1, 2, width, tokens)
        upper = (tensor_pos // bit) % 2
        mine = lax.dynamic_index_in_dim(pairs, upper, 1, keepdims=False)
        other = lax.dynamic_index_in_dim(pairs, 1 - upper, 1, keepdims=False)
        g_part = mine + flip(other, bit, tensor_size)
        x_half = x_half + x_got
        bit *= 2
    x_other = flip(x_half, 1, tensor_size)
    odd = (tensor_pos % 2) == 1
    x_full = jnp.concatenate(
        [jnp.where(odd, x_other, x_half), jnp.where(odd, x_half, x_other)], axis=0
    )
    g_mine = g_part.reshape(width, tokens)

    mask = slot_mask(doc_lengths, doc_owner.T, tokens, data_size, cap, direct)
    query = pick_queries(query_ids[None, :], pieces, data_size)
    *blocks, partial = outer(x_full, g_mine, mask, query, data_size)
    scale = 1.0 / (rank * rank)
    if direct:
        rows = [blocks[0]] + [shift(blocks[k], k, data_size) for k in range(1, data_size)]
        bit = 1
        while bit < tensor_size:
            partial = partial + flip(partial, bit, tensor_size)
            bit *= 2
        scored = [partial[k * cap : (k + 1) * cap] for k in range(data_size)]
        scored = [scored[0]] + [shift(scored[k], k, data_size) for k in range(1, data_size)]
        store, scores = place(rows, scored, scale)
        return store, scores
    rows = lax.all_to_all(jnp.stack(blocks), "dp", split_axis=0, concat_axis=0, tiled=True)
    summed = lax.psum(partial, "tensor").reshape(data_size, cap, -1)
    scores = lax.all_to_all(summed, "dp", split_axis=0, concat_axis=0, tiled=True)
    slots = data_size * cap
    return rows.reshape(slots, -1), scores.reshape(slots, -1) * scale


def solution(mesh):
    return jax.shard_map(
        local,
        mesh=mesh,
        in_specs=(
            P(("groups", "dp"), "tensor"),
            P(("groups", "dp"), "tensor"),
            P("tensor", None),
            P("tensor", None),
            P(("groups", "dp"), None),
            P(("groups", "dp"), None),
            P(("groups", "dp"), "tensor"),
            P("groups"),
        ),
        out_specs=(P(("groups", "dp"), "tensor"), P(("groups", "dp"), None)),
        check_vma=False,
    )
```

```python
import functools

import jax
import jax.numpy as jnp
from jax import lax
from jax.experimental import pallas as pl
from jax.experimental.pallas import tpu as pltpu
from jax.sharding import PartitionSpec as P

F32 = jnp.float32
BF16 = jnp.bfloat16
MIB = 1024 * 1024
NT = (((1,), (1,)), ((), ()))
MOST_DIRECT = 8
TILES = 4


def params(mib):
    return pltpu.CompilerParams(vmem_limit_bytes=mib * MIB)


def cost(flops, nbytes):
    return pl.CostEstimate(flops=flops, bytes_accessed=nbytes, transcendentals=0)


def halves(x):
    high = x.astype(BF16)
    return high, (x - high.astype(F32)).astype(BF16)


def mm(a, b, dims=(((1,), (0,)), ((), ()))):
    return lax.dot_general(a, b, dims, preferred_element_type=F32)


def copies(pairs, sems):
    made = [pltpu.make_async_copy(src, dst, sems.at[i]) for i, (src, dst) in enumerate(pairs)]
    for copy in made:
        copy.start()
    return made


def slot_mask(owners, relative, cap, lengths, owner, slots, tokens):
    docs = lengths.shape[1]
    row = lax.broadcasted_iota(jnp.int32, (docs, docs), 0)
    col = lax.broadcasted_iota(jnp.int32, (docs, docs), 1)
    len_row = lengths.astype(F32)
    place_row = owner ^ lax.axis_index("dp") if relative else owner
    own_row = place_row.astype(F32)

    def column(values):
        return jnp.sum(jnp.where(row == col, values, 0.0), axis=1, keepdims=True)

    ends = jnp.sum(jnp.where(row <= col, column(len_row), 0.0), axis=0, keepdims=True)
    rank = jnp.sum(
        jnp.where((row < col) & (column(own_row) == own_row), 1.0, 0.0), axis=0, keepdims=True
    )
    slot = lax.broadcasted_iota(jnp.int32, (slots, docs), 0).astype(F32)
    hot = slot == own_row * cap + rank
    first = jnp.sum(jnp.where(hot, ends - len_row, 0.0), axis=1, keepdims=True)
    last = jnp.sum(jnp.where(hot, ends, 0.0), axis=1, keepdims=True)
    token = lax.broadcasted_iota(jnp.int32, (slots, tokens), 1).astype(F32)
    return jnp.where((token >= first) & (token < last), 1.0, 0.0)


def project_kernel(
    owners, relative, cap, width, act_hbm, grad_hbm, in_hbm, out_hbm, len_hbm, own_hbm,
    keep_ref, send_ref, mask_ref, act, grad, proj_in, proj_out, lens, owner, turned, sems,
):
    tokens = act.shape[0]
    rank = proj_in.shape[0]
    half = rank // 2
    tile = tokens // TILES
    tiles = [pl.ds(i * tile, tile) for i in range(TILES)]
    pairs = [(len_hbm, lens), (own_hbm, owner), (in_hbm, proj_in), (act_hbm, act)]
    pairs += [(out_hbm, proj_out)]
    pairs += [(grad_hbm.at[t, :], grad.at[t, :]) for t in tiles]
    made = copies(pairs, sems)
    made[0].wait()
    made[1].wait()
    mask_ref[...] = slot_mask(
        owners, relative, cap, lens[...], owner[...], mask_ref.shape[0], tokens
    )
    me = lax.axis_index("tensor")
    parity = lax.rem(me, 2)
    made[2].wait()
    made[3].wait()
    x_t = mm(act[...], proj_in[...], NT).T
    keep_ref[:half, :] = jnp.where(parity == 0, x_t[:half], x_t[half:])
    send_ref[:half, :] = jnp.where(parity == 0, x_t[half:], x_t[:half])
    made[4].wait()
    for i, t in enumerate(tiles):
        made[5 + i].wait()
        turned[:, t] = mm(grad[t, :], proj_out[...], NT).T
    spot = half
    for apart in range(rank // width - 2, -1, -2):
        for ref, who in ((keep_ref, me ^ apart), (send_ref, me ^ (apart ^ 1))):
            block = pl.ds(pl.multiple_of(who * width, width), width)
            ref[spot : spot + width, :] = turned[block, :]
        spot += width


def project(act, grad, in_t, out_t, lengths, owner_row, owners, cap, width, relative):
    tokens, rank = act.shape[0], in_t.shape[0]
    depth = act.shape[1] + grad.shape[1]
    part = jax.ShapeDtypeStruct((rank, tokens), F32)
    hbm = pl.BlockSpec(memory_space=pl.ANY)
    vmem = pl.BlockSpec(memory_space=pltpu.VMEM)
    return pl.pallas_call(
        functools.partial(project_kernel, owners, relative, cap, width),
        in_specs=[hbm] * 6,
        out_specs=[vmem] * 3,
        out_shape=[part, part, jax.ShapeDtypeStruct((owners * cap, tokens), F32)],
        scratch_shapes=[
            pltpu.VMEM(act.shape, BF16),
            pltpu.VMEM(grad.shape, BF16),
            pltpu.VMEM(in_t.shape, BF16),
            pltpu.VMEM(out_t.shape, BF16),
            pltpu.VMEM(lengths.shape, jnp.int32),
            pltpu.VMEM(owner_row.shape, jnp.int32),
            pltpu.VMEM((rank, tokens), F32),
            pltpu.SemaphoreType.DMA((5 + TILES,)),
        ],
        compiler_params=params(24),
        cost_estimate=cost(2 * tokens * depth * rank, 2 * depth * (tokens + rank)),
    )(
        *(
            pltpu.with_memory_space_constraint(x, pltpu.HBM)
            for x in (act, grad, in_t, out_t, lengths, owner_row)
        )
    )


def outer_kernel(x_ref, x_other_ref, g_ref, mask_ref, *blocks):
    width = g_ref.shape[0]
    rank = 2 * x_ref.shape[0]
    odd = lax.rem(lax.axis_index("tensor"), 2) == 1
    own, other = x_ref[...], x_other_ref[...]
    x_full = jnp.concatenate([jnp.where(odd, other, own), jnp.where(odd, own, other)], axis=0)
    x_both = jnp.concatenate(halves(x_full), axis=0)
    g_high = g_ref[...].astype(BF16).astype(F32)
    g_low = g_ref[...] - g_high
    mask = mask_ref[...]
    cap = blocks[0].shape[0]

    def product(i):
        total = None
        for g in (g_high, g_low):
            term = mm((mask * g[i : i + 1, :]).astype(BF16), x_both, NT)
            total = term if total is None else total + term
        return total[:, :rank] + total[:, rank:]

    step = max(1, 128 // rank)
    for i in range(0, width, step):
        columns = jnp.concatenate([product(i + j) for j in range(step)], axis=1)
        for k, block in enumerate(blocks):
            block[:, i * rank : (i + step) * rank] = columns[k * cap : (k + 1) * cap, :]


def outer(x_half, x_other, g_t, mask, owners):
    slots, tokens = mask.shape
    width, rank = g_t.shape[0], 2 * x_half.shape[0]
    cap = slots // owners
    return pl.pallas_call(
        outer_kernel,
        out_shape=[jax.ShapeDtypeStruct((cap, width * rank), F32)] * owners,
        compiler_params=params(24),
        cost_estimate=cost(8 * slots * width * tokens * rank, 4 * slots * width * rank),
    )(x_half, x_other, g_t, mask)


def score_kernel(count, early, size, gaps, relative, ids_ref, *refs):
    rows, pieces, scores_ref = refs[:count], refs[count:-1], refs[-1]
    queries = ids_ref.shape[1]
    me = lax.axis_index("dp")
    cap = rows[0].shape[0]
    high, low = halves(jnp.concatenate([r[:cap, :] for r in rows], axis=0))
    slots = high.shape[0]
    both = jnp.concatenate([high, low], axis=0)
    parts = [piece[...] for piece in pieces]
    parts += [rows[1][cap + i * size : cap + (i + 1) * size, :] for i in range(len(gaps) - early)]
    total = None
    for gap, piece in zip(gaps, parts):
        held = piece.shape[0]
        products = mm(both, jnp.concatenate(halves(piece), axis=0), NT)
        part = products[:slots, :held] + products[:slots, held:] + products[slots:, :held]
        base = (me ^ gap) * held if len(gaps) > 1 else 0
        place = lax.broadcasted_iota(jnp.int32, (held, queries), 0) + base
        hot = jnp.where(place == ids_ref[...], 1.0, 0.0).astype(BF16)
        top, rest = halves(part)
        last = (part - top.astype(F32) - rest.astype(F32)).astype(BF16)
        for term in (top, rest, last):
            picked = mm(term, hot)
            total = picked if total is None else total + picked
    for k in range(count):
        spot = pl.ds(pl.multiple_of((me ^ k) * cap, cap), cap) if relative else pl.ds(k * cap, cap)
        scores_ref[spot, :] = total[k * cap : (k + 1) * cap, :]


def score(ids_row, rows, pieces, gaps, relative):
    slots = rows[0].shape[0] * len(rows)
    queries = ids_row.shape[1]
    size, feats = pieces[0].shape
    flops = 6 * slots * size * len(gaps) * feats
    return pl.pallas_call(
        functools.partial(score_kernel, len(rows), len(pieces), size, gaps, relative),
        out_shape=jax.ShapeDtypeStruct((slots, queries), F32),
        compiler_params=params(24),
        cost_estimate=cost(flops, 4 * size * len(gaps) * feats),
    )(ids_row, *rows, *pieces)


def place_kernel(*refs):
    rows, store_ref = refs[:-1], refs[-1]
    me = lax.axis_index("dp")
    cap = rows[0].shape[0]
    for k, row in enumerate(rows):
        store_ref[pl.ds(pl.multiple_of((me ^ k) * cap, cap), cap), :] = row[:cap, :]


def place(rows):
    slots, feats = rows[0].shape[0] * len(rows), rows[0].shape[1]
    return pl.pallas_call(
        place_kernel,
        out_shape=jax.ShapeDtypeStruct((slots, feats), F32),
        compiler_params=params(16),
        cost_estimate=cost(0, 8 * slots * feats),
    )(*rows)


def swap(x, axis, gap):
    return lax.ppermute(x, axis, [(i, i ^ gap) for i in range(lax.axis_size(axis))])


def gather_pieces(piece):
    pieces, gaps = [piece], [0]
    bit = lax.axis_size("dp") // 2
    while bit > 1:
        pieces, gaps = pieces + [swap(p, "dp", bit) for p in pieces], gaps + [g ^ bit for g in gaps]
        bit //= 2
    return pieces, gaps


def local(
    activations, out_grads, proj_in, proj_out, doc_lengths, doc_owner, query_grads, query_ids
):
    tensor_size = lax.axis_size("tensor")
    data_size = lax.axis_size("dp")
    tokens = activations.shape[0]
    rank = proj_in.shape[1]
    half = rank // 2
    width = rank // tensor_size
    docs = doc_owner.shape[0]
    cap = max(2, 2 * docs // data_size)
    direct = data_size <= MOST_DIRECT

    if direct:
        pieces, gaps = gather_pieces(query_grads)
        mate = swap(query_grads, "dp", 1)
    else:
        pieces, gaps = [lax.all_gather(query_grads, "dp", axis=0, tiled=True)], [0]

    keep, send, mask = project(
        activations, out_grads, proj_in.T, proj_out.T, doc_lengths, doc_owner.T,
        data_size, cap, width, direct,
    )
    part = keep + swap(send, "tensor", 1)
    bit = tensor_size // 2
    while bit > 1:
        cut = half + (part.shape[0] - half) // 2
        got = swap(part[:cut], "tensor", bit)
        part = jnp.concatenate([part[:half] + got[:half], part[cut:] + got[half:]], axis=0)
        bit //= 2
    x_half, g_mine = part[:half], part[half:]
    x_other = swap(x_half, "tensor", 1)
    blocks = outer(x_half, x_other, g_mine, mask, data_size)
    if direct:
        near = swap(jnp.concatenate([blocks[1], *pieces[1:]], axis=0), "dp", 1)
        far = [swap(blocks[k], "dp", k) for k in range(2, data_size)]
        rows = [blocks[0], near, *far]
        pieces, gaps = [*pieces, mate], [*gaps, 1, *(g ^ 1 for g in gaps[1:])]
        store = place(rows)
    else:
        rows = [lax.all_to_all(jnp.stack(blocks), "dp", 0, 0, tiled=True).reshape(-1, width * rank)]
        store = rows[0]
    scores = score(query_ids[None, :], rows, pieces, gaps, direct)
    bit = 1
    while bit < tensor_size:
        scores = scores + swap(scores, "tensor", bit)
        bit *= 2
    return store, scores * (1.0 / (rank * rank))


def solution(mesh):
    return jax.shard_map(
        local,
        mesh=mesh,
        in_specs=(
            P(("groups", "dp"), "tensor"),
            P(("groups", "dp"), "tensor"),
            P("tensor", None),
            P("tensor", None),
            P(("groups", "dp"), None),
            P(("groups", "dp"), None),
            P(("groups", "dp"), "tensor"),
            P("groups"),
        ),
        out_specs=(P(("groups", "dp"), "tensor"), P(("groups", "dp"), None)),
        check_vma=False,
    )
```

```python
import functools

import jax
import jax.numpy as jnp
from jax import lax
from jax.experimental import pallas as pl
from jax.experimental.pallas import tpu as pltpu
from jax.sharding import PartitionSpec as P

F32 = jnp.float32
BF16 = jnp.bfloat16
MIB = 1024 * 1024
NT = (((1,), (1,)), ((), ()))
MOST_DIRECT = 8
CHUNKS = 2


def params(mib):
    return pltpu.CompilerParams(vmem_limit_bytes=mib * MIB)


def cost(flops, nbytes):
    return pl.CostEstimate(flops=flops, bytes_accessed=nbytes, transcendentals=0)


def halves(x):
    high = x.astype(BF16)
    return high, (x - high.astype(F32)).astype(BF16)


def mm(a, b, dims=(((1,), (0,)), ((), ()))):
    return lax.dot_general(a, b, dims, preferred_element_type=F32)


def copies(pairs, sems):
    made = [pltpu.make_async_copy(src, dst, sems.at[i]) for i, (src, dst) in enumerate(pairs)]
    for copy in made:
        copy.start()
    return made


def slot_mask(owners, relative, cap, lengths, owner, slots, tokens):
    docs = lengths.shape[1]
    row = lax.broadcasted_iota(jnp.int32, (docs, docs), 0)
    col = lax.broadcasted_iota(jnp.int32, (docs, docs), 1)
    len_row = lengths.astype(F32)
    place_row = owner ^ lax.axis_index("dp") if relative else owner
    own_row = place_row.astype(F32)

    def column(values):
        return jnp.sum(jnp.where(row == col, values, 0.0), axis=1, keepdims=True)

    ends = jnp.sum(jnp.where(row <= col, column(len_row), 0.0), axis=0, keepdims=True)
    rank = jnp.sum(
        jnp.where((row < col) & (column(own_row) == own_row), 1.0, 0.0), axis=0, keepdims=True
    )
    slot = lax.broadcasted_iota(jnp.int32, (slots, docs), 0).astype(F32)
    hot = slot == own_row * cap + rank
    first = jnp.sum(jnp.where(hot, ends - len_row, 0.0), axis=1, keepdims=True)
    last = jnp.sum(jnp.where(hot, ends, 0.0), axis=1, keepdims=True)
    token = lax.broadcasted_iota(jnp.int32, (slots, tokens), 1).astype(F32)
    return jnp.where((token >= first) & (token < last), 1.0, 0.0)


def project_kernel(
    owners, relative, cap, width, act_hbm, grad_hbm, in_hbm, out_hbm, len_hbm, own_hbm,
    keep_ref, send_ref, mask_ref, act, grad, proj_in, proj_out, lens, owner, turned, sems,
):
    tokens = act.shape[0]
    rank = proj_in.shape[0]
    half = rank // 2
    chunk = grad.shape[1] // CHUNKS
    chunks = [pl.ds(i * chunk, chunk) for i in range(CHUNKS)]
    pairs = [(in_hbm, proj_in), (act_hbm, act), (out_hbm, proj_out)]
    pairs += [(grad_hbm.at[:, c], grad.at[:, c]) for c in chunks]
    pairs += [(len_hbm, lens), (own_hbm, owner)]
    in_copy, act_copy, out_copy, *grad_copies, len_copy, own_copy = copies(pairs, sems)
    me = lax.axis_index("tensor")
    parity = lax.rem(me, 2)
    in_copy.wait()
    act_copy.wait()
    x_t = mm(act[...], proj_in[...], NT).T
    keep_ref[:half, :] = jnp.where(parity == 0, x_t[:half], x_t[half:])
    send_ref[:half, :] = jnp.where(parity == 0, x_t[half:], x_t[:half])
    len_copy.wait()
    own_copy.wait()
    mask_ref[...] = slot_mask(
        owners, relative, cap, lens[...], owner[...], mask_ref.shape[0], tokens
    )
    out_copy.wait()
    total = None
    for c, copy in zip(chunks, grad_copies):
        copy.wait()
        term = mm(grad[:, c], proj_out[:, c], NT)
        total = term if total is None else total + term
    turned[...] = total.T
    spot = half
    for apart in range(rank // width - 2, -1, -2):
        for ref, who in ((keep_ref, me ^ apart), (send_ref, me ^ (apart ^ 1))):
            block = pl.ds(pl.multiple_of(who * width, width), width)
            ref[spot : spot + width, :] = turned[block, :]
        spot += width


def project(act, grad, in_t, out_t, lengths, owner_row, owners, cap, width, relative):
    tokens, rank = act.shape[0], in_t.shape[0]
    depth = act.shape[1] + grad.shape[1]
    part = jax.ShapeDtypeStruct((rank, tokens), F32)
    hbm = pl.BlockSpec(memory_space=pl.ANY)
    vmem = pl.BlockSpec(memory_space=pltpu.VMEM)
    return pl.pallas_call(
        functools.partial(project_kernel, owners, relative, cap, width),
        in_specs=[hbm] * 6,
        out_specs=[vmem] * 3,
        out_shape=[part, part, jax.ShapeDtypeStruct((owners * cap, tokens), F32)],
        scratch_shapes=[
            pltpu.VMEM(act.shape, BF16),
            pltpu.VMEM(grad.shape, BF16),
            pltpu.VMEM(in_t.shape, BF16),
            pltpu.VMEM(out_t.shape, BF16),
            pltpu.VMEM(lengths.shape, jnp.int32),
            pltpu.VMEM(owner_row.shape, jnp.int32),
            pltpu.VMEM((rank, tokens), F32),
            pltpu.SemaphoreType.DMA((5 + CHUNKS,)),
        ],
        compiler_params=params(24),
        cost_estimate=cost(2 * tokens * depth * rank, 2 * depth * (tokens + rank)),
    )(
        *(
            pltpu.with_memory_space_constraint(x, pltpu.HBM)
            for x in (act, grad, in_t, out_t, lengths, owner_row)
        )
    )


def outer_kernel(x_ref, x_other_ref, g_ref, mask_ref, *blocks):
    width = g_ref.shape[0]
    rank = 2 * x_ref.shape[0]
    odd = lax.rem(lax.axis_index("tensor"), 2) == 1
    own, other = x_ref[...], x_other_ref[...]
    x_full = jnp.concatenate([jnp.where(odd, other, own), jnp.where(odd, own, other)], axis=0)
    x_both = jnp.concatenate(halves(x_full), axis=0)
    g_high = g_ref[...].astype(BF16).astype(F32)
    g_low = g_ref[...] - g_high
    mask = mask_ref[...]
    cap = blocks[0].shape[0]

    def product(i):
        pair = [(mask * g[i : i + 1, :]).astype(BF16) for g in (g_high, g_low)]
        both = mm(jnp.concatenate(pair, axis=0), x_both, NT)
        slots = mask.shape[0]
        return both[:slots, :rank] + both[:slots, rank:] + both[slots:, :rank]

    step = max(1, 128 // rank)
    for i in range(0, width, step):
        columns = jnp.concatenate([product(i + j) for j in range(step)], axis=1)
        for k, block in enumerate(blocks):
            block[:, i * rank : (i + step) * rank] = columns[k * cap : (k + 1) * cap, :]


def outer(x_half, x_other, g_t, mask, owners):
    slots, tokens = mask.shape
    width, rank = g_t.shape[0], 2 * x_half.shape[0]
    cap = slots // owners
    return pl.pallas_call(
        outer_kernel,
        out_shape=[jax.ShapeDtypeStruct((cap, width * rank), F32)] * owners,
        compiler_params=params(24),
        cost_estimate=cost(0, 0),
    )(x_half, x_other, g_t, mask)


def join_kernel(block_ref, *refs):
    *pieces, _, joined_ref, _ = refs
    cap = block_ref.shape[0]
    joined_ref[:cap, :] = block_ref[...]
    for i, piece in enumerate(pieces):
        size = piece.shape[0]
        joined_ref[cap + i * size : cap + (i + 1) * size, :] = piece[...]


def join(block, pieces, mate):
    rows = block.shape[0] + sum(p.shape[0] for p in pieces)
    vmem = pl.BlockSpec(memory_space=pltpu.VMEM)
    anywhere = pl.BlockSpec(memory_space=pl.ANY)
    return pl.pallas_call(
        join_kernel,
        in_specs=[vmem] * (1 + len(pieces)) + [anywhere],
        out_specs=[vmem, anywhere],
        out_shape=[
            jax.ShapeDtypeStruct((rows, block.shape[1]), F32),
            jax.ShapeDtypeStruct(mate.shape, mate.dtype),
        ],
        input_output_aliases={1 + len(pieces): 1},
        compiler_params=params(16),
        cost_estimate=cost(0, 0),
    )(block, *pieces, mate)


def score_kernel(count, early, size, gaps, relative, ids_ref, *refs):
    rows, pieces, scores_ref = refs[:count], refs[count:-1], refs[-1]
    queries = ids_ref.shape[1]
    me = lax.axis_index("dp")
    cap = rows[0].shape[0]
    high, low = halves(jnp.concatenate([r[:cap, :] for r in rows], axis=0))
    slots = high.shape[0]
    both = jnp.concatenate([high, low], axis=0)
    parts = [piece[...] for piece in pieces]
    parts += [rows[1][cap + i * size : cap + (i + 1) * size, :] for i in range(len(gaps) - early)]
    held = parts[0].shape[0]
    pool = jnp.concatenate(parts, axis=0)
    products = mm(both, jnp.concatenate(halves(pool), axis=0), NT)
    split = pool.shape[0]
    part = products[:slots, :split] + products[:slots, split:] + products[slots:, :split]
    row = lax.broadcasted_iota(jnp.int32, (held, queries), 0)
    places = [row + ((me ^ gap) * held if len(gaps) > 1 else 0) for gap in gaps]
    hot = (jnp.concatenate(places, axis=0) == ids_ref[...]).astype(F32).astype(BF16)
    top, rest = halves(part)
    last = (part - top.astype(F32) - rest.astype(F32)).astype(BF16)
    picked = mm(jnp.concatenate([top, rest, last], axis=0), hot)
    total = picked[:slots] + picked[slots : 2 * slots] + picked[2 * slots :]
    for k in range(count):
        spot = pl.ds(pl.multiple_of((me ^ k) * cap, cap), cap) if relative else pl.ds(k * cap, cap)
        scores_ref[spot, :] = total[k * cap : (k + 1) * cap, :]


def score(ids_row, rows, pieces, gaps, relative):
    slots = rows[0].shape[0] * len(rows)
    queries = ids_row.shape[1]
    size, feats = pieces[0].shape
    flops = 6 * slots * size * len(gaps) * feats
    return pl.pallas_call(
        functools.partial(score_kernel, len(rows), len(pieces), size, gaps, relative),
        out_shape=jax.ShapeDtypeStruct((slots, queries), F32),
        compiler_params=params(24),
        cost_estimate=cost(flops, 4 * size * len(gaps) * feats),
    )(ids_row, *rows, *pieces)


def place_kernel(*refs):
    rows, store_ref = refs[:-1], refs[-1]
    me = lax.axis_index("dp")
    cap = rows[0].shape[0]
    for k, row in enumerate(rows):
        store_ref[pl.ds(pl.multiple_of((me ^ k) * cap, cap), cap), :] = row[:cap, :]


def place(rows):
    slots, feats = rows[0].shape[0] * len(rows), rows[0].shape[1]
    return pl.pallas_call(
        place_kernel,
        out_shape=jax.ShapeDtypeStruct((slots, feats), F32),
        compiler_params=params(16),
        cost_estimate=cost(0, 8 * slots * feats),
    )(*rows)


def swap(x, axis, gap):
    return lax.ppermute(x, axis, [(i, i ^ gap) for i in range(lax.axis_size(axis))])


def gather_pieces(piece):
    pieces, gaps = [piece], [0]
    bit = lax.axis_size("dp") // 2
    while bit > 1:
        pieces, gaps = pieces + [swap(p, "dp", bit) for p in pieces], gaps + [g ^ bit for g in gaps]
        bit //= 2
    return pieces, gaps


def local(
    activations, out_grads, proj_in, proj_out, doc_lengths, doc_owner, query_grads, query_ids
):
    tensor_size = lax.axis_size("tensor")
    data_size = lax.axis_size("dp")
    tokens = activations.shape[0]
    rank = proj_in.shape[1]
    half = rank // 2
    width = rank // tensor_size
    docs = doc_owner.shape[0]
    cap = max(2, 2 * docs // data_size)
    direct = data_size <= MOST_DIRECT

    if direct:
        pieces, gaps = gather_pieces(query_grads)
        mate = swap(query_grads, "dp", 1)
    else:
        pieces, gaps = [lax.all_gather(query_grads, "dp", axis=0, tiled=True)], [0]

    keep, send, mask = project(
        activations, out_grads, proj_in.T, proj_out.T, doc_lengths, doc_owner.T,
        data_size, cap, width, direct,
    )
    part = keep + swap(send, "tensor", 1)
    bit = tensor_size // 2
    while bit > 1:
        cut = half + (part.shape[0] - half) // 2
        got = swap(part[:cut], "tensor", bit)
        part = jnp.concatenate([part[:half] + got[:half], part[cut:] + got[half:]], axis=0)
        bit //= 2
    x_half, g_mine = part[:half], part[half:]
    x_other = swap(x_half, "tensor", 1)
    blocks = outer(x_half, x_other, g_mine, mask, data_size)
    if direct:
        joined, mate = join(blocks[1], pieces[1:], mate)
        near = swap(joined, "dp", 1)
        far = [swap(blocks[k], "dp", k) for k in range(2, data_size)]
        rows = [blocks[0], near, *far]
        pieces, gaps = [*pieces, mate], [*gaps, 1, *(g ^ 1 for g in gaps[1:])]
        store = place(rows)
    else:
        rows = [lax.all_to_all(jnp.stack(blocks), "dp", 0, 0, tiled=True).reshape(-1, width * rank)]
        store = rows[0]
    scores = score(query_ids[None, :], rows, pieces, gaps, direct)
    bit = 1
    while bit < tensor_size:
        scores = scores + swap(scores, "tensor", bit)
        bit *= 2
    return store, scores * (1.0 / (rank * rank))


def solution(mesh):
    return jax.shard_map(
        local,
        mesh=mesh,
        in_specs=(
            P(("groups", "dp"), "tensor"),
            P(("groups", "dp"), "tensor"),
            P("tensor", None),
            P("tensor", None),
            P(("groups", "dp"), None),
            P(("groups", "dp"), None),
            P(("groups", "dp"), "tensor"),
            P("groups"),
        ),
        out_specs=(P(("groups", "dp"), "tensor"), P(("groups", "dp"), None)),
        check_vma=False,
    )
```

```python
import functools

import jax
import jax.numpy as jnp
from jax import lax
from jax.experimental import pallas as pl
from jax.experimental.pallas import tpu as pltpu
from jax.sharding import PartitionSpec as P

F32 = jnp.float32
BF16 = jnp.bfloat16
MIB = 1024 * 1024
NT = (((1,), (1,)), ((), ()))
MOST_DIRECT = 8
CHUNKS = 2


def params(mib):
    return pltpu.CompilerParams(vmem_limit_bytes=mib * MIB)


def cost(flops, nbytes):
    return pl.CostEstimate(flops=flops, bytes_accessed=nbytes, transcendentals=0)


def halves(x):
    high = x.astype(BF16)
    return high, (x - high.astype(F32)).astype(BF16)


def mm(a, b, dims=(((1,), (0,)), ((), ()))):
    return lax.dot_general(a, b, dims, preferred_element_type=F32)


def copies(pairs, sems):
    made = [pltpu.make_async_copy(src, dst, sems.at[i]) for i, (src, dst) in enumerate(pairs)]
    for copy in made:
        copy.start()
    return made


def slot_mask(owners, relative, cap, lengths, owner, slots, tokens):
    docs = lengths.shape[1]
    row = lax.broadcasted_iota(jnp.int32, (docs, docs), 0)
    col = lax.broadcasted_iota(jnp.int32, (docs, docs), 1)
    len_row = lengths.astype(F32)
    place_row = owner ^ lax.axis_index("dp") if relative else owner
    own_row = place_row.astype(F32)

    def column(values):
        return jnp.sum(jnp.where(row == col, values, 0.0), axis=1, keepdims=True)

    ends = jnp.sum(jnp.where(row <= col, column(len_row), 0.0), axis=0, keepdims=True)
    rank = jnp.sum(
        jnp.where((row < col) & (column(own_row) == own_row), 1.0, 0.0), axis=0, keepdims=True
    )
    slot = lax.broadcasted_iota(jnp.int32, (slots, docs), 0).astype(F32)
    hot = slot == own_row * cap + rank
    first = jnp.sum(jnp.where(hot, ends - len_row, 0.0), axis=1, keepdims=True)
    last = jnp.sum(jnp.where(hot, ends, 0.0), axis=1, keepdims=True)
    token = lax.broadcasted_iota(jnp.int32, (slots, tokens), 1).astype(F32)
    return jnp.where((token >= first) & (token < last), 1.0, 0.0)


def project_kernel(
    owners, relative, cap, width, act_hbm, grad_hbm, in_hbm, out_hbm, len_hbm, own_hbm,
    keep_ref, send_ref, mask_ref, act, grad, proj_in, proj_out, lens, owner, turned, sems,
):
    tokens = act.shape[0]
    rank = proj_in.shape[0]
    half = rank // 2
    chunk = grad.shape[1] // CHUNKS
    chunks = [pl.ds(i * chunk, chunk) for i in range(CHUNKS)]
    pairs = [(in_hbm, proj_in), (act_hbm, act), (out_hbm, proj_out)]
    pairs += [(grad_hbm.at[:, c], grad.at[:, c]) for c in chunks]
    pairs += [(len_hbm, lens), (own_hbm, owner)]
    in_copy, act_copy, out_copy, *grad_copies, len_copy, own_copy = copies(pairs, sems)
    me = lax.axis_index("tensor")
    parity = lax.rem(me, 2)
    in_copy.wait()
    act_copy.wait()
    x_t = mm(proj_in[...], act[...], NT)
    keep_ref[:half, :] = jnp.where(parity == 0, x_t[:half], x_t[half:])
    send_ref[:half, :] = jnp.where(parity == 0, x_t[half:], x_t[:half])
    len_copy.wait()
    own_copy.wait()
    mask_ref[...] = slot_mask(
        owners, relative, cap, lens[...], owner[...], mask_ref.shape[0], tokens
    )
    out_copy.wait()
    total = None
    for c, copy in zip(chunks, grad_copies):
        copy.wait()
        term = mm(proj_out[:, c], grad[:, c], NT)
        total = term if total is None else total + term
    turned[...] = total
    spot = half
    for apart in range(rank // width - 2, -1, -2):
        for ref, who in ((keep_ref, me ^ apart), (send_ref, me ^ (apart ^ 1))):
            block = pl.ds(pl.multiple_of(who * width, width), width)
            ref[spot : spot + width, :] = turned[block, :]
        spot += width


def project(act, grad, in_t, out_t, lengths, owner_row, owners, cap, width, relative):
    tokens, rank = act.shape[0], in_t.shape[0]
    depth = act.shape[1] + grad.shape[1]
    part = jax.ShapeDtypeStruct((rank, tokens), F32)
    hbm = pl.BlockSpec(memory_space=pl.ANY)
    vmem = pl.BlockSpec(memory_space=pltpu.VMEM)
    return pl.pallas_call(
        functools.partial(project_kernel, owners, relative, cap, width),
        in_specs=[hbm] * 6,
        out_specs=[vmem] * 3,
        out_shape=[part, part, jax.ShapeDtypeStruct((owners * cap, tokens), F32)],
        scratch_shapes=[
            pltpu.VMEM(act.shape, BF16),
            pltpu.VMEM(grad.shape, BF16),
            pltpu.VMEM(in_t.shape, BF16),
            pltpu.VMEM(out_t.shape, BF16),
            pltpu.VMEM(lengths.shape, jnp.int32),
            pltpu.VMEM(owner_row.shape, jnp.int32),
            pltpu.VMEM((rank, tokens), F32),
            pltpu.SemaphoreType.DMA((5 + CHUNKS,)),
        ],
        compiler_params=params(24),
        cost_estimate=cost(2 * tokens * depth * rank, 2 * depth * (tokens + rank)),
    )(
        *(
            pltpu.with_memory_space_constraint(x, pltpu.HBM)
            for x in (act, grad, in_t, out_t, lengths, owner_row)
        )
    )


def outer_kernel(x_ref, x_other_ref, g_ref, mask_ref, *blocks):
    width = g_ref.shape[0]
    rank = 2 * x_ref.shape[0]
    odd = lax.rem(lax.axis_index("tensor"), 2) == 1
    own, other = x_ref[...], x_other_ref[...]
    x_full = jnp.concatenate([jnp.where(odd, other, own), jnp.where(odd, own, other)], axis=0)
    x_both = jnp.concatenate(halves(x_full), axis=0)
    g_high = g_ref[...].astype(BF16).astype(F32)
    g_low = g_ref[...] - g_high
    mask = mask_ref[...]
    cap = blocks[0].shape[0]

    def product(i):
        pair = [(mask * g[i : i + 1, :]).astype(BF16) for g in (g_high, g_low)]
        both = mm(jnp.concatenate(pair, axis=0), x_both, NT)
        slots = mask.shape[0]
        return both[:slots, :rank] + both[:slots, rank:] + both[slots:, :rank]

    step = max(1, 128 // rank)
    for i in range(0, width, step):
        columns = jnp.concatenate([product(i + j) for j in range(step)], axis=1)
        for k, block in enumerate(blocks):
            block[:, i * rank : (i + step) * rank] = columns[k * cap : (k + 1) * cap, :]


def outer(x_half, x_other, g_t, mask, owners):
    slots, tokens = mask.shape
    width, rank = g_t.shape[0], 2 * x_half.shape[0]
    cap = slots // owners
    return pl.pallas_call(
        outer_kernel,
        out_shape=[jax.ShapeDtypeStruct((cap, width * rank), F32)] * owners,
        compiler_params=params(24),
        cost_estimate=cost(0, 0),
    )(x_half, x_other, g_t, mask)


def join_kernel(block_ref, *refs):
    *pieces, _, joined_ref, _ = refs
    cap = block_ref.shape[0]
    joined_ref[:cap, :] = block_ref[...]
    for i, piece in enumerate(pieces):
        size = piece.shape[0]
        joined_ref[cap + i * size : cap + (i + 1) * size, :] = piece[...]


def join(block, pieces, mate):
    rows = block.shape[0] + sum(p.shape[0] for p in pieces)
    vmem = pl.BlockSpec(memory_space=pltpu.VMEM)
    anywhere = pl.BlockSpec(memory_space=pl.ANY)
    return pl.pallas_call(
        join_kernel,
        in_specs=[vmem] * (1 + len(pieces)) + [anywhere],
        out_specs=[vmem, anywhere],
        out_shape=[
            jax.ShapeDtypeStruct((rows, block.shape[1]), F32),
            jax.ShapeDtypeStruct(mate.shape, mate.dtype),
        ],
        input_output_aliases={1 + len(pieces): 1},
        compiler_params=params(16),
        cost_estimate=cost(0, 0),
    )(block, *pieces, mate)


def score_kernel(count, early, size, gaps, relative, ids_ref, *refs):
    rows, pieces, scores_ref = refs[:count], refs[count:-1], refs[-1]
    queries = ids_ref.shape[1]
    me = lax.axis_index("dp")
    cap = rows[0].shape[0]
    high, low = halves(jnp.concatenate([r[:cap, :] for r in rows], axis=0))
    slots = high.shape[0]
    both = jnp.concatenate([high, low], axis=0)
    parts = [piece[...] for piece in pieces]
    parts += [rows[1][cap + i * size : cap + (i + 1) * size, :] for i in range(len(gaps) - early)]
    held = parts[0].shape[0]
    pool = jnp.concatenate(parts, axis=0)
    products = mm(both, jnp.concatenate(halves(pool), axis=0), NT)
    split = pool.shape[0]
    part = products[:slots, :split] + products[:slots, split:] + products[slots:, :split]
    row = lax.broadcasted_iota(jnp.int32, (held, queries), 0)
    places = [row + ((me ^ gap) * held if len(gaps) > 1 else 0) for gap in gaps]
    hot = (jnp.concatenate(places, axis=0) == ids_ref[...]).astype(F32).astype(BF16)
    top, rest = halves(part)
    last = (part - top.astype(F32) - rest.astype(F32)).astype(BF16)
    picked = mm(jnp.concatenate([top, rest, last], axis=0), hot)
    total = picked[:slots] + picked[slots : 2 * slots] + picked[2 * slots :]
    for k in range(count):
        spot = pl.ds(pl.multiple_of((me ^ k) * cap, cap), cap) if relative else pl.ds(k * cap, cap)
        scores_ref[spot, :] = total[k * cap : (k + 1) * cap, :]


def score(ids_row, rows, pieces, gaps, relative):
    slots = rows[0].shape[0] * len(rows)
    queries = ids_row.shape[1]
    size, feats = pieces[0].shape
    flops = 6 * slots * size * len(gaps) * feats
    return pl.pallas_call(
        functools.partial(score_kernel, len(rows), len(pieces), size, gaps, relative),
        out_shape=jax.ShapeDtypeStruct((slots, queries), F32),
        compiler_params=params(24),
        cost_estimate=cost(flops, 4 * size * len(gaps) * feats),
    )(ids_row, *rows, *pieces)


def place_kernel(*refs):
    rows, store_ref = refs[:-1], refs[-1]
    me = lax.axis_index("dp")
    cap = rows[0].shape[0]
    for k, row in enumerate(rows):
        store_ref[pl.ds(pl.multiple_of((me ^ k) * cap, cap), cap), :] = row[:cap, :]


def place(rows):
    slots, feats = rows[0].shape[0] * len(rows), rows[0].shape[1]
    return pl.pallas_call(
        place_kernel,
        out_shape=jax.ShapeDtypeStruct((slots, feats), F32),
        compiler_params=params(16),
        cost_estimate=cost(0, 8 * slots * feats),
    )(*rows)


def swap(x, axis, gap):
    return lax.ppermute(x, axis, [(i, i ^ gap) for i in range(lax.axis_size(axis))])


def gather_pieces(piece):
    pieces, gaps = [piece], [0]
    bit = lax.axis_size("dp") // 2
    while bit > 1:
        pieces, gaps = pieces + [swap(p, "dp", bit) for p in pieces], gaps + [g ^ bit for g in gaps]
        bit //= 2
    return pieces, gaps


def local(
    activations, out_grads, proj_in, proj_out, doc_lengths, doc_owner, query_grads, query_ids
):
    tensor_size = lax.axis_size("tensor")
    data_size = lax.axis_size("dp")
    tokens = activations.shape[0]
    rank = proj_in.shape[1]
    half = rank // 2
    width = rank // tensor_size
    docs = doc_owner.shape[0]
    cap = max(2, 2 * docs // data_size)
    direct = data_size <= MOST_DIRECT

    if direct:
        pieces, gaps = gather_pieces(query_grads)
        mate = swap(query_grads, "dp", 1)
    else:
        pieces, gaps = [lax.all_gather(query_grads, "dp", axis=0, tiled=True)], [0]

    keep, send, mask = project(
        activations, out_grads, proj_in.T, proj_out.T, doc_lengths, doc_owner.T,
        data_size, cap, width, direct,
    )
    part = keep + swap(send, "tensor", 1)
    bit = tensor_size // 2
    while bit > 1:
        cut = half + (part.shape[0] - half) // 2
        got = swap(part[:cut], "tensor", bit)
        part = jnp.concatenate([part[:half] + got[:half], part[cut:] + got[half:]], axis=0)
        bit //= 2
    x_half, g_mine = part[:half], part[half:]
    x_other = swap(x_half, "tensor", 1)
    blocks = outer(x_half, x_other, g_mine, mask, data_size)
    if direct:
        joined, mate = join(blocks[1], pieces[1:], mate)
        near = swap(joined, "dp", 1)
        far = [swap(blocks[k], "dp", k) for k in range(2, data_size)]
        rows = [blocks[0], near, *far]
        pieces, gaps = [*pieces, mate], [*gaps, 1, *(g ^ 1 for g in gaps[1:])]
        store = place(rows)
    else:
        rows = [lax.all_to_all(jnp.stack(blocks), "dp", 0, 0, tiled=True).reshape(-1, width * rank)]
        store = rows[0]
    scores = score(query_ids[None, :], rows, pieces, gaps, direct)
    bit = 1
    while bit < tensor_size:
        scores = scores + swap(scores, "tensor", bit)
        bit *= 2
    return store, scores * (1.0 / (rank * rank))


def solution(mesh):
    return jax.shard_map(
        local,
        mesh=mesh,
        in_specs=(
            P(("groups", "dp"), "tensor"),
            P(("groups", "dp"), "tensor"),
            P("tensor", None),
            P("tensor", None),
            P(("groups", "dp"), None),
            P(("groups", "dp"), None),
            P(("groups", "dp"), "tensor"),
            P("groups"),
        ),
        out_specs=(P(("groups", "dp"), "tensor"), P(("groups", "dp"), None)),
        check_vma=False,
    )
```

```python
import functools

import jax
import jax.numpy as jnp
from jax import lax
from jax.experimental import pallas as pl
from jax.experimental.pallas import tpu as pltpu
from jax.sharding import PartitionSpec as P

F32 = jnp.float32
BF16 = jnp.bfloat16
MIB = 1024 * 1024
NT = (((1,), (1,)), ((), ()))
MOST_DIRECT = 8
CHUNKS = 2


def params(mib):
    return pltpu.CompilerParams(vmem_limit_bytes=mib * MIB)


def cost(flops, nbytes):
    return pl.CostEstimate(flops=flops, bytes_accessed=nbytes, transcendentals=0)


def halves(x):
    high = x.astype(BF16)
    return high, (x - high.astype(F32)).astype(BF16)


def mm(a, b, dims=(((1,), (0,)), ((), ()))):
    return lax.dot_general(a, b, dims, preferred_element_type=F32)


def copies(pairs, sems):
    made = [pltpu.make_async_copy(src, dst, sems.at[i]) for i, (src, dst) in enumerate(pairs)]
    for copy in made:
        copy.start()
    return made


def slot_mask(owners, relative, cap, lengths, owner, slots, tokens):
    docs = lengths.shape[1]
    row = lax.broadcasted_iota(jnp.int32, (docs, docs), 0)
    col = lax.broadcasted_iota(jnp.int32, (docs, docs), 1)
    len_row = lengths.astype(F32)
    place_row = owner ^ lax.axis_index("dp") if relative else owner
    own_row = place_row.astype(F32)

    def column(values):
        return jnp.sum(jnp.where(row == col, values, 0.0), axis=1, keepdims=True)

    ends = jnp.sum(jnp.where(row <= col, column(len_row), 0.0), axis=0, keepdims=True)
    rank = jnp.sum(
        jnp.where((row < col) & (column(own_row) == own_row), 1.0, 0.0), axis=0, keepdims=True
    )
    slot = lax.broadcasted_iota(jnp.int32, (slots, docs), 0).astype(F32)
    hot = slot == own_row * cap + rank
    first = jnp.sum(jnp.where(hot, ends - len_row, 0.0), axis=1, keepdims=True)
    last = jnp.sum(jnp.where(hot, ends, 0.0), axis=1, keepdims=True)
    token = lax.broadcasted_iota(jnp.int32, (slots, tokens), 1).astype(F32)
    return jnp.where((token >= first) & (token < last), 1.0, 0.0)


def project_kernel(
    owners, relative, cap, width, act_hbm, grad_hbm, in_hbm, out_hbm, len_hbm, own_hbm,
    keep_ref, send_ref, mask_ref, act, grad, proj_in, proj_out, lens, owner, turned, sems,
):
    tokens = act.shape[0]
    rank = proj_in.shape[0]
    half = rank // 2
    chunk = grad.shape[1] // CHUNKS
    chunks = [pl.ds(i * chunk, chunk) for i in range(CHUNKS)]
    pairs = [(in_hbm, proj_in), (act_hbm, act), (out_hbm, proj_out)]
    pairs += [(grad_hbm.at[:, c], grad.at[:, c]) for c in chunks]
    pairs += [(len_hbm, lens), (own_hbm, owner)]
    in_copy, act_copy, out_copy, *grad_copies, len_copy, own_copy = copies(pairs, sems)
    me = lax.axis_index("tensor")
    parity = lax.rem(me, 2)
    in_copy.wait()
    act_copy.wait()
    x_t = mm(proj_in[...], act[...], NT)
    keep_ref[:half, :] = jnp.where(parity == 0, x_t[:half], x_t[half:])
    send_ref[:half, :] = jnp.where(parity == 0, x_t[half:], x_t[:half])
    len_copy.wait()
    own_copy.wait()
    mask_ref[...] = slot_mask(
        owners, relative, cap, lens[...], owner[...], mask_ref.shape[0], tokens
    )
    out_copy.wait()
    total = None
    for c, copy in zip(chunks, grad_copies):
        copy.wait()
        term = mm(proj_out[:, c], grad[:, c], NT)
        total = term if total is None else total + term
    turned[...] = total
    spot = half
    for apart in range(rank // width - 2, -1, -2):
        for ref, who in ((keep_ref, me ^ apart), (send_ref, me ^ (apart ^ 1))):
            block = pl.ds(pl.multiple_of(who * width, width), width)
            ref[spot : spot + width, :] = turned[block, :]
        spot += width


def project(act, grad, in_t, out_t, lengths, owner_row, owners, cap, width, relative):
    tokens, rank = act.shape[0], in_t.shape[0]
    depth = act.shape[1] + grad.shape[1]
    part = jax.ShapeDtypeStruct((rank, tokens), F32)
    hbm = pl.BlockSpec(memory_space=pl.ANY)
    vmem = pl.BlockSpec(memory_space=pltpu.VMEM)
    return pl.pallas_call(
        functools.partial(project_kernel, owners, relative, cap, width),
        in_specs=[hbm] * 6,
        out_specs=[vmem] * 3,
        out_shape=[part, part, jax.ShapeDtypeStruct((owners * cap, tokens), F32)],
        scratch_shapes=[
            pltpu.VMEM(act.shape, BF16),
            pltpu.VMEM(grad.shape, BF16),
            pltpu.VMEM(in_t.shape, BF16),
            pltpu.VMEM(out_t.shape, BF16),
            pltpu.VMEM(lengths.shape, jnp.int32),
            pltpu.VMEM(owner_row.shape, jnp.int32),
            pltpu.VMEM((rank, tokens), F32),
            pltpu.SemaphoreType.DMA((5 + CHUNKS,)),
        ],
        compiler_params=params(24),
        cost_estimate=cost(0, 0),
    )(
        *(
            pltpu.with_memory_space_constraint(x, pltpu.HBM)
            for x in (act, grad, in_t, out_t, lengths, owner_row)
        )
    )


def fold_kernel(keeps, gots, low, high, cuts, *refs):
    kept = jnp.concatenate([r[...] for r in refs[:keeps]], axis=0)
    got = jnp.concatenate([r[...] for r in refs[keeps : keeps + gots]], axis=0)
    if low < high:
        kept = jnp.concatenate([kept[:low], kept[high:]], axis=0)
    total = kept + got
    for first, last, out in zip(cuts, cuts[1:], refs[keeps + gots :]):
        out[...] = total[first:last]


def fold(keeps, gots, low, high, cuts):
    tokens = keeps[0].shape[1]
    return list(
        pl.pallas_call(
            functools.partial(fold_kernel, len(keeps), len(gots), low, high, tuple(cuts)),
            out_shape=[
                jax.ShapeDtypeStruct((last - first, tokens), F32)
                for first, last in zip(cuts, cuts[1:])
            ],
            compiler_params=params(16),
            cost_estimate=cost(0, 0),
        )(*keeps, *gots)
    )


def sum_tensor(keep, send, half, width):
    rows = keep.shape[0]
    bit = lax.axis_size("tensor")
    low, high = rows, rows
    keeps, gots = [keep], [swap(send, "tensor", 1)]
    while bit > 2:
        bit //= 2
        cut = half + (rows - half) // 2
        parts = fold(keeps, gots, low, high, [0, cut // 16 * 8, cut, rows])
        gots = [swap(p, "tensor", bit) for p in parts[:2]]
        keeps, low, high = parts, half, cut
        rows -= cut - half
    return fold(keeps, gots, low, high, [0, half, half + width])


def outer_kernel(owners, x_ref, x_other_ref, g_ref, mask_ref, *refs):
    blocks = refs[-owners:]
    width = g_ref.shape[0]
    rank = 2 * x_ref.shape[0]
    odd = lax.rem(lax.axis_index("tensor"), 2) == 1
    own, other = x_ref[...], x_other_ref[...]
    x_full = jnp.concatenate([jnp.where(odd, other, own), jnp.where(odd, own, other)], axis=0)
    x_both = jnp.concatenate(halves(x_full), axis=0)
    g_high = g_ref[...].astype(BF16).astype(F32)
    g_low = g_ref[...] - g_high
    mask = mask_ref[...]
    cap = blocks[0].shape[0]

    def product(i):
        pair = [(mask * g[i : i + 1, :]).astype(BF16) for g in (g_high, g_low)]
        both = mm(jnp.concatenate(pair, axis=0), x_both, NT)
        slots = mask.shape[0]
        return both[:slots, :rank] + both[:slots, rank:] + both[slots:, :rank]

    step = max(1, 128 // rank)
    for i in range(0, width, step):
        columns = jnp.concatenate([product(i + j) for j in range(step)], axis=1)
        for k, block in enumerate(blocks):
            block[:, i * rank : (i + step) * rank] = columns[k * cap : (k + 1) * cap, :]


def outer(x_half, x_other, g_t, mask, owners, pieces):
    slots, tokens = mask.shape
    width, rank = g_t.shape[0], 2 * x_half.shape[0]
    cap = slots // owners
    return pl.pallas_call(
        functools.partial(outer_kernel, owners),
        in_specs=[pl.BlockSpec(memory_space=pltpu.VMEM)] * 4
        + [pl.BlockSpec(memory_space=pl.ANY)] * len(pieces),
        out_shape=[jax.ShapeDtypeStruct((cap, width * rank), F32)] * owners,
        compiler_params=params(24),
        cost_estimate=cost(8 * slots * width * tokens * rank, 4 * slots * width * rank),
    )(x_half, x_other, g_t, mask, *pieces)


def join_kernel(block_ref, *refs):
    *pieces, _, joined_ref, _ = refs
    cap = block_ref.shape[0]
    joined_ref[:cap, :] = block_ref[...]
    for i, piece in enumerate(pieces):
        size = piece.shape[0]
        joined_ref[cap + i * size : cap + (i + 1) * size, :] = piece[...]


def join(block, pieces, mate):
    rows = block.shape[0] + sum(p.shape[0] for p in pieces)
    vmem = pl.BlockSpec(memory_space=pltpu.VMEM)
    anywhere = pl.BlockSpec(memory_space=pl.ANY)
    return pl.pallas_call(
        join_kernel,
        in_specs=[vmem] * (1 + len(pieces)) + [anywhere],
        out_specs=[vmem, anywhere],
        out_shape=[
            jax.ShapeDtypeStruct((rows, block.shape[1]), F32),
            jax.ShapeDtypeStruct(mate.shape, mate.dtype),
        ],
        input_output_aliases={1 + len(pieces): 1},
        compiler_params=params(16),
        cost_estimate=cost(0, 0),
    )(block, *pieces, mate)


def score_kernel(count, early, size, gaps, relative, ids_ref, *refs):
    rows, pieces, scores_ref = refs[:count], refs[count:-1], refs[-1]
    queries = ids_ref.shape[1]
    me = lax.axis_index("dp")
    cap = rows[0].shape[0]
    high, low = halves(jnp.concatenate([r[:cap, :] for r in rows], axis=0))
    slots = high.shape[0]
    both = jnp.concatenate([high, low], axis=0)
    parts = [piece[...] for piece in pieces]
    parts += [rows[1][cap + i * size : cap + (i + 1) * size, :] for i in range(len(gaps) - early)]
    held = parts[0].shape[0]
    pool = jnp.concatenate(parts, axis=0)
    products = mm(both, jnp.concatenate(halves(pool), axis=0), NT)
    split = pool.shape[0]
    part = products[:slots, :split] + products[:slots, split:] + products[slots:, :split]
    row = lax.broadcasted_iota(jnp.int32, (held, queries), 0)
    places = [row + ((me ^ gap) * held if len(gaps) > 1 else 0) for gap in gaps]
    hot = (jnp.concatenate(places, axis=0) == ids_ref[...]).astype(F32).astype(BF16)
    top, rest = halves(part)
    last = (part - top.astype(F32) - rest.astype(F32)).astype(BF16)
    picked = mm(jnp.concatenate([top, rest, last], axis=0), hot)
    total = picked[:slots] + picked[slots : 2 * slots] + picked[2 * slots :]
    for k in range(count):
        spot = pl.ds(pl.multiple_of((me ^ k) * cap, cap), cap) if relative else pl.ds(k * cap, cap)
        scores_ref[spot, :] = total[k * cap : (k + 1) * cap, :]


def score(ids_row, rows, pieces, gaps, relative):
    slots = rows[0].shape[0] * len(rows)
    queries = ids_row.shape[1]
    size, feats = pieces[0].shape
    flops = 6 * slots * size * len(gaps) * feats
    return pl.pallas_call(
        functools.partial(score_kernel, len(rows), len(pieces), size, gaps, relative),
        out_shape=jax.ShapeDtypeStruct((slots, queries), F32),
        compiler_params=params(24),
        cost_estimate=cost(flops, 4 * size * len(gaps) * feats),
    )(ids_row, *rows, *pieces)


def place_kernel(*refs):
    rows, store_ref = refs[:-1], refs[-1]
    me = lax.axis_index("dp")
    cap = rows[0].shape[0]
    for k, row in enumerate(rows):
        store_ref[pl.ds(pl.multiple_of((me ^ k) * cap, cap), cap), :] = row[:cap, :]


def place(rows):
    slots, feats = rows[0].shape[0] * len(rows), rows[0].shape[1]
    return pl.pallas_call(
        place_kernel,
        out_shape=jax.ShapeDtypeStruct((slots, feats), F32),
        compiler_params=params(16),
        cost_estimate=cost(0, 8 * slots * feats),
    )(*rows)


def swap(x, axis, gap):
    return lax.ppermute(x, axis, [(i, i ^ gap) for i in range(lax.axis_size(axis))])


def gather_pieces(piece):
    pieces, gaps = [piece], [0]
    bit = lax.axis_size("dp") // 2
    while bit > 1:
        pieces, gaps = pieces + [swap(p, "dp", bit) for p in pieces], gaps + [g ^ bit for g in gaps]
        bit //= 2
    return pieces, gaps


def local(
    activations, out_grads, proj_in, proj_out, doc_lengths, doc_owner, query_grads, query_ids
):
    tensor_size = lax.axis_size("tensor")
    data_size = lax.axis_size("dp")
    tokens = activations.shape[0]
    rank = proj_in.shape[1]
    half = rank // 2
    width = rank // tensor_size
    docs = doc_owner.shape[0]
    cap = max(2, 2 * docs // data_size)
    direct = data_size <= MOST_DIRECT

    if direct:
        pieces, gaps = gather_pieces(query_grads)
        mate = swap(query_grads, "dp", 1)
    else:
        pieces, gaps = [lax.all_gather(query_grads, "dp", axis=0, tiled=True)], [0]

    keep, send, mask = project(
        activations, out_grads, proj_in.T, proj_out.T, doc_lengths, doc_owner.T,
        data_size, cap, width, direct,
    )
    x_half, g_mine = sum_tensor(keep, send, half, width)
    x_other = swap(x_half, "tensor", 1)
    blocks = outer(x_half, x_other, g_mine, mask, data_size, pieces[1:])
    if direct:
        joined, mate = join(blocks[1], pieces[1:], mate)
        near = swap(joined, "dp", 1)
        far = [swap(blocks[k], "dp", k) for k in range(2, data_size)]
        rows = [blocks[0], near, *far]
        pieces, gaps = [*pieces, mate], [*gaps, 1, *(g ^ 1 for g in gaps[1:])]
        store = place(rows)
    else:
        rows = [lax.all_to_all(jnp.stack(blocks), "dp", 0, 0, tiled=True).reshape(-1, width * rank)]
        store = rows[0]
    scores = score(query_ids[None, :], rows, pieces, gaps, direct)
    bit = 1
    while bit < tensor_size:
        scores = scores + swap(scores, "tensor", bit)
        bit *= 2
    return store, scores * (1.0 / (rank * rank))


def solution(mesh):
    return jax.shard_map(
        local,
        mesh=mesh,
        in_specs=(
            P(("groups", "dp"), "tensor"),
            P(("groups", "dp"), "tensor"),
            P("tensor", None),
            P("tensor", None),
            P(("groups", "dp"), None),
            P(("groups", "dp"), None),
            P(("groups", "dp"), "tensor"),
            P("groups"),
        ),
        out_specs=(P(("groups", "dp"), "tensor"), P(("groups", "dp"), None)),
        check_vma=False,
    )
```

```python
import functools

import jax
import jax.numpy as jnp
from jax import lax
from jax.experimental import pallas as pl
from jax.experimental.pallas import tpu as pltpu
from jax.sharding import PartitionSpec as P

F32 = jnp.float32
BF16 = jnp.bfloat16
MIB = 1024 * 1024
NT = (((1,), (1,)), ((), ()))
MOST_DIRECT = 8


def params(mib):
    return pltpu.CompilerParams(vmem_limit_bytes=mib * MIB)


def cost(flops, nbytes):
    return pl.CostEstimate(flops=flops, bytes_accessed=nbytes, transcendentals=0)


def halves(x):
    high = x.astype(BF16)
    return high, (x - high.astype(F32)).astype(BF16)


def mm(a, b, dims=(((1,), (0,)), ((), ()))):
    return lax.dot_general(a, b, dims, preferred_element_type=F32)


def copies(pairs, sems):
    made = [pltpu.make_async_copy(src, dst, sems.at[i]) for i, (src, dst) in enumerate(pairs)]
    for copy in made:
        copy.start()
    return made


def slot_mask(owners, relative, cap, lengths, owner, slots, tokens):
    docs = lengths.shape[1]
    row = lax.broadcasted_iota(jnp.int32, (docs, docs), 0)
    col = lax.broadcasted_iota(jnp.int32, (docs, docs), 1)
    len_row = lengths.astype(F32)
    place_row = owner ^ lax.axis_index("dp") if relative else owner
    own_row = place_row.astype(F32)

    def column(values):
        return jnp.sum(jnp.where(row == col, values, 0.0), axis=1, keepdims=True)

    ends = jnp.sum(jnp.where(row <= col, column(len_row), 0.0), axis=0, keepdims=True)
    rank = jnp.sum(
        jnp.where((row < col) & (column(own_row) == own_row), 1.0, 0.0), axis=0, keepdims=True
    )
    slot = lax.broadcasted_iota(jnp.int32, (slots, docs), 0).astype(F32)
    hot = slot == own_row * cap + rank
    first = jnp.sum(jnp.where(hot, ends - len_row, 0.0), axis=1, keepdims=True)
    last = jnp.sum(jnp.where(hot, ends, 0.0), axis=1, keepdims=True)
    token = lax.broadcasted_iota(jnp.int32, (slots, tokens), 1).astype(F32)
    return jnp.where((token >= first) & (token < last), 1.0, 0.0)


def x_kernel(
    owners, relative, cap, act_hbm, grad_hbm, in_hbm, out_hbm, len_hbm, own_hbm,
    x_ref, mask_ref, grad, proj_out, act, proj_in, lens, owner, sems,
):
    pairs = [(in_hbm, proj_in), (act_hbm, act), (len_hbm, lens), (own_hbm, owner)]
    pairs += [(out_hbm, proj_out), (grad_hbm, grad)]
    in_copy, act_copy, len_copy, own_copy, out_copy, grad_copy = copies(pairs, sems)
    len_copy.wait()
    own_copy.wait()
    mask_ref[...] = slot_mask(owners, relative, cap, lens[...], owner[...], *mask_ref.shape)
    in_copy.wait()
    act_copy.wait()
    x_ref[...] = mm(proj_in[...], act[...], NT)
    out_copy.wait()
    grad_copy.wait()


def project_x(act, grad, in_t, out_t, lengths, owner_row, owners, cap, relative):
    tokens, rank = act.shape[0], in_t.shape[0]
    hbm = pl.BlockSpec(memory_space=pl.ANY)
    vmem = pl.BlockSpec(memory_space=pltpu.VMEM)
    return pl.pallas_call(
        functools.partial(x_kernel, owners, relative, cap),
        in_specs=[hbm] * 6,
        out_specs=[vmem] * 4,
        out_shape=[
            jax.ShapeDtypeStruct((rank, tokens), F32),
            jax.ShapeDtypeStruct((owners * cap, tokens), F32),
            jax.ShapeDtypeStruct(grad.shape, BF16),
            jax.ShapeDtypeStruct(out_t.shape, BF16),
        ],
        scratch_shapes=[
            pltpu.VMEM(act.shape, BF16),
            pltpu.VMEM(in_t.shape, BF16),
            pltpu.VMEM(lengths.shape, jnp.int32),
            pltpu.VMEM(owner_row.shape, jnp.int32),
            pltpu.SemaphoreType.DMA((6,)),
        ],
        compiler_params=params(24),
        cost_estimate=cost(0, 0),
    )(
        *(
            pltpu.with_memory_space_constraint(x, pltpu.HBM)
            for x in (act, grad, in_t, out_t, lengths, owner_row)
        )
    )


def g_kernel(width, grad_ref, proj_ref, keep_ref, send_ref, full):
    full[...] = mm(proj_ref[...], grad_ref[...], NT)
    me = lax.axis_index("tensor")
    count = full.shape[0] // width
    for apart in range(count):
        block = pl.ds(pl.multiple_of((me ^ apart) * width, width), width)
        ref, spot = (keep_ref, apart) if apart < count // 2 else (send_ref, apart - count // 2)
        ref[spot * width : (spot + 1) * width, :] = full[block, :]


def project_g(grad, out_t, width):
    tokens, rank = grad.shape[0], out_t.shape[0]
    part = jax.ShapeDtypeStruct((rank // 2, tokens), F32)
    return pl.pallas_call(
        functools.partial(g_kernel, width),
        out_shape=[part, part],
        scratch_shapes=[pltpu.VMEM((rank, tokens), F32)],
        compiler_params=params(24),
        cost_estimate=cost(0, 0),
    )(grad, out_t)


def stack(refs):
    return jnp.concatenate([r[...] for r in refs], axis=0)


def fold_kernel(rank, owned, came, keep_ref, *refs):
    first_ref, second_ref, kept_ref = refs[-3:]
    got = stack(refs[owned : owned + came])
    total = keep_ref[...] + got[rank:]
    kept = kept_ref.shape[0]
    kept_ref[...] = total[:kept]
    x = stack(refs[:owned])[:rank] + got[:rank]
    sent = jnp.concatenate([x, total[kept:]], axis=0)
    cut = first_ref.shape[0]
    first_ref[...] = sent[:cut]
    second_ref[...] = sent[cut:]


def fold(rank, keep, own, gots, pieces):
    tokens = keep.shape[1]
    kept = keep.shape[0] // 2
    cut = (rank + kept) // 16 * 8
    *sent, keep = pl.pallas_call(
        functools.partial(fold_kernel, rank, len(own), len(gots)),
        in_specs=[pl.BlockSpec(memory_space=pltpu.VMEM)] * (1 + len(own) + len(gots))
        + [pl.BlockSpec(memory_space=pl.ANY)] * len(pieces),
        out_shape=[
            jax.ShapeDtypeStruct((rows, tokens), F32) for rows in (cut, rank + kept - cut, kept)
        ],
        compiler_params=params(16),
        cost_estimate=cost(0, 0),
    )(keep, *own, *gots, *pieces)
    return keep, sent


def outer_kernel(owners, sent, g_ref, mask_ref, *refs):
    blocks = refs[-owners:]
    width = g_ref.shape[0]
    own, got = stack(refs[:sent]), stack(refs[sent : 2 * sent])
    rank = got.shape[0] - width
    x_full = own[:rank] + got[:rank]
    g_full = g_ref[...] + got[rank:]
    x_both = jnp.concatenate(halves(x_full), axis=0)
    g_high = g_full.astype(BF16).astype(F32)
    g_low = g_full - g_high
    mask = mask_ref[...]
    cap = blocks[0].shape[0]

    def product(i):
        pair = [(mask * g[i : i + 1, :]).astype(BF16) for g in (g_high, g_low)]
        both = mm(jnp.concatenate(pair, axis=0), x_both, NT)
        slots = mask.shape[0]
        return both[:slots, :rank] + both[:slots, rank:] + both[slots:, :rank]

    step = max(1, 128 // rank)
    for i in range(0, width, step):
        columns = jnp.concatenate([product(i + j) for j in range(step)], axis=1)
        for k, block in enumerate(blocks):
            block[:, i * rank : (i + step) * rank] = columns[k * cap : (k + 1) * cap, :]


def outer(sent, gots, g, mask, owners, pieces):
    slots, tokens = mask.shape
    width = g.shape[0]
    rank = sum(p.shape[0] for p in sent) - width
    cap = slots // owners
    return pl.pallas_call(
        functools.partial(outer_kernel, owners, len(sent)),
        in_specs=[pl.BlockSpec(memory_space=pltpu.VMEM)] * (2 + 2 * len(sent))
        + [pl.BlockSpec(memory_space=pl.ANY)] * len(pieces),
        out_shape=[jax.ShapeDtypeStruct((cap, width * rank), F32)] * owners,
        compiler_params=params(24),
        cost_estimate=cost(8 * slots * width * tokens * rank, 4 * slots * width * rank),
    )(g, mask, *sent, *gots, *pieces)


def join_kernel(*refs):
    refs[-1][...] = stack(refs[:-1])


def join(block, pieces):
    rows = block.shape[0] + sum(p.shape[0] for p in pieces)
    return pl.pallas_call(
        join_kernel,
        out_shape=jax.ShapeDtypeStruct((rows, block.shape[1]), F32),
        compiler_params=params(16),
        cost_estimate=cost(0, 0),
    )(block, *pieces)


def score_kernel(count, early, size, gaps, relative, ids_ref, *refs):
    rows, pieces, scores_ref = refs[:count], refs[count:-1], refs[-1]
    queries = ids_ref.shape[1]
    me = lax.axis_index("dp")
    cap = rows[0].shape[0]
    high, low = halves(jnp.concatenate([r[:cap, :] for r in rows], axis=0))
    slots = high.shape[0]
    both = jnp.concatenate([high, low], axis=0)
    parts = [piece[...] for piece in pieces]
    parts += [rows[1][cap + i * size : cap + (i + 1) * size, :] for i in range(len(gaps) - early)]
    held = parts[0].shape[0]
    pool = jnp.concatenate(parts, axis=0)
    products = mm(both, jnp.concatenate(halves(pool), axis=0), NT)
    split = pool.shape[0]
    part = products[:slots, :split] + products[:slots, split:] + products[slots:, :split]
    row = lax.broadcasted_iota(jnp.int32, (held, queries), 0)
    places = [row + ((me ^ gap) * held if len(gaps) > 1 else 0) for gap in gaps]
    hot = (jnp.concatenate(places, axis=0) == ids_ref[...]).astype(F32).astype(BF16)
    top, rest = halves(part)
    last = (part - top.astype(F32) - rest.astype(F32)).astype(BF16)
    picked = mm(jnp.concatenate([top, rest, last], axis=0), hot)
    total = picked[:slots] + picked[slots : 2 * slots] + picked[2 * slots :]
    for k in range(count):
        spot = pl.ds(pl.multiple_of((me ^ k) * cap, cap), cap) if relative else pl.ds(k * cap, cap)
        scores_ref[spot, :] = total[k * cap : (k + 1) * cap, :]


def score(ids_row, rows, pieces, gaps, relative):
    slots = rows[0].shape[0] * len(rows)
    queries = ids_row.shape[1]
    size, feats = pieces[0].shape
    flops = 6 * slots * size * len(gaps) * feats
    return pl.pallas_call(
        functools.partial(score_kernel, len(rows), len(pieces), size, gaps, relative),
        out_shape=jax.ShapeDtypeStruct((slots, queries), F32),
        compiler_params=params(24),
        cost_estimate=cost(flops, 4 * size * len(gaps) * feats),
    )(ids_row, *rows, *pieces)


def place_kernel(*refs):
    rows, store_ref = refs[:-1], refs[-1]
    me = lax.axis_index("dp")
    cap = rows[0].shape[0]
    for k, row in enumerate(rows):
        store_ref[pl.ds(pl.multiple_of((me ^ k) * cap, cap), cap), :] = row[:cap, :]


def place(rows):
    slots, feats = rows[0].shape[0] * len(rows), rows[0].shape[1]
    return pl.pallas_call(
        place_kernel,
        out_shape=jax.ShapeDtypeStruct((slots, feats), F32),
        compiler_params=params(16),
        cost_estimate=cost(0, 8 * slots * feats),
    )(*rows)


def swap(x, axis, gap):
    return lax.ppermute(x, axis, [(i, i ^ gap) for i in range(lax.axis_size(axis))])


def gather_pieces(piece):
    pieces, gaps = [piece], [0]
    bit = lax.axis_size("dp") // 2
    while bit > 1:
        pieces, gaps = pieces + [swap(p, "dp", bit) for p in pieces], gaps + [g ^ bit for g in gaps]
        bit //= 2
    return pieces, gaps


def local(
    activations, out_grads, proj_in, proj_out, doc_lengths, doc_owner, query_grads, query_ids
):
    tensor_size = lax.axis_size("tensor")
    data_size = lax.axis_size("dp")
    tokens = activations.shape[0]
    rank = proj_in.shape[1]
    width = rank // tensor_size
    docs = doc_owner.shape[0]
    cap = max(2, 2 * docs // data_size)
    direct = data_size <= MOST_DIRECT

    if direct:
        pieces, gaps = gather_pieces(query_grads)
        mate = swap(query_grads, "dp", 1)
    else:
        pieces, gaps = [lax.all_gather(query_grads, "dp", axis=0, tiled=True)], [0]
        mate = pieces[0]

    x, mask, grad, out_t = project_x(
        activations, out_grads, proj_in.T, proj_out.T, doc_lengths, doc_owner.T,
        data_size, cap, direct,
    )
    bit = tensor_size // 2
    x_got = swap(x, "tensor", bit)
    keep, send = project_g(grad, out_t, width)
    own, gots = [x], [x_got, swap(send, "tensor", bit)]
    while bit > 1:
        bit //= 2
        keep, own = fold(rank, keep, own, gots, pieces[1:])
        gots = [swap(part, "tensor", bit) for part in own]
    blocks = outer(own, gots, keep, mask, data_size, [mate])
    if direct:
        near = swap(join(blocks[1], pieces[1:]), "dp", 1)
        far = [swap(blocks[k], "dp", k) for k in range(2, data_size)]
        rows = [blocks[0], near, *far]
        pieces, gaps = [*pieces, mate], [*gaps, 1, *(g ^ 1 for g in gaps[1:])]
        store = place(rows)
    else:
        rows = [lax.all_to_all(jnp.stack(blocks), "dp", 0, 0, tiled=True).reshape(-1, width * rank)]
        store = rows[0]
    scores = score(query_ids[None, :], rows, pieces, gaps, direct)
    bit = 1
    while bit < tensor_size:
        scores = scores + swap(scores, "tensor", bit)
        bit *= 2
    return store, scores * (1.0 / (rank * rank))


def solution(mesh):
    return jax.shard_map(
        local,
        mesh=mesh,
        in_specs=(
            P(("groups", "dp"), "tensor"),
            P(("groups", "dp"), "tensor"),
            P("tensor", None),
            P("tensor", None),
            P(("groups", "dp"), None),
            P(("groups", "dp"), None),
            P(("groups", "dp"), "tensor"),
            P("groups"),
        ),
        out_specs=(P(("groups", "dp"), "tensor"), P(("groups", "dp"), None)),
        check_vma=False,
    )
```

```python
import functools

import jax
import jax.numpy as jnp
from jax import lax
from jax.experimental import pallas as pl
from jax.experimental.pallas import tpu as pltpu
from jax.sharding import PartitionSpec as P

F32 = jnp.float32
BF16 = jnp.bfloat16
MIB = 1024 * 1024
NT = (((1,), (1,)), ((), ()))
MOST_DIRECT = 8


def params(mib):
    return pltpu.CompilerParams(vmem_limit_bytes=mib * MIB)


def cost(flops, nbytes):
    return pl.CostEstimate(flops=flops, bytes_accessed=nbytes, transcendentals=0)


def halves(x):
    high = x.astype(BF16)
    return high, (x - high.astype(F32)).astype(BF16)


def mm(a, b, dims=(((1,), (0,)), ((), ()))):
    return lax.dot_general(a, b, dims, preferred_element_type=F32)


def copies(pairs, sems):
    made = [pltpu.make_async_copy(src, dst, sems.at[i]) for i, (src, dst) in enumerate(pairs)]
    for copy in made:
        copy.start()
    return made


def slot_mask(owners, relative, cap, lengths, owner, slots, tokens):
    docs = lengths.shape[1]
    row = lax.broadcasted_iota(jnp.int32, (docs, docs), 0)
    col = lax.broadcasted_iota(jnp.int32, (docs, docs), 1)
    len_row = lengths.astype(F32)
    place_row = owner ^ lax.axis_index("dp") if relative else owner
    own_row = place_row.astype(F32)

    def column(values):
        return jnp.sum(jnp.where(row == col, values, 0.0), axis=1, keepdims=True)

    ends = jnp.sum(jnp.where(row <= col, column(len_row), 0.0), axis=0, keepdims=True)
    rank = jnp.sum(
        jnp.where((row < col) & (column(own_row) == own_row), 1.0, 0.0), axis=0, keepdims=True
    )
    slot = lax.broadcasted_iota(jnp.int32, (slots, docs), 0).astype(F32)
    hot = slot == own_row * cap + rank
    first = jnp.sum(jnp.where(hot, ends - len_row, 0.0), axis=1, keepdims=True)
    last = jnp.sum(jnp.where(hot, ends, 0.0), axis=1, keepdims=True)
    token = lax.broadcasted_iota(jnp.int32, (slots, tokens), 1).astype(F32)
    return jnp.where((token >= first) & (token < last), 1.0, 0.0)


def x_kernel(
    owners, relative, cap, act_hbm, in_hbm, len_hbm, own_hbm, x_ref, mask_ref,
    act, proj_in, lens, owner, sems,
):
    pairs = [(in_hbm, proj_in), (act_hbm, act), (len_hbm, lens), (own_hbm, owner)]
    in_copy, act_copy, len_copy, own_copy = copies(pairs, sems)
    len_copy.wait()
    own_copy.wait()
    mask_ref[...] = slot_mask(owners, relative, cap, lens[...], owner[...], *mask_ref.shape)
    in_copy.wait()
    act_copy.wait()
    x_ref[...] = mm(proj_in[...], act[...], NT)


def project_x(act, in_t, lengths, owner_row, owners, cap, relative):
    tokens, rank = act.shape[0], in_t.shape[0]
    hbm = pl.BlockSpec(memory_space=pl.ANY)
    vmem = pl.BlockSpec(memory_space=pltpu.VMEM)
    return pl.pallas_call(
        functools.partial(x_kernel, owners, relative, cap),
        in_specs=[hbm] * 4,
        out_specs=[vmem] * 2,
        out_shape=[
            jax.ShapeDtypeStruct((rank, tokens), F32),
            jax.ShapeDtypeStruct((owners * cap, tokens), F32),
        ],
        scratch_shapes=[
            pltpu.VMEM(act.shape, BF16),
            pltpu.VMEM(in_t.shape, BF16),
            pltpu.VMEM(lengths.shape, jnp.int32),
            pltpu.VMEM(owner_row.shape, jnp.int32),
            pltpu.SemaphoreType.DMA((4,)),
        ],
        compiler_params=params(24),
        cost_estimate=cost(15 * 10**8, 0),
    )(
        *(
            pltpu.with_memory_space_constraint(x, pltpu.HBM)
            for x in (act, in_t, lengths, owner_row)
        )
    )


def g_kernel(width, grad_ref, proj_ref, keep_ref, send_ref, full):
    full[...] = mm(proj_ref[...], grad_ref[...], NT)
    me = lax.axis_index("tensor")
    count = full.shape[0] // width
    for apart in range(count):
        block = pl.ds(pl.multiple_of((me ^ apart) * width, width), width)
        ref, spot = (keep_ref, apart) if apart < count // 2 else (send_ref, apart - count // 2)
        ref[spot * width : (spot + 1) * width, :] = full[block, :]


def project_g(grad, out_t, width):
    tokens, rank = grad.shape[0], out_t.shape[0]
    part = jax.ShapeDtypeStruct((rank // 2, tokens), F32)
    return pl.pallas_call(
        functools.partial(g_kernel, width),
        out_shape=[part, part],
        scratch_shapes=[pltpu.VMEM((rank, tokens), F32)],
        compiler_params=params(24),
        cost_estimate=cost(0, 0),
    )(grad, out_t)


def stack(refs):
    return jnp.concatenate([r[...] for r in refs], axis=0)


def fold_kernel(rank, owned, came, keep_ref, *refs):
    first_ref, second_ref, kept_ref = refs[-3:]
    got = stack(refs[owned : owned + came])
    total = keep_ref[...] + got[rank:]
    kept = kept_ref.shape[0]
    kept_ref[...] = total[:kept]
    x = stack(refs[:owned])[:rank] + got[:rank]
    sent = jnp.concatenate([x, total[kept:]], axis=0)
    cut = first_ref.shape[0]
    first_ref[...] = sent[:cut]
    second_ref[...] = sent[cut:]


def fold(rank, keep, own, gots, pieces):
    tokens = keep.shape[1]
    kept = keep.shape[0] // 2
    cut = (rank + kept) // 16 * 8
    *sent, keep = pl.pallas_call(
        functools.partial(fold_kernel, rank, len(own), len(gots)),
        in_specs=[pl.BlockSpec(memory_space=pltpu.VMEM)] * (1 + len(own) + len(gots))
        + [pl.BlockSpec(memory_space=pl.ANY)] * len(pieces),
        out_shape=[
            jax.ShapeDtypeStruct((rows, tokens), F32) for rows in (cut, rank + kept - cut, kept)
        ],
        compiler_params=params(16),
        cost_estimate=cost(0, 0),
    )(keep, *own, *gots, *pieces)
    return keep, sent


def outer_kernel(owners, sent, g_ref, mask_ref, *refs):
    blocks = refs[-owners:]
    width = g_ref.shape[0]
    own, got = stack(refs[:sent]), stack(refs[sent : 2 * sent])
    rank = got.shape[0] - width
    x_full = own[:rank] + got[:rank]
    g_full = g_ref[...] + got[rank:]
    x_both = jnp.concatenate(halves(x_full), axis=0)
    g_high = g_full.astype(BF16).astype(F32)
    g_low = g_full - g_high
    mask = mask_ref[...]
    cap = blocks[0].shape[0]

    def product(i):
        pair = [(mask * g[i : i + 1, :]).astype(BF16) for g in (g_high, g_low)]
        both = mm(jnp.concatenate(pair, axis=0), x_both, NT)
        slots = mask.shape[0]
        return both[:slots, :rank] + both[:slots, rank:] + both[slots:, :rank]

    step = max(1, 128 // rank)
    for i in range(0, width, step):
        columns = jnp.concatenate([product(i + j) for j in range(step)], axis=1)
        for k, block in enumerate(blocks):
            block[:, i * rank : (i + step) * rank] = columns[k * cap : (k + 1) * cap, :]


def outer(sent, gots, g, mask, owners, pieces):
    slots, tokens = mask.shape
    width = g.shape[0]
    rank = sum(p.shape[0] for p in sent) - width
    cap = slots // owners
    return pl.pallas_call(
        functools.partial(outer_kernel, owners, len(sent)),
        in_specs=[pl.BlockSpec(memory_space=pltpu.VMEM)] * (2 + 2 * len(sent))
        + [pl.BlockSpec(memory_space=pl.ANY)] * len(pieces),
        out_shape=[jax.ShapeDtypeStruct((cap, width * rank), F32)] * owners,
        compiler_params=params(24),
        cost_estimate=cost(8 * slots * width * tokens * rank, 4 * slots * width * rank),
    )(g, mask, *sent, *gots, *pieces)


def join_kernel(*refs):
    refs[-1][...] = stack(refs[:-1])


def join(block, pieces):
    rows = block.shape[0] + sum(p.shape[0] for p in pieces)
    return pl.pallas_call(
        join_kernel,
        out_shape=jax.ShapeDtypeStruct((rows, block.shape[1]), F32),
        compiler_params=params(16),
        cost_estimate=cost(0, 0),
    )(block, *pieces)


def score_kernel(count, early, size, gaps, relative, ids_ref, *refs):
    rows, pieces, scores_ref = refs[:count], refs[count:-1], refs[-1]
    queries = ids_ref.shape[1]
    me = lax.axis_index("dp")
    cap = rows[0].shape[0]
    high, low = halves(jnp.concatenate([r[:cap, :] for r in rows], axis=0))
    slots = high.shape[0]
    both = jnp.concatenate([high, low], axis=0)
    parts = [piece[...] for piece in pieces]
    parts += [rows[1][cap + i * size : cap + (i + 1) * size, :] for i in range(len(gaps) - early)]
    held = parts[0].shape[0]
    pool = jnp.concatenate(parts, axis=0)
    products = mm(both, jnp.concatenate(halves(pool), axis=0), NT)
    split = pool.shape[0]
    part = products[:slots, :split] + products[:slots, split:] + products[slots:, :split]
    row = lax.broadcasted_iota(jnp.int32, (held, queries), 0)
    places = [row + ((me ^ gap) * held if len(gaps) > 1 else 0) for gap in gaps]
    hot = (jnp.concatenate(places, axis=0) == ids_ref[...]).astype(F32).astype(BF16)
    top, rest = halves(part)
    last = (part - top.astype(F32) - rest.astype(F32)).astype(BF16)
    picked = mm(jnp.concatenate([top, rest, last], axis=0), hot)
    total = picked[:slots] + picked[slots : 2 * slots] + picked[2 * slots :]
    for k in range(count):
        spot = pl.ds(pl.multiple_of((me ^ k) * cap, cap), cap) if relative else pl.ds(k * cap, cap)
        scores_ref[spot, :] = total[k * cap : (k + 1) * cap, :]


def score(ids_row, rows, pieces, gaps, relative):
    slots = rows[0].shape[0] * len(rows)
    queries = ids_row.shape[1]
    size, feats = pieces[0].shape
    flops = 6 * slots * size * len(gaps) * feats
    return pl.pallas_call(
        functools.partial(score_kernel, len(rows), len(pieces), size, gaps, relative),
        out_shape=jax.ShapeDtypeStruct((slots, queries), F32),
        compiler_params=params(24),
        cost_estimate=cost(flops, 4 * size * len(gaps) * feats),
    )(ids_row, *rows, *pieces)


def place_kernel(*refs):
    rows, store_ref = refs[:-1], refs[-1]
    me = lax.axis_index("dp")
    cap = rows[0].shape[0]
    for k, row in enumerate(rows):
        store_ref[pl.ds(pl.multiple_of((me ^ k) * cap, cap), cap), :] = row[:cap, :]


def place(rows):
    slots, feats = rows[0].shape[0] * len(rows), rows[0].shape[1]
    return pl.pallas_call(
        place_kernel,
        out_shape=jax.ShapeDtypeStruct((slots, feats), F32),
        compiler_params=params(16),
        cost_estimate=cost(0, 8 * slots * feats),
    )(*rows)


def swap(x, axis, gap):
    return lax.ppermute(x, axis, [(i, i ^ gap) for i in range(lax.axis_size(axis))])


def gather_pieces(piece):
    pieces, gaps = [piece], [0]
    bit = lax.axis_size("dp") // 2
    while bit > 1:
        pieces, gaps = pieces + [swap(p, "dp", bit) for p in pieces], gaps + [g ^ bit for g in gaps]
        bit //= 2
    return pieces, gaps


def local(
    activations, out_grads, proj_in, proj_out, doc_lengths, doc_owner, query_grads, query_ids
):
    tensor_size = lax.axis_size("tensor")
    data_size = lax.axis_size("dp")
    tokens = activations.shape[0]
    rank = proj_in.shape[1]
    width = rank // tensor_size
    docs = doc_owner.shape[0]
    cap = max(2, 2 * docs // data_size)
    direct = data_size <= MOST_DIRECT

    if direct:
        pieces, gaps = gather_pieces(query_grads)
        mate = swap(query_grads, "dp", 1)
    else:
        pieces, gaps = [lax.all_gather(query_grads, "dp", axis=0, tiled=True)], [0]
        mate = pieces[0]

    x, mask = project_x(
        activations, proj_in.T, doc_lengths, doc_owner.T, data_size, cap, direct
    )
    bit = tensor_size // 2
    x_got = swap(x, "tensor", bit)
    keep, send = project_g(out_grads, proj_out.T, width)
    own, gots = [x], [x_got, swap(send, "tensor", bit)]
    while bit > 1:
        bit //= 2
        keep, own = fold(rank, keep, own, gots, pieces[1:])
        gots = [swap(part, "tensor", bit) for part in own]
    blocks = outer(own, gots, keep, mask, data_size, [mate])
    if direct:
        near = swap(join(blocks[1], pieces[1:]), "dp", 1)
        far = [swap(blocks[k], "dp", k) for k in range(2, data_size)]
        rows = [blocks[0], near, *far]
        pieces, gaps = [*pieces, mate], [*gaps, 1, *(g ^ 1 for g in gaps[1:])]
        store = place(rows)
    else:
        rows = [lax.all_to_all(jnp.stack(blocks), "dp", 0, 0, tiled=True).reshape(-1, width * rank)]
        store = rows[0]
    scores = score(query_ids[None, :], rows, pieces, gaps, direct)
    bit = 1
    while bit < tensor_size:
        scores = scores + swap(scores, "tensor", bit)
        bit *= 2
    return store, scores * (1.0 / (rank * rank))


def solution(mesh):
    return jax.shard_map(
        local,
        mesh=mesh,
        in_specs=(
            P(("groups", "dp"), "tensor"),
            P(("groups", "dp"), "tensor"),
            P("tensor", None),
            P("tensor", None),
            P(("groups", "dp"), None),
            P(("groups", "dp"), None),
            P(("groups", "dp"), "tensor"),
            P("groups"),
        ),
        out_specs=(P(("groups", "dp"), "tensor"), P(("groups", "dp"), None)),
        check_vma=False,
    )
```

```python
import functools

import jax
import jax.numpy as jnp
from jax import lax
from jax.experimental import pallas as pl
from jax.experimental.pallas import tpu as pltpu
from jax.sharding import PartitionSpec as P

F32 = jnp.float32
BF16 = jnp.bfloat16
MIB = 1024 * 1024
NT = (((1,), (1,)), ((), ()))
MOST_DIRECT = 8
LATE_FLOPS = 16 * 10**8


def params(mib):
    return pltpu.CompilerParams(vmem_limit_bytes=mib * MIB)


def cost(flops, nbytes):
    return pl.CostEstimate(flops=flops, bytes_accessed=nbytes, transcendentals=0)


def halves(x):
    high = x.astype(BF16)
    return high, (x - high.astype(F32)).astype(BF16)


def mm(a, b, dims=(((1,), (0,)), ((), ()))):
    return lax.dot_general(a, b, dims, preferred_element_type=F32)


def copies(pairs, sems):
    made = [pltpu.make_async_copy(src, dst, sems.at[i]) for i, (src, dst) in enumerate(pairs)]
    for copy in made:
        copy.start()
    return made


def slot_mask(owners, relative, cap, lengths, owner, slots, tokens):
    docs = lengths.shape[1]
    row = lax.broadcasted_iota(jnp.int32, (docs, docs), 0)
    col = lax.broadcasted_iota(jnp.int32, (docs, docs), 1)
    len_row = lengths.astype(F32)
    place_row = owner ^ lax.axis_index("dp") if relative else owner
    own_row = place_row.astype(F32)

    def column(values):
        return jnp.sum(jnp.where(row == col, values, 0.0), axis=1, keepdims=True)

    ends = jnp.sum(jnp.where(row <= col, column(len_row), 0.0), axis=0, keepdims=True)
    rank = jnp.sum(
        jnp.where((row < col) & (column(own_row) == own_row), 1.0, 0.0), axis=0, keepdims=True
    )
    slot = lax.broadcasted_iota(jnp.int32, (slots, docs), 0).astype(F32)
    hot = slot == own_row * cap + rank
    first = jnp.sum(jnp.where(hot, ends - len_row, 0.0), axis=1, keepdims=True)
    last = jnp.sum(jnp.where(hot, ends, 0.0), axis=1, keepdims=True)
    token = lax.broadcasted_iota(jnp.int32, (slots, tokens), 1).astype(F32)
    return jnp.where((token >= first) & (token < last), 1.0, 0.0)


def x_kernel(
    owners, relative, cap, act_hbm, in_hbm, len_hbm, own_hbm, keep_ref, send_ref, mask_ref,
    act, proj_in, lens, owner, sems,
):
    pairs = [(in_hbm, proj_in), (act_hbm, act), (len_hbm, lens), (own_hbm, owner)]
    in_copy, act_copy, len_copy, own_copy = copies(pairs, sems)
    len_copy.wait()
    own_copy.wait()
    mask_ref[...] = slot_mask(owners, relative, cap, lens[...], owner[...], *mask_ref.shape)
    in_copy.wait()
    act_copy.wait()
    full = mm(proj_in[...], act[...], NT)
    half = full.shape[0] // 2
    odd = lax.rem(lax.axis_index("tensor"), 2) == 1
    keep_ref[...] = jnp.where(odd, full[half:], full[:half])
    send_ref[...] = jnp.where(odd, full[:half], full[half:])


def project_x(act, in_t, lengths, owner_row, owners, cap, relative):
    tokens, rank = act.shape[0], in_t.shape[0]
    hbm = pl.BlockSpec(memory_space=pl.ANY)
    vmem = pl.BlockSpec(memory_space=pltpu.VMEM)
    return pl.pallas_call(
        functools.partial(x_kernel, owners, relative, cap),
        in_specs=[hbm] * 4,
        out_specs=[vmem] * 3,
        out_shape=[
            jax.ShapeDtypeStruct((rank // 2, tokens), F32),
            jax.ShapeDtypeStruct((rank // 2, tokens), F32),
            jax.ShapeDtypeStruct((owners * cap, tokens), F32),
        ],
        scratch_shapes=[
            pltpu.VMEM(act.shape, BF16),
            pltpu.VMEM(in_t.shape, BF16),
            pltpu.VMEM(lengths.shape, jnp.int32),
            pltpu.VMEM(owner_row.shape, jnp.int32),
            pltpu.SemaphoreType.DMA((4,)),
        ],
        compiler_params=params(24),
        cost_estimate=cost(15 * 10**8, 0),
    )(
        *(
            pltpu.with_memory_space_constraint(x, pltpu.HBM)
            for x in (act, in_t, lengths, owner_row)
        )
    )


def g_kernel(width, grad_ref, proj_ref, keep_ref, send_ref, full):
    full[...] = mm(proj_ref[...], grad_ref[...], NT)
    me = lax.axis_index("tensor")
    spot = 0
    for apart in range(full.shape[0] // width - 2, -1, -2):
        for ref, who in ((keep_ref, me ^ apart), (send_ref, me ^ (apart ^ 1))):
            block = pl.ds(pl.multiple_of(who * width, width), width)
            ref[spot : spot + width, :] = full[block, :]
        spot += width


def project_g(grad, out_t, width):
    tokens, rank = grad.shape[0], out_t.shape[0]
    part = jax.ShapeDtypeStruct((rank // 2, tokens), F32)
    return pl.pallas_call(
        functools.partial(g_kernel, width),
        out_shape=[part, part],
        scratch_shapes=[pltpu.VMEM((rank, tokens), F32)],
        compiler_params=params(24),
        cost_estimate=cost(0, 0),
    )(grad, out_t)


def stack(refs):
    return jnp.concatenate([r[...] for r in refs], axis=0)


def sum_kernel(cuts, *refs):
    count = len(cuts)
    outs = list(refs[2 * count :])
    for i, cut in enumerate(cuts):
        total = refs[i][...] + refs[count + i][...]
        if cut:
            outs.pop(0)[...] = total[:cut]
        outs.pop(0)[...] = total[cut:]


def add(owns, gots, cuts):
    shapes = []
    for own, cut in zip(owns, cuts):
        rows, tokens = own.shape
        shapes += [jax.ShapeDtypeStruct((n, tokens), F32) for n in (cut, rows - cut) if n]
    return pl.pallas_call(
        functools.partial(sum_kernel, tuple(cuts)),
        out_shape=shapes,
        compiler_params=params(16),
        cost_estimate=cost(0, 0),
    )(*owns, *gots)


def outer_kernel(x_ref, x_other_ref, g_ref, mask_ref, *blocks):
    width = g_ref.shape[0]
    rank = 2 * x_ref.shape[0]
    odd = lax.rem(lax.axis_index("tensor"), 2) == 1
    own, other = x_ref[...], x_other_ref[...]
    x_full = jnp.concatenate([jnp.where(odd, other, own), jnp.where(odd, own, other)], axis=0)
    g_full = g_ref[...]
    x_both = jnp.concatenate(halves(x_full), axis=0)
    g_high = g_full.astype(BF16).astype(F32)
    g_low = g_full - g_high
    mask = mask_ref[...]
    cap = blocks[0].shape[0]

    def product(i):
        pair = [(mask * g[i : i + 1, :]).astype(BF16) for g in (g_high, g_low)]
        both = mm(jnp.concatenate(pair, axis=0), x_both, NT)
        slots = mask.shape[0]
        return both[:slots, :rank] + both[:slots, rank:] + both[slots:, :rank]

    step = max(1, 128 // rank)
    for i in range(0, width, step):
        columns = jnp.concatenate([product(i + j) for j in range(step)], axis=1)
        for k, block in enumerate(blocks):
            block[:, i * rank : (i + step) * rank] = columns[k * cap : (k + 1) * cap, :]


def outer(x_half, x_other, g, mask, owners):
    slots, tokens = mask.shape
    width, rank = g.shape[0], 2 * x_half.shape[0]
    cap = slots // owners
    return pl.pallas_call(
        outer_kernel,
        out_shape=[jax.ShapeDtypeStruct((cap, width * rank), F32)] * owners,
        compiler_params=params(24),
        cost_estimate=cost(14 * slots * width * tokens * rank, 0),
    )(x_half, x_other, g, mask)


def pass_kernel(*refs):
    del refs


def pass_on(arrays, flops):
    anywhere = pl.BlockSpec(memory_space=pl.ANY)
    return pl.pallas_call(
        pass_kernel,
        in_specs=[anywhere] * len(arrays),
        out_specs=[anywhere] * len(arrays),
        out_shape=[jax.ShapeDtypeStruct(a.shape, a.dtype) for a in arrays],
        input_output_aliases={i: i for i in range(len(arrays))},
        cost_estimate=cost(flops, 0),
    )(*arrays)


def join_kernel(*refs):
    refs[-1][...] = stack(refs[:-1])


def join(block, pieces):
    rows = block.shape[0] + sum(p.shape[0] for p in pieces)
    return pl.pallas_call(
        join_kernel,
        out_shape=jax.ShapeDtypeStruct((rows, block.shape[1]), F32),
        compiler_params=params(16),
        cost_estimate=cost(0, 0),
    )(block, *pieces)


def score_kernel(count, early, size, gaps, relative, ids_ref, *refs):
    rows, pieces, scores_ref = refs[:count], refs[count:-1], refs[-1]
    queries = ids_ref.shape[1]
    me = lax.axis_index("dp")
    cap = rows[0].shape[0]
    high, low = halves(jnp.concatenate([r[:cap, :] for r in rows], axis=0))
    slots = high.shape[0]
    both = jnp.concatenate([high, low], axis=0)
    parts = [piece[...] for piece in pieces]
    parts += [rows[1][cap + i * size : cap + (i + 1) * size, :] for i in range(len(gaps) - early)]
    held = parts[0].shape[0]
    pool = jnp.concatenate(parts, axis=0)
    products = mm(both, jnp.concatenate(halves(pool), axis=0), NT)
    split = pool.shape[0]
    part = products[:slots, :split] + products[:slots, split:] + products[slots:, :split]
    row = lax.broadcasted_iota(jnp.int32, (held, queries), 0)
    places = [row + ((me ^ gap) * held if len(gaps) > 1 else 0) for gap in gaps]
    hot = (jnp.concatenate(places, axis=0) == ids_ref[...]).astype(F32).astype(BF16)
    top, rest = halves(part)
    last = (part - top.astype(F32) - rest.astype(F32)).astype(BF16)
    picked = mm(jnp.concatenate([top, rest, last], axis=0), hot)
    total = picked[:slots] + picked[slots : 2 * slots] + picked[2 * slots :]
    for k in range(count):
        spot = pl.ds(pl.multiple_of((me ^ k) * cap, cap), cap) if relative else pl.ds(k * cap, cap)
        scores_ref[spot, :] = total[k * cap : (k + 1) * cap, :]


def score(ids_row, rows, pieces, gaps, relative):
    slots = rows[0].shape[0] * len(rows)
    queries = ids_row.shape[1]
    size, feats = pieces[0].shape
    flops = 6 * slots * size * len(gaps) * feats
    return pl.pallas_call(
        functools.partial(score_kernel, len(rows), len(pieces), size, gaps, relative),
        out_shape=jax.ShapeDtypeStruct((slots, queries), F32),
        compiler_params=params(24),
        cost_estimate=cost(flops, 4 * size * len(gaps) * feats),
    )(ids_row, *rows, *pieces)


def place_kernel(*refs):
    rows, store_ref = refs[:-1], refs[-1]
    me = lax.axis_index("dp")
    cap = rows[0].shape[0]
    for k, row in enumerate(rows):
        store_ref[pl.ds(pl.multiple_of((me ^ k) * cap, cap), cap), :] = row[:cap, :]


def place(rows):
    slots, feats = rows[0].shape[0] * len(rows), rows[0].shape[1]
    return pl.pallas_call(
        place_kernel,
        out_shape=jax.ShapeDtypeStruct((slots, feats), F32),
        compiler_params=params(16),
        cost_estimate=cost(0, 8 * slots * feats),
    )(*rows)


def swap(x, axis, gap):
    return lax.ppermute(x, axis, [(i, i ^ gap) for i in range(lax.axis_size(axis))])


def gather_pieces(piece):
    pieces, gaps = [piece], [0]
    bit = lax.axis_size("dp") // 2
    while bit > 1:
        pieces, gaps = pieces + [swap(p, "dp", bit) for p in pieces], gaps + [g ^ bit for g in gaps]
        bit //= 2
    return pieces, gaps


def local(
    activations, out_grads, proj_in, proj_out, doc_lengths, doc_owner, query_grads, query_ids
):
    tensor_size = lax.axis_size("tensor")
    data_size = lax.axis_size("dp")
    tokens = activations.shape[0]
    rank = proj_in.shape[1]
    width = rank // tensor_size
    docs = doc_owner.shape[0]
    cap = max(2, 2 * docs // data_size)
    direct = data_size <= MOST_DIRECT

    if direct:
        pieces, gaps = gather_pieces(query_grads)
        mate = swap(query_grads, "dp", 1)
    else:
        pieces, gaps = [lax.all_gather(query_grads, "dp", axis=0, tiled=True)], [0]

    x_keep, x_send, mask = project_x(
        activations, proj_in.T, doc_lengths, doc_owner.T, data_size, cap, direct
    )
    x_got = swap(x_send, "tensor", 1)
    g_keep, g_send = project_g(out_grads, proj_out.T, width)
    (x_half,) = add([x_keep], [x_got], [0])
    bit = tensor_size // 2
    parts = add([g_keep], [swap(g_send, "tensor", 1)], [g_keep.shape[0] // 2 if bit > 1 else 0])
    while bit > 1:
        away, g_mine = parts
        gots = [swap(x_half, "tensor", bit), swap(away, "tensor", bit)]
        bit //= 2
        x_half, *parts = add([x_half, g_mine], gots, [0, g_mine.shape[0] // 2 if bit > 1 else 0])
    x_other = swap(x_half, "tensor", 1)
    blocks = outer(x_half, x_other, parts[0], mask, data_size)
    if direct:
        far = [swap(blocks[k], "dp", k) for k in range(data_size - 1, 1, -1)]
        near = swap(join(blocks[1], pieces[1:]), "dp", 1)
        mate, *far = pass_on([mate, *far], LATE_FLOPS)
        rows = [blocks[0], near, *far[::-1]]
        pieces, gaps = [*pieces, mate], [*gaps, 1, *(g ^ 1 for g in gaps[1:])]
        store = place(rows)
    else:
        rows = [lax.all_to_all(jnp.stack(blocks), "dp", 0, 0, tiled=True).reshape(-1, width * rank)]
        store = rows[0]
    scores = score(query_ids[None, :], rows, pieces, gaps, direct)
    bit = 1
    while bit < tensor_size:
        scores = scores + swap(scores, "tensor", bit)
        bit *= 2
    return store, scores * (1.0 / (rank * rank))


def solution(mesh):
    return jax.shard_map(
        local,
        mesh=mesh,
        in_specs=(
            P(("groups", "dp"), "tensor"),
            P(("groups", "dp"), "tensor"),
            P("tensor", None),
            P("tensor", None),
            P(("groups", "dp"), None),
            P(("groups", "dp"), None),
            P(("groups", "dp"), "tensor"),
            P("groups"),
        ),
        out_specs=(P(("groups", "dp"), "tensor"), P(("groups", "dp"), None)),
        check_vma=False,
    )
```

```python
import functools

import jax
import jax.numpy as jnp
from jax import lax
from jax.experimental import pallas as pl
from jax.experimental.pallas import tpu as pltpu
from jax.sharding import PartitionSpec as P

F32 = jnp.float32
BF16 = jnp.bfloat16
MIB = 1024 * 1024
NT = (((1,), (1,)), ((), ()))
MOST_DIRECT = 8
EARLY_FLOPS = 3 * 10**8
LATE_FLOPS = 13 * 10**8


def params(mib):
    return pltpu.CompilerParams(vmem_limit_bytes=mib * MIB)


def cost(flops, nbytes):
    return pl.CostEstimate(flops=flops, bytes_accessed=nbytes, transcendentals=0)


def halves(x):
    high = x.astype(BF16)
    return high, (x - high.astype(F32)).astype(BF16)


def mm(a, b, dims=(((1,), (0,)), ((), ()))):
    return lax.dot_general(a, b, dims, preferred_element_type=F32)


def copies(pairs, sems):
    made = [pltpu.make_async_copy(src, dst, sems.at[i]) for i, (src, dst) in enumerate(pairs)]
    for copy in made:
        copy.start()
    return made


def slot_mask(owners, relative, cap, lengths, owner, slots, tokens):
    docs = lengths.shape[1]
    row = lax.broadcasted_iota(jnp.int32, (docs, docs), 0)
    col = lax.broadcasted_iota(jnp.int32, (docs, docs), 1)
    len_row = lengths.astype(F32)
    place_row = owner ^ lax.axis_index("dp") if relative else owner
    own_row = place_row.astype(F32)

    def column(values):
        return jnp.sum(jnp.where(row == col, values, 0.0), axis=1, keepdims=True)

    ends = jnp.sum(jnp.where(row <= col, column(len_row), 0.0), axis=0, keepdims=True)
    rank = jnp.sum(
        jnp.where((row < col) & (column(own_row) == own_row), 1.0, 0.0), axis=0, keepdims=True
    )
    slot = lax.broadcasted_iota(jnp.int32, (slots, docs), 0).astype(F32)
    hot = slot == own_row * cap + rank
    first = jnp.sum(jnp.where(hot, ends - len_row, 0.0), axis=1, keepdims=True)
    last = jnp.sum(jnp.where(hot, ends, 0.0), axis=1, keepdims=True)
    token = lax.broadcasted_iota(jnp.int32, (slots, tokens), 1).astype(F32)
    return jnp.where((token >= first) & (token < last), 1.0, 0.0)


def x_kernel(
    owners, relative, cap, act_hbm, in_hbm, len_hbm, own_hbm, keep_ref, send_ref, mask_ref,
    act, proj_in, lens, owner, sems,
):
    pairs = [(in_hbm, proj_in), (act_hbm, act), (len_hbm, lens), (own_hbm, owner)]
    in_copy, act_copy, len_copy, own_copy = copies(pairs, sems)
    len_copy.wait()
    own_copy.wait()
    mask_ref[...] = slot_mask(owners, relative, cap, lens[...], owner[...], *mask_ref.shape)
    in_copy.wait()
    act_copy.wait()
    full = mm(proj_in[...], act[...], NT)
    half = full.shape[0] // 2
    odd = lax.rem(lax.axis_index("tensor"), 2) == 1
    keep_ref[...] = jnp.where(odd, full[half:], full[:half])
    send_ref[...] = jnp.where(odd, full[:half], full[half:])


def project_x(act, in_t, lengths, owner_row, owners, cap, relative):
    tokens, rank = act.shape[0], in_t.shape[0]
    hbm = pl.BlockSpec(memory_space=pl.ANY)
    vmem = pl.BlockSpec(memory_space=pltpu.VMEM)
    return pl.pallas_call(
        functools.partial(x_kernel, owners, relative, cap),
        in_specs=[hbm] * 4,
        out_specs=[vmem] * 3,
        out_shape=[
            jax.ShapeDtypeStruct((rank // 2, tokens), F32),
            jax.ShapeDtypeStruct((rank // 2, tokens), F32),
            jax.ShapeDtypeStruct((owners * cap, tokens), F32),
        ],
        scratch_shapes=[
            pltpu.VMEM(act.shape, BF16),
            pltpu.VMEM(in_t.shape, BF16),
            pltpu.VMEM(lengths.shape, jnp.int32),
            pltpu.VMEM(owner_row.shape, jnp.int32),
            pltpu.SemaphoreType.DMA((4,)),
        ],
        compiler_params=params(24),
        cost_estimate=cost(15 * 10**8, 0),
    )(
        *(
            pltpu.with_memory_space_constraint(x, pltpu.HBM)
            for x in (act, in_t, lengths, owner_row)
        )
    )


def g_kernel(width, grad_ref, proj_ref, keep_ref, send_ref, full):
    full[...] = mm(proj_ref[...], grad_ref[...], NT)
    me = lax.axis_index("tensor")
    spot = 0
    for apart in range(full.shape[0] // width - 2, -1, -2):
        for ref, who in ((keep_ref, me ^ apart), (send_ref, me ^ (apart ^ 1))):
            block = pl.ds(pl.multiple_of(who * width, width), width)
            ref[spot : spot + width, :] = full[block, :]
        spot += width


def project_g(grad, out_t, width):
    tokens, rank = grad.shape[0], out_t.shape[0]
    part = jax.ShapeDtypeStruct((rank // 2, tokens), F32)
    return pl.pallas_call(
        functools.partial(g_kernel, width),
        out_shape=[part, part],
        scratch_shapes=[pltpu.VMEM((rank, tokens), F32)],
        compiler_params=params(24),
        cost_estimate=cost(0, 0),
    )(grad, out_t)


def stack(refs):
    return jnp.concatenate([r[...] for r in refs], axis=0)


def sum_kernel(cuts, tokens, *refs):
    count = len(cuts)
    outs = list(refs[2 * count + tokens :])
    for i, cut in enumerate(cuts):
        total = refs[i][...] + refs[count + i][...]
        if cut:
            outs.pop(0)[...] = total[:cut]
        outs.pop(0)[...] = total[cut:]


def add(owns, gots, cuts, tokens=()):
    shapes = []
    for own, cut in zip(owns, cuts):
        rows, width = own.shape
        shapes += [jax.ShapeDtypeStruct((n, width), F32) for n in (cut, rows - cut) if n]
    vmem = pl.BlockSpec(memory_space=pltpu.VMEM)
    anywhere = pl.BlockSpec(memory_space=pl.ANY)
    return pl.pallas_call(
        functools.partial(sum_kernel, tuple(cuts), len(tokens)),
        in_specs=[vmem] * (2 * len(cuts)) + [anywhere] * len(tokens),
        out_shape=shapes,
        compiler_params=params(16),
        cost_estimate=cost(0, 0),
    )(*owns, *gots, *tokens)


def outer_kernel(x_ref, x_other_ref, g_ref, mask_ref, *blocks):
    width = g_ref.shape[0]
    rank = 2 * x_ref.shape[0]
    odd = lax.rem(lax.axis_index("tensor"), 2) == 1
    own, other = x_ref[...], x_other_ref[...]
    x_full = jnp.concatenate([jnp.where(odd, other, own), jnp.where(odd, own, other)], axis=0)
    g_full = g_ref[...]
    x_both = jnp.concatenate(halves(x_full), axis=0)
    g_high = g_full.astype(BF16).astype(F32)
    g_low = g_full - g_high
    mask = mask_ref[...]
    cap = blocks[0].shape[0]

    def product(i):
        pair = [(mask * g[i : i + 1, :]).astype(BF16) for g in (g_high, g_low)]
        both = mm(jnp.concatenate(pair, axis=0), x_both, NT)
        slots = mask.shape[0]
        return both[:slots, :rank] + both[:slots, rank:] + both[slots:, :rank]

    step = max(1, 128 // rank)
    for i in range(0, width, step):
        columns = jnp.concatenate([product(i + j) for j in range(step)], axis=1)
        for k, block in enumerate(blocks):
            block[:, i * rank : (i + step) * rank] = columns[k * cap : (k + 1) * cap, :]


def outer(x_half, x_other, g, mask, owners):
    slots, tokens = mask.shape
    width, rank = g.shape[0], 2 * x_half.shape[0]
    cap = slots // owners
    return pl.pallas_call(
        outer_kernel,
        out_shape=[jax.ShapeDtypeStruct((cap, width * rank), F32)] * owners,
        compiler_params=params(24),
        cost_estimate=cost(14 * slots * width * tokens * rank, 0),
    )(x_half, x_other, g, mask)


def token_kernel(*refs):
    refs[-1][...] = jnp.zeros_like(refs[-1])


def token(arrays, flops):
    return pl.pallas_call(
        token_kernel,
        in_specs=[pl.BlockSpec(memory_space=pl.ANY)] * len(arrays),
        out_shape=jax.ShapeDtypeStruct((8, 128), F32),
        cost_estimate=cost(flops, 0),
    )(*arrays)


def join_kernel(*refs):
    refs[-1][...] = stack(refs[:-1])


def join(block, pieces):
    rows = block.shape[0] + sum(p.shape[0] for p in pieces)
    return pl.pallas_call(
        join_kernel,
        out_shape=jax.ShapeDtypeStruct((rows, block.shape[1]), F32),
        compiler_params=params(16),
        cost_estimate=cost(0, 0),
    )(block, *pieces)


def score_kernel(count, early, size, gaps, relative, ids_ref, *refs):
    rows, pieces, scores_ref = refs[:count], refs[count : count + early], refs[-1]
    queries = ids_ref.shape[1]
    me = lax.axis_index("dp")
    cap = rows[0].shape[0]
    high, low = halves(jnp.concatenate([r[:cap, :] for r in rows], axis=0))
    slots = high.shape[0]
    both = jnp.concatenate([high, low], axis=0)
    parts = [piece[...] for piece in pieces]
    parts += [rows[1][cap + i * size : cap + (i + 1) * size, :] for i in range(len(gaps) - early)]
    held = parts[0].shape[0]
    pool = jnp.concatenate(parts, axis=0)
    products = mm(both, jnp.concatenate(halves(pool), axis=0), NT)
    split = pool.shape[0]
    part = products[:slots, :split] + products[:slots, split:] + products[slots:, :split]
    row = lax.broadcasted_iota(jnp.int32, (held, queries), 0)
    places = [row + ((me ^ gap) * held if len(gaps) > 1 else 0) for gap in gaps]
    hot = (jnp.concatenate(places, axis=0) == ids_ref[...]).astype(F32).astype(BF16)
    top, rest = halves(part)
    last = (part - top.astype(F32) - rest.astype(F32)).astype(BF16)
    picked = mm(jnp.concatenate([top, rest, last], axis=0), hot)
    total = picked[:slots] + picked[slots : 2 * slots] + picked[2 * slots :]
    for k in range(count):
        spot = pl.ds(pl.multiple_of((me ^ k) * cap, cap), cap) if relative else pl.ds(k * cap, cap)
        scores_ref[spot, :] = total[k * cap : (k + 1) * cap, :]


def score(ids_row, rows, pieces, gaps, relative, tokens):
    slots = rows[0].shape[0] * len(rows)
    queries = ids_row.shape[1]
    size, feats = pieces[0].shape
    flops = 6 * slots * size * len(gaps) * feats
    return pl.pallas_call(
        functools.partial(score_kernel, len(rows), len(pieces), size, gaps, relative),
        in_specs=[pl.BlockSpec(memory_space=pltpu.VMEM)] * (1 + len(rows) + len(pieces))
        + [pl.BlockSpec(memory_space=pl.ANY)] * len(tokens),
        out_shape=jax.ShapeDtypeStruct((slots, queries), F32),
        compiler_params=params(24),
        cost_estimate=cost(flops, 4 * size * len(gaps) * feats),
    )(ids_row, *rows, *pieces, *tokens)


def place_kernel(*refs):
    rows, store_ref = refs[:-1], refs[-1]
    me = lax.axis_index("dp")
    cap = rows[0].shape[0]
    for k, row in enumerate(rows):
        store_ref[pl.ds(pl.multiple_of((me ^ k) * cap, cap), cap), :] = row[:cap, :]


def place(rows):
    slots, feats = rows[0].shape[0] * len(rows), rows[0].shape[1]
    return pl.pallas_call(
        place_kernel,
        out_shape=jax.ShapeDtypeStruct((slots, feats), F32),
        compiler_params=params(16),
        cost_estimate=cost(0, 8 * slots * feats),
    )(*rows)


def swap(x, axis, gap):
    return lax.ppermute(x, axis, [(i, i ^ gap) for i in range(lax.axis_size(axis))])


def gather_pieces(piece):
    pieces, gaps = [piece], [0]
    bit = lax.axis_size("dp") // 2
    while bit > 1:
        pieces, gaps = pieces + [swap(p, "dp", bit) for p in pieces], gaps + [g ^ bit for g in gaps]
        bit //= 2
    return pieces, gaps


def local(
    activations, out_grads, proj_in, proj_out, doc_lengths, doc_owner, query_grads, query_ids
):
    tensor_size = lax.axis_size("tensor")
    data_size = lax.axis_size("dp")
    tokens = activations.shape[0]
    rank = proj_in.shape[1]
    width = rank // tensor_size
    docs = doc_owner.shape[0]
    cap = max(2, 2 * docs // data_size)
    direct = data_size <= MOST_DIRECT

    if direct:
        pieces, gaps = gather_pieces(query_grads)
        mate = swap(query_grads, "dp", 1)
    else:
        pieces, gaps = [lax.all_gather(query_grads, "dp", axis=0, tiled=True)], [0]

    x_keep, x_send, mask = project_x(
        activations, proj_in.T, doc_lengths, doc_owner.T, data_size, cap, direct
    )
    x_got = swap(x_send, "tensor", 1)
    g_keep, g_send = project_g(out_grads, proj_out.T, width)
    (x_half,) = add([x_keep], [x_got], [0])
    bit = tensor_size // 2
    parts = add([g_keep], [swap(g_send, "tensor", 1)], [g_keep.shape[0] // 2 if bit > 1 else 0])
    while bit > 1:
        away, g_mine = parts
        gots = [swap(x_half, "tensor", bit), swap(away, "tensor", bit)]
        bit //= 2
        early = [token(pieces[1:], EARLY_FLOPS)] if direct and bit == 1 else []
        cut = g_mine.shape[0] // 2 if bit > 1 else 0
        x_half, *parts = add([x_half, g_mine], gots, [0, cut], early)
    x_other = swap(x_half, "tensor", 1)
    blocks = outer(x_half, x_other, parts[0], mask, data_size)
    if direct:
        far = [swap(blocks[k], "dp", k) for k in range(data_size - 1, 1, -1)]
        near = swap(join(blocks[1], pieces[1:]), "dp", 1)
        late = [token([mate, *far], LATE_FLOPS)]
        rows = [blocks[0], near, *far[::-1]]
        pieces, gaps = [*pieces, mate], [*gaps, 1, *(g ^ 1 for g in gaps[1:])]
        store = place(rows)
    else:
        rows = [lax.all_to_all(jnp.stack(blocks), "dp", 0, 0, tiled=True).reshape(-1, width * rank)]
        store, late = rows[0], []
    scores = score(query_ids[None, :], rows, pieces, gaps, direct, late)
    bit = 1
    while bit < tensor_size:
        scores = scores + swap(scores, "tensor", bit)
        bit *= 2
    return store, scores * (1.0 / (rank * rank))


def solution(mesh):
    return jax.shard_map(
        local,
        mesh=mesh,
        in_specs=(
            P(("groups", "dp"), "tensor"),
            P(("groups", "dp"), "tensor"),
            P("tensor", None),
            P("tensor", None),
            P(("groups", "dp"), None),
            P(("groups", "dp"), None),
            P(("groups", "dp"), "tensor"),
            P("groups"),
        ),
        out_specs=(P(("groups", "dp"), "tensor"), P(("groups", "dp"), None)),
        check_vma=False,
    )
```

```python
import functools

import jax
import jax.numpy as jnp
from jax import lax
from jax.experimental import pallas as pl
from jax.experimental.pallas import tpu as pltpu
from jax.sharding import PartitionSpec as P

F32 = jnp.float32
BF16 = jnp.bfloat16
MIB = 1024 * 1024
NT = (((1,), (1,)), ((), ()))
MOST_DIRECT = 8
EARLY_FLOPS = 3 * 10**8
LATE_FLOPS = 2 * 10**8


def params(mib):
    return pltpu.CompilerParams(vmem_limit_bytes=mib * MIB)


def cost(flops, nbytes):
    return pl.CostEstimate(flops=flops, bytes_accessed=nbytes, transcendentals=0)


def halves(x):
    high = x.astype(BF16)
    return high, (x - high.astype(F32)).astype(BF16)


def mm(a, b, dims=(((1,), (0,)), ((), ()))):
    return lax.dot_general(a, b, dims, preferred_element_type=F32)


def copies(pairs, sems):
    made = [pltpu.make_async_copy(src, dst, sems.at[i]) for i, (src, dst) in enumerate(pairs)]
    for copy in made:
        copy.start()
    return made


def slot_mask(owners, relative, cap, lengths, owner, slots, tokens):
    docs = lengths.shape[1]
    row = lax.broadcasted_iota(jnp.int32, (docs, docs), 0)
    col = lax.broadcasted_iota(jnp.int32, (docs, docs), 1)
    len_row = lengths.astype(F32)
    place_row = owner ^ lax.axis_index("dp") if relative else owner
    own_row = place_row.astype(F32)

    def column(values):
        return jnp.sum(jnp.where(row == col, values, 0.0), axis=1, keepdims=True)

    ends = jnp.sum(jnp.where(row <= col, column(len_row), 0.0), axis=0, keepdims=True)
    rank = jnp.sum(
        jnp.where((row < col) & (column(own_row) == own_row), 1.0, 0.0), axis=0, keepdims=True
    )
    slot = lax.broadcasted_iota(jnp.int32, (slots, docs), 0).astype(F32)
    hot = slot == own_row * cap + rank
    first = jnp.sum(jnp.where(hot, ends - len_row, 0.0), axis=1, keepdims=True)
    last = jnp.sum(jnp.where(hot, ends, 0.0), axis=1, keepdims=True)
    token = lax.broadcasted_iota(jnp.int32, (slots, tokens), 1).astype(F32)
    return jnp.where((token >= first) & (token < last), 1.0, 0.0)


def x_kernel(
    owners, relative, cap, act_hbm, in_hbm, len_hbm, own_hbm, x_ref, mask_ref,
    act, proj_in, lens, owner, sems,
):
    pairs = [(in_hbm, proj_in), (act_hbm, act), (len_hbm, lens), (own_hbm, owner)]
    in_copy, act_copy, len_copy, own_copy = copies(pairs, sems)
    len_copy.wait()
    own_copy.wait()
    mask_ref[...] = slot_mask(owners, relative, cap, lens[...], owner[...], *mask_ref.shape)
    in_copy.wait()
    act_copy.wait()
    x_ref[...] = mm(proj_in[...], act[...], NT)


def project_x(act, in_t, lengths, owner_row, owners, cap, relative):
    tokens, rank = act.shape[0], in_t.shape[0]
    hbm = pl.BlockSpec(memory_space=pl.ANY)
    vmem = pl.BlockSpec(memory_space=pltpu.VMEM)
    return pl.pallas_call(
        functools.partial(x_kernel, owners, relative, cap),
        in_specs=[hbm] * 4,
        out_specs=[vmem] * 2,
        out_shape=[
            jax.ShapeDtypeStruct((rank, tokens), F32),
            jax.ShapeDtypeStruct((owners * cap, tokens), F32),
        ],
        scratch_shapes=[
            pltpu.VMEM(act.shape, BF16),
            pltpu.VMEM(in_t.shape, BF16),
            pltpu.VMEM(lengths.shape, jnp.int32),
            pltpu.VMEM(owner_row.shape, jnp.int32),
            pltpu.SemaphoreType.DMA((4,)),
        ],
        compiler_params=params(24),
        cost_estimate=cost(15 * 10**8, 0),
    )(
        *(
            pltpu.with_memory_space_constraint(x, pltpu.HBM)
            for x in (act, in_t, lengths, owner_row)
        )
    )


def g_kernel(width, grad_ref, proj_ref, keep_ref, send_ref, full):
    full[...] = mm(proj_ref[...], grad_ref[...], NT)
    me = lax.axis_index("tensor")
    count = full.shape[0] // width
    for apart in range(count):
        block = pl.ds(pl.multiple_of((me ^ apart) * width, width), width)
        ref, spot = (keep_ref, apart) if apart < count // 2 else (send_ref, apart - count // 2)
        ref[spot * width : (spot + 1) * width, :] = full[block, :]


def project_g(grad, out_t, width):
    tokens, rank = grad.shape[0], out_t.shape[0]
    part = jax.ShapeDtypeStruct((rank // 2, tokens), F32)
    return pl.pallas_call(
        functools.partial(g_kernel, width),
        out_shape=[part, part],
        scratch_shapes=[pltpu.VMEM((rank, tokens), F32)],
        compiler_params=params(24),
        cost_estimate=cost(0, 0),
    )(grad, out_t)


def stack(refs):
    return jnp.concatenate([r[...] for r in refs], axis=0)


def fold_kernel(rank, owned, came, keep_ref, *refs):
    first_ref, second_ref, kept_ref = refs[-3:]
    got = stack(refs[owned : owned + came])
    total = keep_ref[...] + got[rank:]
    kept = kept_ref.shape[0]
    kept_ref[...] = total[:kept]
    x = stack(refs[:owned])[:rank] + got[:rank]
    sent = jnp.concatenate([x, total[kept:]], axis=0)
    cut = first_ref.shape[0]
    first_ref[...] = sent[:cut]
    second_ref[...] = sent[cut:]


def fold(rank, keep, own, gots, pieces):
    tokens = keep.shape[1]
    kept = keep.shape[0] // 2
    cut = (rank + kept) // 16 * 8
    *sent, keep = pl.pallas_call(
        functools.partial(fold_kernel, rank, len(own), len(gots)),
        in_specs=[pl.BlockSpec(memory_space=pltpu.VMEM)] * (1 + len(own) + len(gots))
        + [pl.BlockSpec(memory_space=pl.ANY)] * len(pieces),
        out_shape=[
            jax.ShapeDtypeStruct((rows, tokens), F32) for rows in (cut, rank + kept - cut, kept)
        ],
        compiler_params=params(16),
        cost_estimate=cost(0, 0),
    )(keep, *own, *gots, *pieces)
    return keep, sent


def outer_kernel(owners, sent, g_ref, mask_ref, *refs):
    blocks = refs[-owners:]
    width = g_ref.shape[0]
    own, got = stack(refs[:sent]), stack(refs[sent : 2 * sent])
    rank = got.shape[0] - width
    x_full = own[:rank] + got[:rank]
    g_full = g_ref[...] + got[rank:]
    x_both = jnp.concatenate(halves(x_full), axis=0)
    g_high = g_full.astype(BF16).astype(F32)
    g_low = g_full - g_high
    mask = mask_ref[...]
    cap = blocks[0].shape[0]

    def product(i):
        pair = [(mask * g[i : i + 1, :]).astype(BF16) for g in (g_high, g_low)]
        both = mm(jnp.concatenate(pair, axis=0), x_both, NT)
        slots = mask.shape[0]
        return both[:slots, :rank] + both[:slots, rank:] + both[slots:, :rank]

    step = max(1, 128 // rank)
    for i in range(0, width, step):
        columns = jnp.concatenate([product(i + j) for j in range(step)], axis=1)
        for k, block in enumerate(blocks):
            block[:, i * rank : (i + step) * rank] = columns[k * cap : (k + 1) * cap, :]


def outer(sent, gots, g, mask, owners):
    slots, tokens = mask.shape
    width = g.shape[0]
    rank = sum(p.shape[0] for p in sent) - width
    cap = slots // owners
    return pl.pallas_call(
        functools.partial(outer_kernel, owners, len(sent)),
        out_shape=[jax.ShapeDtypeStruct((cap, width * rank), F32)] * owners,
        compiler_params=params(24),
        cost_estimate=cost(8 * slots * width * tokens * rank, 4 * slots * width * rank),
    )(g, mask, *sent, *gots)


def token_kernel(*refs):
    refs[-1][...] = jnp.zeros_like(refs[-1])


def token(arrays, flops):
    return pl.pallas_call(
        token_kernel,
        in_specs=[pl.BlockSpec(memory_space=pl.ANY)] * len(arrays),
        out_shape=jax.ShapeDtypeStruct((8, 128), F32),
        compiler_params=params(4),
        cost_estimate=cost(flops, 0),
    )(*arrays)


def after_kernel(block_ref, piece, out_ref):
    out_ref[...] = block_ref[...]


def after(block, piece):
    return pl.pallas_call(
        after_kernel,
        in_specs=[pl.BlockSpec(memory_space=pltpu.VMEM), pl.BlockSpec(memory_space=pl.ANY)],
        out_shape=jax.ShapeDtypeStruct(block.shape, F32),
        compiler_params=params(4),
        cost_estimate=cost(0, 0),
    )(block, piece)


def score_kernel(count, gaps, relative, ids_ref, *refs):
    rows, pieces, scores_ref = refs[:count], refs[count : count + len(gaps)], refs[-1]
    queries = ids_ref.shape[1]
    me = lax.axis_index("dp")
    cap = rows[0].shape[0]
    high, low = halves(stack(rows))
    slots = high.shape[0]
    both = jnp.concatenate([high, low], axis=0)
    held = pieces[0].shape[0]
    pool = stack(pieces)
    products = mm(both, jnp.concatenate(halves(pool), axis=0), NT)
    split = pool.shape[0]
    part = products[:slots, :split] + products[:slots, split:] + products[slots:, :split]
    row = lax.broadcasted_iota(jnp.int32, (held, queries), 0)
    places = [row + ((me ^ gap) * held if len(gaps) > 1 else 0) for gap in gaps]
    hot = (jnp.concatenate(places, axis=0) == ids_ref[...]).astype(F32).astype(BF16)
    top, rest = halves(part)
    last = (part - top.astype(F32) - rest.astype(F32)).astype(BF16)
    picked = mm(jnp.concatenate([top, rest, last], axis=0), hot)
    total = picked[:slots] + picked[slots : 2 * slots] + picked[2 * slots :]
    for k in range(count):
        spot = pl.ds(pl.multiple_of((me ^ k) * cap, cap), cap) if relative else pl.ds(k * cap, cap)
        scores_ref[spot, :] = total[k * cap : (k + 1) * cap, :]


def score(ids_row, rows, pieces, gaps, relative, tokens):
    slots = rows[0].shape[0] * len(rows)
    queries = ids_row.shape[1]
    size, feats = pieces[0].shape
    flops = 6 * slots * size * len(gaps) * feats
    return pl.pallas_call(
        functools.partial(score_kernel, len(rows), gaps, relative),
        in_specs=[pl.BlockSpec(memory_space=pltpu.VMEM)] * (1 + len(rows) + len(pieces))
        + [pl.BlockSpec(memory_space=pl.ANY)] * len(tokens),
        out_shape=jax.ShapeDtypeStruct((slots, queries), F32),
        compiler_params=params(24),
        cost_estimate=cost(flops, 4 * size * len(gaps) * feats),
    )(ids_row, *rows, *pieces, *tokens)


def place_kernel(*refs):
    rows, store_ref = refs[:-1], refs[-1]
    me = lax.axis_index("dp")
    cap = rows[0].shape[0]
    for k, row in enumerate(rows):
        store_ref[pl.ds(pl.multiple_of((me ^ k) * cap, cap), cap), :] = row[...]


def place(rows):
    slots, feats = rows[0].shape[0] * len(rows), rows[0].shape[1]
    return pl.pallas_call(
        place_kernel,
        out_shape=jax.ShapeDtypeStruct((slots, feats), F32),
        compiler_params=params(16),
        cost_estimate=cost(0, 8 * slots * feats),
    )(*rows)


def swap(x, axis, gap):
    return lax.ppermute(x, axis, [(i, i ^ gap) for i in range(lax.axis_size(axis))])


def gather_pieces(piece):
    pieces, gaps = [piece], [0]
    bit = lax.axis_size("dp") // 2
    while bit > 1:
        pieces, gaps = pieces + [swap(p, "dp", bit) for p in pieces], gaps + [g ^ bit for g in gaps]
        bit //= 2
    return pieces, gaps


def local(
    activations, out_grads, proj_in, proj_out, doc_lengths, doc_owner, query_grads, query_ids
):
    tensor_size = lax.axis_size("tensor")
    data_size = lax.axis_size("dp")
    tokens = activations.shape[0]
    rank = proj_in.shape[1]
    width = rank // tensor_size
    docs = doc_owner.shape[0]
    cap = max(2, 2 * docs // data_size)
    direct = data_size <= MOST_DIRECT

    if direct:
        pieces, gaps = gather_pieces(query_grads)
        mate = swap(query_grads, "dp", 1)
        passed = [swap(piece, "dp", 1) for piece in pieces[1:]]
    else:
        pieces, gaps = [lax.all_gather(query_grads, "dp", axis=0, tiled=True)], [0]

    x, mask = project_x(
        activations, proj_in.T, doc_lengths, doc_owner.T, data_size, cap, direct
    )
    bit = tensor_size // 2
    x_got = swap(x, "tensor", bit)
    keep, send = project_g(out_grads, proj_out.T, width)
    early = [token(pieces[1:], EARLY_FLOPS)] if direct else []
    own, gots = [x], [x_got, swap(send, "tensor", bit)]
    while bit > 1:
        bit //= 2
        keep, own = fold(rank, keep, own, gots, early)
        gots = [swap(part, "tensor", bit) for part in own]
    blocks = outer(own, gots, keep, mask, data_size)
    if direct:
        far = [swap(blocks[k], "dp", k) for k in range(data_size - 1, 1, -1)]
        rows = [blocks[0], swap(after(blocks[1], mate), "dp", 1), *far[::-1]]
        late = [token(far, LATE_FLOPS)]
        pieces, gaps = [*pieces, mate, *passed], [*gaps, *(g ^ 1 for g in gaps)]
        store = place(rows)
    else:
        rows = [lax.all_to_all(jnp.stack(blocks), "dp", 0, 0, tiled=True).reshape(-1, width * rank)]
        store, late = rows[0], []
    scores = score(query_ids[None, :], rows, pieces, gaps, direct, late)
    bit = 1
    while bit < tensor_size:
        scores = scores + swap(scores, "tensor", bit)
        bit *= 2
    return store, scores * (1.0 / (rank * rank))


def solution(mesh):
    return jax.shard_map(
        local,
        mesh=mesh,
        in_specs=(
            P(("groups", "dp"), "tensor"),
            P(("groups", "dp"), "tensor"),
            P("tensor", None),
            P("tensor", None),
            P(("groups", "dp"), None),
            P(("groups", "dp"), None),
            P(("groups", "dp"), "tensor"),
            P("groups"),
        ),
        out_specs=(P(("groups", "dp"), "tensor"), P(("groups", "dp"), None)),
        check_vma=False,
    )
```

```python
import functools

import jax
import jax.numpy as jnp
from jax import lax
from jax.experimental import pallas as pl
from jax.experimental.pallas import tpu as pltpu
from jax.sharding import PartitionSpec as P

F32 = jnp.float32
BF16 = jnp.bfloat16
MIB = 1024 * 1024
NT = (((1,), (1,)), ((), ()))
MOST_DIRECT = 8
FIRST_FLOPS = 10 * 10**8
X_FLOPS = 6 * 10**8
MASK_FLOPS = 2 * 10**8
EARLY_FLOPS = 3 * 10**8
LATE_FLOPS = 2 * 10**8


def params(mib):
    return pltpu.CompilerParams(vmem_limit_bytes=mib * MIB)


def cost(flops, nbytes):
    return pl.CostEstimate(flops=flops, bytes_accessed=nbytes, transcendentals=0)


def halves(x):
    high = x.astype(BF16)
    return high, (x - high.astype(F32)).astype(BF16)


def mm(a, b, dims=(((1,), (0,)), ((), ()))):
    return lax.dot_general(a, b, dims, preferred_element_type=F32)


def slot_mask(owners, relative, cap, lengths, owner, slots, tokens):
    docs = lengths.shape[1]
    row = lax.broadcasted_iota(jnp.int32, (docs, docs), 0)
    col = lax.broadcasted_iota(jnp.int32, (docs, docs), 1)
    len_row = lengths.astype(F32)
    place_row = owner ^ lax.axis_index("dp") if relative else owner
    own_row = place_row.astype(F32)

    def column(values):
        return jnp.sum(jnp.where(row == col, values, 0.0), axis=1, keepdims=True)

    ends = jnp.sum(jnp.where(row <= col, column(len_row), 0.0), axis=0, keepdims=True)
    rank = jnp.sum(
        jnp.where((row < col) & (column(own_row) == own_row), 1.0, 0.0), axis=0, keepdims=True
    )
    slot = lax.broadcasted_iota(jnp.int32, (slots, docs), 0).astype(F32)
    hot = slot == own_row * cap + rank
    first = jnp.sum(jnp.where(hot, ends - len_row, 0.0), axis=1, keepdims=True)
    last = jnp.sum(jnp.where(hot, ends, 0.0), axis=1, keepdims=True)
    token = lax.broadcasted_iota(jnp.int32, (slots, tokens), 1).astype(F32)
    return jnp.where((token >= first) & (token < last), 1.0, 0.0)


def mask_kernel(owners, relative, cap, lengths_ref, owner_ref, mask_ref):
    mask_ref[...] = slot_mask(owners, relative, cap, lengths_ref[...], owner_ref[...], *mask_ref.shape)


def dispatch_mask(lengths, owner_row, owners, cap, tokens, relative):
    return pl.pallas_call(
        functools.partial(mask_kernel, owners, relative, cap),
        out_shape=jax.ShapeDtypeStruct((owners * cap, tokens), F32),
        compiler_params=params(8),
        cost_estimate=cost(MASK_FLOPS, 0),
    )(lengths, owner_row)


def x_kernel(act_ref, proj_ref, *refs):
    refs[-1][...] = mm(proj_ref[...], act_ref[...], NT)


def project_x(act, in_t, tokens):
    return pl.pallas_call(
        x_kernel,
        in_specs=[pl.BlockSpec(memory_space=pltpu.VMEM)] * 2
        + [pl.BlockSpec(memory_space=pl.ANY)] * len(tokens),
        out_shape=jax.ShapeDtypeStruct((in_t.shape[0], act.shape[0]), F32),
        compiler_params=params(8),
        cost_estimate=cost(X_FLOPS, 0),
    )(act, in_t, *tokens)


def g_kernel(width, grad_ref, proj_ref, keep_ref, send_ref, full):
    full[...] = mm(proj_ref[...], grad_ref[...], NT)
    me = lax.axis_index("tensor")
    count = full.shape[0] // width
    for apart in range(count):
        block = pl.ds(pl.multiple_of((me ^ apart) * width, width), width)
        ref, spot = (keep_ref, apart) if apart < count // 2 else (send_ref, apart - count // 2)
        ref[spot * width : (spot + 1) * width, :] = full[block, :]


def project_g(grad, out_t, width):
    tokens, rank = grad.shape[0], out_t.shape[0]
    part = jax.ShapeDtypeStruct((rank // 2, tokens), F32)
    return pl.pallas_call(
        functools.partial(g_kernel, width),
        out_shape=[part, part],
        scratch_shapes=[pltpu.VMEM((rank, tokens), F32)],
        compiler_params=params(24),
        cost_estimate=cost(0, 0),
    )(grad, out_t)


def stack(refs):
    return jnp.concatenate([r[...] for r in refs], axis=0)


def fold_kernel(rank, owned, came, keep_ref, *refs):
    first_ref, second_ref, kept_ref = refs[-3:]
    got = stack(refs[owned : owned + came])
    total = keep_ref[...] + got[rank:]
    kept = kept_ref.shape[0]
    kept_ref[...] = total[:kept]
    x = stack(refs[:owned])[:rank] + got[:rank]
    sent = jnp.concatenate([x, total[kept:]], axis=0)
    cut = first_ref.shape[0]
    first_ref[...] = sent[:cut]
    second_ref[...] = sent[cut:]


def fold(rank, keep, own, gots, pieces):
    tokens = keep.shape[1]
    kept = keep.shape[0] // 2
    cut = (rank + kept) // 16 * 8
    *sent, keep = pl.pallas_call(
        functools.partial(fold_kernel, rank, len(own), len(gots)),
        in_specs=[pl.BlockSpec(memory_space=pltpu.VMEM)] * (1 + len(own) + len(gots))
        + [pl.BlockSpec(memory_space=pl.ANY)] * len(pieces),
        out_shape=[
            jax.ShapeDtypeStruct((rows, tokens), F32) for rows in (cut, rank + kept - cut, kept)
        ],
        compiler_params=params(16),
        cost_estimate=cost(0, 0),
    )(keep, *own, *gots, *pieces)
    return keep, sent


def outer_kernel(owners, sent, g_ref, mask_ref, *refs):
    blocks = refs[-owners:]
    width = g_ref.shape[0]
    own, got = stack(refs[:sent]), stack(refs[sent : 2 * sent])
    rank = got.shape[0] - width
    x_full = own[:rank] + got[:rank]
    g_full = g_ref[...] + got[rank:]
    x_both = jnp.concatenate(halves(x_full), axis=0)
    g_high = g_full.astype(BF16).astype(F32)
    g_low = g_full - g_high
    mask = mask_ref[...]
    cap = blocks[0].shape[0]

    def product(i):
        pair = [(mask * g[i : i + 1, :]).astype(BF16) for g in (g_high, g_low)]
        both = mm(jnp.concatenate(pair, axis=0), x_both, NT)
        slots = mask.shape[0]
        return both[:slots, :rank] + both[:slots, rank:] + both[slots:, :rank]

    step = max(1, 128 // rank)
    for i in range(0, width, step):
        columns = jnp.concatenate([product(i + j) for j in range(step)], axis=1)
        for k, block in enumerate(blocks):
            block[:, i * rank : (i + step) * rank] = columns[k * cap : (k + 1) * cap, :]


def outer(sent, gots, g, mask, owners):
    slots, tokens = mask.shape
    width = g.shape[0]
    rank = sum(p.shape[0] for p in sent) - width
    cap = slots // owners
    return pl.pallas_call(
        functools.partial(outer_kernel, owners, len(sent)),
        out_shape=[jax.ShapeDtypeStruct((cap, width * rank), F32)] * owners,
        compiler_params=params(24),
        cost_estimate=cost(8 * slots * width * tokens * rank, 4 * slots * width * rank),
    )(g, mask, *sent, *gots)


def token_kernel(*refs):
    refs[-1][...] = jnp.zeros_like(refs[-1])


def token(arrays, flops):
    return pl.pallas_call(
        token_kernel,
        in_specs=[pl.BlockSpec(memory_space=pl.ANY)] * len(arrays),
        out_shape=jax.ShapeDtypeStruct((8, 128), F32),
        compiler_params=params(4),
        cost_estimate=cost(flops, 0),
    )(*arrays)


def after_kernel(block_ref, piece, out_ref):
    out_ref[...] = block_ref[...]


def after(block, piece):
    return pl.pallas_call(
        after_kernel,
        in_specs=[pl.BlockSpec(memory_space=pltpu.VMEM), pl.BlockSpec(memory_space=pl.ANY)],
        out_shape=jax.ShapeDtypeStruct(block.shape, F32),
        compiler_params=params(4),
        cost_estimate=cost(0, 0),
    )(block, piece)


def score_kernel(count, gaps, relative, ids_ref, *refs):
    rows, pieces, scores_ref = refs[:count], refs[count : count + len(gaps)], refs[-1]
    queries = ids_ref.shape[1]
    me = lax.axis_index("dp")
    cap = rows[0].shape[0]
    high, low = halves(stack(rows))
    slots = high.shape[0]
    both = jnp.concatenate([high, low], axis=0)
    held = pieces[0].shape[0]
    pool = stack(pieces)
    products = mm(both, jnp.concatenate(halves(pool), axis=0), NT)
    split = pool.shape[0]
    part = products[:slots, :split] + products[:slots, split:] + products[slots:, :split]
    row = lax.broadcasted_iota(jnp.int32, (held, queries), 0)
    places = [row + ((me ^ gap) * held if len(gaps) > 1 else 0) for gap in gaps]
    hot = (jnp.concatenate(places, axis=0) == ids_ref[...]).astype(F32).astype(BF16)
    top, rest = halves(part)
    last = (part - top.astype(F32) - rest.astype(F32)).astype(BF16)
    picked = mm(jnp.concatenate([top, rest, last], axis=0), hot)
    total = picked[:slots] + picked[slots : 2 * slots] + picked[2 * slots :]
    for k in range(count):
        spot = pl.ds(pl.multiple_of((me ^ k) * cap, cap), cap) if relative else pl.ds(k * cap, cap)
        scores_ref[spot, :] = total[k * cap : (k + 1) * cap, :]


def score(ids_row, rows, pieces, gaps, relative, tokens):
    slots = rows[0].shape[0] * len(rows)
    queries = ids_row.shape[1]
    size, feats = pieces[0].shape
    flops = 6 * slots * size * len(gaps) * feats
    return pl.pallas_call(
        functools.partial(score_kernel, len(rows), gaps, relative),
        in_specs=[pl.BlockSpec(memory_space=pltpu.VMEM)] * (1 + len(rows) + len(pieces))
        + [pl.BlockSpec(memory_space=pl.ANY)] * len(tokens),
        out_shape=jax.ShapeDtypeStruct((slots, queries), F32),
        compiler_params=params(24),
        cost_estimate=cost(flops, 4 * size * len(gaps) * feats),
    )(ids_row, *rows, *pieces, *tokens)


def place_kernel(*refs):
    rows, store_ref = refs[:-1], refs[-1]
    me = lax.axis_index("dp")
    cap = rows[0].shape[0]
    for k, row in enumerate(rows):
        store_ref[pl.ds(pl.multiple_of((me ^ k) * cap, cap), cap), :] = row[...]


def place(rows):
    slots, feats = rows[0].shape[0] * len(rows), rows[0].shape[1]
    return pl.pallas_call(
        place_kernel,
        out_shape=jax.ShapeDtypeStruct((slots, feats), F32),
        compiler_params=params(16),
        cost_estimate=cost(0, 8 * slots * feats),
    )(*rows)


def swap(x, axis, gap):
    return lax.ppermute(x, axis, [(i, i ^ gap) for i in range(lax.axis_size(axis))])


def gather_pieces(piece):
    pieces, gaps = [piece], [0]
    bit = lax.axis_size("dp") // 2
    while bit > 1:
        pieces, gaps = pieces + [swap(p, "dp", bit) for p in pieces], gaps + [g ^ bit for g in gaps]
        bit //= 2
    return pieces, gaps


def local(
    activations, out_grads, proj_in, proj_out, doc_lengths, doc_owner, query_grads, query_ids
):
    tensor_size = lax.axis_size("tensor")
    data_size = lax.axis_size("dp")
    tokens = activations.shape[0]
    rank = proj_in.shape[1]
    width = rank // tensor_size
    docs = doc_owner.shape[0]
    cap = max(2, 2 * docs // data_size)
    direct = data_size <= MOST_DIRECT

    if direct:
        pieces, gaps = gather_pieces(query_grads)
        mate = swap(query_grads, "dp", 1)
        passed = [swap(piece, "dp", 1) for piece in pieces[1:]]
    else:
        pieces, gaps = [lax.all_gather(query_grads, "dp", axis=0, tiled=True)], [0]

    mask = dispatch_mask(doc_lengths, doc_owner.T, data_size, cap, activations.shape[0], direct)
    x = project_x(activations, proj_in.T, [token([], FIRST_FLOPS)])
    bit = tensor_size // 2
    x_got = swap(x, "tensor", bit)
    keep, send = project_g(out_grads, proj_out.T, width)
    early = [mask] + ([token(pieces[1:], EARLY_FLOPS)] if direct else [])
    own, gots = [x], [x_got, swap(send, "tensor", bit)]
    while bit > 1:
        bit //= 2
        keep, own = fold(rank, keep, own, gots, early)
        gots = [swap(part, "tensor", bit) for part in own]
    blocks = outer(own, gots, keep, mask, data_size)
    if direct:
        far = [swap(blocks[k], "dp", k) for k in range(data_size - 1, 1, -1)]
        rows = [blocks[0], swap(after(blocks[1], mate), "dp", 1), *far[::-1]]
        late = [token(far, LATE_FLOPS)]
        pieces, gaps = [*pieces, mate, *passed], [*gaps, *(g ^ 1 for g in gaps)]
        store = place(rows)
    else:
        rows = [lax.all_to_all(jnp.stack(blocks), "dp", 0, 0, tiled=True).reshape(-1, width * rank)]
        store, late = rows[0], []
    scores = score(query_ids[None, :], rows, pieces, gaps, direct, late)
    bit = 1
    while bit < tensor_size:
        scores = scores + swap(scores, "tensor", bit)
        bit *= 2
    return store, scores * (1.0 / (rank * rank))


def solution(mesh):
    return jax.shard_map(
        local,
        mesh=mesh,
        in_specs=(
            P(("groups", "dp"), "tensor"),
            P(("groups", "dp"), "tensor"),
            P("tensor", None),
            P("tensor", None),
            P(("groups", "dp"), None),
            P(("groups", "dp"), None),
            P(("groups", "dp"), "tensor"),
            P("groups"),
        ),
        out_specs=(P(("groups", "dp"), "tensor"), P(("groups", "dp"), None)),
        check_vma=False,
    )
```

```python
import functools

import jax
import jax.numpy as jnp
from jax import lax
from jax.experimental import pallas as pl
from jax.experimental.pallas import tpu as pltpu
from jax.sharding import PartitionSpec as P

F32 = jnp.float32
BF16 = jnp.bfloat16
MIB = 1024 * 1024
NT = (((1,), (1,)), ((), ()))
MOST_DIRECT = 8
FIRST_FLOPS = 10 * 10**8
X_FLOPS = 6 * 10**8
MASK_FLOPS = 2 * 10**8
EARLY_FLOPS = 3 * 10**8
LATE_FLOPS = 2 * 10**8


def params(mib):
    return pltpu.CompilerParams(vmem_limit_bytes=mib * MIB)


def cost(flops, nbytes):
    return pl.CostEstimate(flops=flops, bytes_accessed=nbytes, transcendentals=0)


def halves(x):
    high = x.astype(BF16)
    return high, (x - high.astype(F32)).astype(BF16)


def mm(a, b, dims=(((1,), (0,)), ((), ()))):
    return lax.dot_general(a, b, dims, preferred_element_type=F32)


def slot_mask(owners, relative, cap, lengths, owner, slots, tokens):
    docs = lengths.shape[1]
    row = lax.broadcasted_iota(jnp.int32, (docs, docs), 0)
    col = lax.broadcasted_iota(jnp.int32, (docs, docs), 1)
    len_row = lengths.astype(F32)
    place_row = owner ^ lax.axis_index("dp") if relative else owner
    own_row = place_row.astype(F32)

    def column(values):
        return jnp.sum(jnp.where(row == col, values, 0.0), axis=1, keepdims=True)

    ends = jnp.sum(jnp.where(row <= col, column(len_row), 0.0), axis=0, keepdims=True)
    rank = jnp.sum(
        jnp.where((row < col) & (column(own_row) == own_row), 1.0, 0.0), axis=0, keepdims=True
    )
    slot = lax.broadcasted_iota(jnp.int32, (slots, docs), 0).astype(F32)
    hot = slot == own_row * cap + rank
    first = jnp.sum(jnp.where(hot, ends - len_row, 0.0), axis=1, keepdims=True)
    last = jnp.sum(jnp.where(hot, ends, 0.0), axis=1, keepdims=True)
    token = lax.broadcasted_iota(jnp.int32, (slots, tokens), 1).astype(F32)
    return jnp.where((token >= first) & (token < last), 1.0, 0.0)


def mask_kernel(owners, relative, cap, lengths_ref, owner_ref, mask_ref):
    mask_ref[...] = slot_mask(owners, relative, cap, lengths_ref[...], owner_ref[...], *mask_ref.shape)


def dispatch_mask(lengths, owner_row, owners, cap, tokens, relative):
    return pl.pallas_call(
        functools.partial(mask_kernel, owners, relative, cap),
        out_shape=jax.ShapeDtypeStruct((owners * cap, tokens), F32),
        compiler_params=params(8),
        cost_estimate=cost(MASK_FLOPS, 0),
    )(lengths, owner_row)


def x_kernel(act_ref, proj_ref, *refs):
    refs[-1][...] = mm(proj_ref[...], act_ref[...], NT)


def project_x(act, in_t, tokens):
    return pl.pallas_call(
        x_kernel,
        in_specs=[pl.BlockSpec(memory_space=pltpu.VMEM)] * 2
        + [pl.BlockSpec(memory_space=pl.ANY)] * len(tokens),
        out_shape=jax.ShapeDtypeStruct((in_t.shape[0], act.shape[0]), F32),
        compiler_params=params(8),
        cost_estimate=cost(X_FLOPS, 0),
    )(act, in_t, *tokens)


def g_kernel(width, grad_ref, proj_ref, keep_ref, send_ref, full):
    full[...] = mm(proj_ref[...], grad_ref[...], NT)
    me = lax.axis_index("tensor")
    count = full.shape[0] // width
    for apart in range(count):
        block = pl.ds(pl.multiple_of((me ^ apart) * width, width), width)
        ref, spot = (keep_ref, apart) if apart < count // 2 else (send_ref, apart - count // 2)
        ref[spot * width : (spot + 1) * width, :] = full[block, :]


def project_g(grad, out_t, width):
    tokens, rank = grad.shape[0], out_t.shape[0]
    part = jax.ShapeDtypeStruct((rank // 2, tokens), F32)
    return pl.pallas_call(
        functools.partial(g_kernel, width),
        out_shape=[part, part],
        scratch_shapes=[pltpu.VMEM((rank, tokens), F32)],
        compiler_params=params(24),
        cost_estimate=cost(0, 0),
    )(grad, out_t)


def stack(refs):
    return jnp.concatenate([r[...] for r in refs], axis=0)


def fold_kernel(rank, owned, came, keep_ref, *refs):
    first_ref, second_ref, kept_ref = refs[-3:]
    got = stack(refs[owned : owned + came])
    total = keep_ref[...] + got[rank:]
    kept = kept_ref.shape[0]
    kept_ref[...] = total[:kept]
    x = stack(refs[:owned])[:rank] + got[:rank]
    sent = jnp.concatenate([x, total[kept:]], axis=0)
    cut = first_ref.shape[0]
    first_ref[...] = sent[:cut]
    second_ref[...] = sent[cut:]


def fold(rank, keep, own, gots, pieces):
    tokens = keep.shape[1]
    kept = keep.shape[0] // 2
    cut = (rank + kept) // 16 * 8
    *sent, keep = pl.pallas_call(
        functools.partial(fold_kernel, rank, len(own), len(gots)),
        in_specs=[pl.BlockSpec(memory_space=pltpu.VMEM)] * (1 + len(own) + len(gots))
        + [pl.BlockSpec(memory_space=pl.ANY)] * len(pieces),
        out_shape=[
            jax.ShapeDtypeStruct((rows, tokens), F32) for rows in (cut, rank + kept - cut, kept)
        ],
        compiler_params=params(16),
        cost_estimate=cost(0, 0),
    )(keep, *own, *gots, *pieces)
    return keep, sent


def outer_kernel(first, owners, sent, g_ref, mask_ref, *refs):
    blocks = refs[-owners:]
    width = g_ref.shape[0]
    own, got = stack(refs[:sent]), stack(refs[sent : 2 * sent])
    rank = got.shape[0] - width
    x_full = own[:rank] + got[:rank]
    g_full = g_ref[...] + got[rank:]
    x_both = jnp.concatenate(halves(x_full), axis=0)
    g_high = g_full.astype(BF16).astype(F32)
    g_low = g_full - g_high
    cap = blocks[0].shape[0]
    slots = owners * cap
    mask = mask_ref[first * cap : first * cap + slots, :]

    def product(i):
        pair = [(mask * g[i : i + 1, :]).astype(BF16) for g in (g_high, g_low)]
        both = mm(jnp.concatenate(pair, axis=0), x_both, NT)
        return both[:slots, :rank] + both[:slots, rank:] + both[slots:, :rank]

    step = max(1, 128 // rank)
    for i in range(0, width, step):
        columns = jnp.concatenate([product(i + j) for j in range(step)], axis=1)
        for k, block in enumerate(blocks):
            block[:, i * rank : (i + step) * rank] = columns[k * cap : (k + 1) * cap, :]


def outer(sent, gots, g, mask, cap, first, owners):
    width = g.shape[0]
    rank = sum(p.shape[0] for p in sent) - width
    return pl.pallas_call(
        functools.partial(outer_kernel, first, owners, len(sent)),
        out_shape=[jax.ShapeDtypeStruct((cap, width * rank), F32)] * owners,
        compiler_params=params(24),
        cost_estimate=cost(8 * owners * cap * width * mask.shape[1] * rank, 0),
    )(g, mask, *sent, *gots)


def token_kernel(*refs):
    refs[-1][...] = jnp.zeros_like(refs[-1])


def token(arrays, flops):
    return pl.pallas_call(
        token_kernel,
        in_specs=[pl.BlockSpec(memory_space=pl.ANY)] * len(arrays),
        out_shape=jax.ShapeDtypeStruct((8, 128), F32),
        compiler_params=params(4),
        cost_estimate=cost(flops, 0),
    )(*arrays)


def after_kernel(block_ref, piece, out_ref):
    out_ref[...] = block_ref[...]


def after(block, piece):
    return pl.pallas_call(
        after_kernel,
        in_specs=[pl.BlockSpec(memory_space=pltpu.VMEM), pl.BlockSpec(memory_space=pl.ANY)],
        out_shape=jax.ShapeDtypeStruct(block.shape, F32),
        compiler_params=params(4),
        cost_estimate=cost(0, 0),
    )(block, piece)


def score_kernel(count, gaps, relative, ids_ref, *refs):
    rows, pieces, scores_ref = refs[:count], refs[count : count + len(gaps)], refs[-1]
    queries = ids_ref.shape[1]
    me = lax.axis_index("dp")
    cap = rows[0].shape[0]
    high, low = halves(stack(rows))
    slots = high.shape[0]
    both = jnp.concatenate([high, low], axis=0)
    held = pieces[0].shape[0]
    pool = stack(pieces)
    products = mm(both, jnp.concatenate(halves(pool), axis=0), NT)
    split = pool.shape[0]
    part = products[:slots, :split] + products[:slots, split:] + products[slots:, :split]
    row = lax.broadcasted_iota(jnp.int32, (held, queries), 0)
    places = [row + ((me ^ gap) * held if len(gaps) > 1 else 0) for gap in gaps]
    hot = (jnp.concatenate(places, axis=0) == ids_ref[...]).astype(F32).astype(BF16)
    top, rest = halves(part)
    last = (part - top.astype(F32) - rest.astype(F32)).astype(BF16)
    picked = mm(jnp.concatenate([top, rest, last], axis=0), hot)
    total = picked[:slots] + picked[slots : 2 * slots] + picked[2 * slots :]
    for k in range(count):
        spot = pl.ds(pl.multiple_of((me ^ k) * cap, cap), cap) if relative else pl.ds(k * cap, cap)
        scores_ref[spot, :] = total[k * cap : (k + 1) * cap, :]


def score(ids_row, rows, pieces, gaps, relative, tokens):
    slots = rows[0].shape[0] * len(rows)
    queries = ids_row.shape[1]
    size, feats = pieces[0].shape
    flops = 6 * slots * size * len(gaps) * feats
    return pl.pallas_call(
        functools.partial(score_kernel, len(rows), gaps, relative),
        in_specs=[pl.BlockSpec(memory_space=pltpu.VMEM)] * (1 + len(rows) + len(pieces))
        + [pl.BlockSpec(memory_space=pl.ANY)] * len(tokens),
        out_shape=jax.ShapeDtypeStruct((slots, queries), F32),
        compiler_params=params(24),
        cost_estimate=cost(flops, 4 * size * len(gaps) * feats),
    )(ids_row, *rows, *pieces, *tokens)


def place_kernel(*refs):
    rows, store_ref = refs[:-1], refs[-1]
    me = lax.axis_index("dp")
    cap = rows[0].shape[0]
    for k, row in enumerate(rows):
        store_ref[pl.ds(pl.multiple_of((me ^ k) * cap, cap), cap), :] = row[...]


def place(rows):
    slots, feats = rows[0].shape[0] * len(rows), rows[0].shape[1]
    return pl.pallas_call(
        place_kernel,
        out_shape=jax.ShapeDtypeStruct((slots, feats), F32),
        compiler_params=params(16),
        cost_estimate=cost(0, 8 * slots * feats),
    )(*rows)


def swap(x, axis, gap):
    return lax.ppermute(x, axis, [(i, i ^ gap) for i in range(lax.axis_size(axis))])


def gather_pieces(piece):
    pieces, gaps = [piece], [0]
    bit = lax.axis_size("dp") // 2
    while bit > 1:
        pieces, gaps = pieces + [swap(p, "dp", bit) for p in pieces], gaps + [g ^ bit for g in gaps]
        bit //= 2
    return pieces, gaps


def local(
    activations, out_grads, proj_in, proj_out, doc_lengths, doc_owner, query_grads, query_ids
):
    tensor_size = lax.axis_size("tensor")
    data_size = lax.axis_size("dp")
    tokens = activations.shape[0]
    rank = proj_in.shape[1]
    width = rank // tensor_size
    docs = doc_owner.shape[0]
    cap = max(2, 2 * docs // data_size)
    direct = data_size <= MOST_DIRECT

    if direct:
        pieces, gaps = gather_pieces(query_grads)
        mate = swap(query_grads, "dp", 1)
        passed = [swap(piece, "dp", 1) for piece in pieces[1:]]
    else:
        pieces, gaps = [lax.all_gather(query_grads, "dp", axis=0, tiled=True)], [0]

    mask = dispatch_mask(doc_lengths, doc_owner.T, data_size, cap, activations.shape[0], direct)
    x = project_x(activations, proj_in.T, [token([], FIRST_FLOPS)])
    bit = tensor_size // 2
    x_got = swap(x, "tensor", bit)
    keep, send = project_g(out_grads, proj_out.T, width)
    early = [mask] + ([token(pieces[1:], EARLY_FLOPS)] if direct else [])
    own, gots = [x], [x_got, swap(send, "tensor", bit)]
    while bit > 1:
        bit //= 2
        keep, own = fold(rank, keep, own, gots, early)
        gots = [swap(part, "tensor", bit) for part in own]
    if direct:
        split = max(1, data_size // 2)
        blocks = outer(own, gots, keep, mask, cap, split, data_size - split)
        far = [swap(blocks[k - split], "dp", k) for k in range(data_size - 1, split - 1, -1)]
        blocks = outer(own, gots, keep, mask, cap, 0, split)
        rows = [swap(after(blocks[k], mate), "dp", k) for k in range(1, split)]
        rows = [blocks[0], *rows, *far[::-1]]
        late = [token(far, LATE_FLOPS)]
        pieces, gaps = [*pieces, mate, *passed], [*gaps, *(g ^ 1 for g in gaps)]
        store = place(rows)
    else:
        blocks = outer(own, gots, keep, mask, cap, 0, data_size)
        rows = [lax.all_to_all(jnp.stack(blocks), "dp", 0, 0, tiled=True).reshape(-1, width * rank)]
        store, late = rows[0], []
    scores = score(query_ids[None, :], rows, pieces, gaps, direct, late)
    bit = 1
    while bit < tensor_size:
        scores = scores + swap(scores, "tensor", bit)
        bit *= 2
    return store, scores * (1.0 / (rank * rank))


def solution(mesh):
    return jax.shard_map(
        local,
        mesh=mesh,
        in_specs=(
            P(("groups", "dp"), "tensor"),
            P(("groups", "dp"), "tensor"),
            P("tensor", None),
            P("tensor", None),
            P(("groups", "dp"), None),
            P(("groups", "dp"), None),
            P(("groups", "dp"), "tensor"),
            P("groups"),
        ),
        out_specs=(P(("groups", "dp"), "tensor"), P(("groups", "dp"), None)),
        check_vma=False,
    )
```

```python
import functools

import jax
import jax.numpy as jnp
from jax import lax
from jax.experimental import pallas as pl
from jax.experimental.pallas import tpu as pltpu
from jax.sharding import PartitionSpec as P

F32 = jnp.float32
BF16 = jnp.bfloat16
MIB = 1024 * 1024
NT = (((1,), (1,)), ((), ()))
MOST_DIRECT = 8
GROUP = 4
FIRST_FLOPS = 10 * 10**8
X_FLOPS = 6 * 10**8
MASK_FLOPS = 2 * 10**8
EARLY_FLOPS = 3 * 10**8
LATE_FLOPS = 2 * 10**8


def params(mib):
    return pltpu.CompilerParams(vmem_limit_bytes=mib * MIB)


def cost(flops, nbytes):
    return pl.CostEstimate(flops=flops, bytes_accessed=nbytes, transcendentals=0)


def halves(x):
    high = x.astype(BF16)
    return high, (x - high.astype(F32)).astype(BF16)


def mm(a, b, dims=(((1,), (0,)), ((), ()))):
    return lax.dot_general(a, b, dims, preferred_element_type=F32)


def slot_mask(owners, relative, cap, lengths, owner, slots, tokens):
    docs = lengths.shape[1]
    row = lax.broadcasted_iota(jnp.int32, (docs, docs), 0)
    col = lax.broadcasted_iota(jnp.int32, (docs, docs), 1)
    len_row = lengths.astype(F32)
    place_row = owner ^ lax.axis_index("dp") if relative else owner
    own_row = place_row.astype(F32)

    def column(values):
        return jnp.sum(jnp.where(row == col, values, 0.0), axis=1, keepdims=True)

    ends = jnp.sum(jnp.where(row <= col, column(len_row), 0.0), axis=0, keepdims=True)
    rank = jnp.sum(
        jnp.where((row < col) & (column(own_row) == own_row), 1.0, 0.0), axis=0, keepdims=True
    )
    slot = lax.broadcasted_iota(jnp.int32, (slots, docs), 0).astype(F32)
    hot = slot == own_row * cap + rank
    first = jnp.sum(jnp.where(hot, ends - len_row, 0.0), axis=1, keepdims=True)
    last = jnp.sum(jnp.where(hot, ends, 0.0), axis=1, keepdims=True)
    token = lax.broadcasted_iota(jnp.int32, (slots, tokens), 1).astype(F32)
    return jnp.where((token >= first) & (token < last), 1.0, 0.0)


def mask_kernel(owners, relative, cap, lengths_ref, owner_ref, mask_ref):
    mask_ref[...] = slot_mask(owners, relative, cap, lengths_ref[...], owner_ref[...], *mask_ref.shape)


def dispatch_mask(lengths, owner_row, owners, cap, tokens, relative):
    return pl.pallas_call(
        functools.partial(mask_kernel, owners, relative, cap),
        out_shape=jax.ShapeDtypeStruct((owners * cap, tokens), F32),
        compiler_params=params(8),
        cost_estimate=cost(MASK_FLOPS, 0),
    )(lengths, owner_row)


def put_projection(out_ref, proj_ref, act_ref):
    half = act_ref.shape[0] // 2
    out_ref[:, :half] = mm(proj_ref[...], act_ref[:half, :], NT)
    out_ref[:, half:] = mm(act_ref[half:, :], proj_ref[...], NT).T


def x_kernel(act_ref, proj_ref, *refs):
    put_projection(refs[-1], proj_ref, act_ref)


def project_x(act, in_t, tokens):
    return pl.pallas_call(
        x_kernel,
        in_specs=[pl.BlockSpec(memory_space=pltpu.VMEM)] * 2
        + [pl.BlockSpec(memory_space=pl.ANY)] * len(tokens),
        out_shape=jax.ShapeDtypeStruct((in_t.shape[0], act.shape[0]), F32),
        compiler_params=params(8),
        cost_estimate=cost(X_FLOPS, 0),
    )(act, in_t, *tokens)


def g_kernel(width, grad_ref, proj_ref, keep_ref, send_ref, full):
    put_projection(full, proj_ref, grad_ref)
    me = lax.axis_index("tensor")
    count = full.shape[0] // width
    for apart in range(count):
        block = pl.ds(pl.multiple_of((me ^ apart) * width, width), width)
        ref, spot = (keep_ref, apart) if apart < count // 2 else (send_ref, apart - count // 2)
        ref[spot * width : (spot + 1) * width, :] = full[block, :]


def project_g(grad, out_t, width):
    tokens, rank = grad.shape[0], out_t.shape[0]
    part = jax.ShapeDtypeStruct((rank // 2, tokens), F32)
    return pl.pallas_call(
        functools.partial(g_kernel, width),
        out_shape=[part, part],
        scratch_shapes=[pltpu.VMEM((rank, tokens), F32)],
        compiler_params=params(24),
        cost_estimate=cost(0, 0),
    )(grad, out_t)


def stack(refs):
    return jnp.concatenate([r[...] for r in refs], axis=0)


def fold_kernel(rank, owned, came, keep_ref, *refs):
    first_ref, second_ref, kept_ref = refs[-3:]
    got = stack(refs[owned : owned + came])
    total = keep_ref[...] + got[rank:]
    kept = kept_ref.shape[0]
    kept_ref[...] = total[:kept]
    x = stack(refs[:owned])[:rank] + got[:rank]
    sent = jnp.concatenate([x, total[kept:]], axis=0)
    cut = first_ref.shape[0]
    first_ref[...] = sent[:cut]
    second_ref[...] = sent[cut:]


def fold(rank, keep, own, gots, pieces):
    tokens = keep.shape[1]
    kept = keep.shape[0] // 2
    cut = (rank + kept) // 16 * 8
    *sent, keep = pl.pallas_call(
        functools.partial(fold_kernel, rank, len(own), len(gots)),
        in_specs=[pl.BlockSpec(memory_space=pltpu.VMEM)] * (1 + len(own) + len(gots))
        + [pl.BlockSpec(memory_space=pl.ANY)] * len(pieces),
        out_shape=[
            jax.ShapeDtypeStruct((rows, tokens), F32) for rows in (cut, rank + kept - cut, kept)
        ],
        compiler_params=params(16),
        cost_estimate=cost(0, 0),
    )(keep, *own, *gots, *pieces)
    return keep, sent


def outer_kernel(owners, sent, g_ref, mask_ref, *refs):
    blocks = refs[-owners:]
    width = g_ref.shape[0]
    own, got = stack(refs[:sent]), stack(refs[sent : 2 * sent])
    rank = got.shape[0] - width
    x_full = own[:rank] + got[:rank]
    g_full = g_ref[...] + got[rank:]
    x_both = jnp.concatenate(halves(x_full), axis=0)
    g_high = g_full.astype(BF16).astype(F32)
    g_low = g_full - g_high
    mask = mask_ref[...]
    cap = blocks[0].shape[0]

    slots = mask.shape[0]
    group = min(width, GROUP)
    for i in range(0, width, group):
        rows = [mask * g[j : j + 1, :] for j in range(i, i + group) for g in (g_high, g_low)]
        both = mm(jnp.concatenate([r.astype(BF16) for r in rows], axis=0), x_both, NT)
        columns = []
        for j in range(group):
            high = both[2 * j * slots : (2 * j + 1) * slots]
            low = both[(2 * j + 1) * slots : (2 * j + 2) * slots]
            columns.append(high[:, :rank] + high[:, rank:] + low[:, :rank])
        out = jnp.concatenate(columns, axis=1)
        for k, block in enumerate(blocks):
            block[:, i * rank : (i + group) * rank] = out[k * cap : (k + 1) * cap, :]


def outer(sent, gots, g, mask, owners):
    slots, tokens = mask.shape
    width = g.shape[0]
    rank = sum(p.shape[0] for p in sent) - width
    cap = slots // owners
    return pl.pallas_call(
        functools.partial(outer_kernel, owners, len(sent)),
        out_shape=[jax.ShapeDtypeStruct((cap, width * rank), F32)] * owners,
        compiler_params=params(24),
        cost_estimate=cost(8 * slots * width * tokens * rank, 4 * slots * width * rank),
    )(g, mask, *sent, *gots)


def token_kernel(*refs):
    refs[-1][...] = jnp.zeros_like(refs[-1])


def token(arrays, flops):
    return pl.pallas_call(
        token_kernel,
        in_specs=[pl.BlockSpec(memory_space=pl.ANY)] * len(arrays),
        out_shape=jax.ShapeDtypeStruct((8, 128), F32),
        compiler_params=params(4),
        cost_estimate=cost(flops, 0),
    )(*arrays)


def after_kernel(block_ref, piece, out_ref):
    out_ref[...] = block_ref[...]


def after(block, piece):
    return pl.pallas_call(
        after_kernel,
        in_specs=[pl.BlockSpec(memory_space=pltpu.VMEM), pl.BlockSpec(memory_space=pl.ANY)],
        out_shape=jax.ShapeDtypeStruct(block.shape, F32),
        compiler_params=params(4),
        cost_estimate=cost(0, 0),
    )(block, piece)


def score_kernel(count, gaps, relative, ids_ref, *refs):
    rows, pieces, scores_ref = refs[:count], refs[count : count + len(gaps)], refs[-1]
    queries = ids_ref.shape[1]
    me = lax.axis_index("dp")
    cap = rows[0].shape[0]
    high, low = halves(stack(rows))
    slots = high.shape[0]
    both = jnp.concatenate([high, low], axis=0)
    held = pieces[0].shape[0]
    pool = stack(pieces)
    products = mm(both, jnp.concatenate(halves(pool), axis=0), NT)
    split = pool.shape[0]
    part = products[:slots, :split] + products[:slots, split:] + products[slots:, :split]
    row = lax.broadcasted_iota(jnp.int32, (held, queries), 0)
    places = [row + ((me ^ gap) * held if len(gaps) > 1 else 0) for gap in gaps]
    hot = (jnp.concatenate(places, axis=0) == ids_ref[...]).astype(F32).astype(BF16)
    top, rest = halves(part)
    last = (part - top.astype(F32) - rest.astype(F32)).astype(BF16)
    picked = mm(jnp.concatenate([top, rest, last], axis=0), hot)
    total = picked[:slots] + picked[slots : 2 * slots] + picked[2 * slots :]
    for k in range(count):
        spot = pl.ds(pl.multiple_of((me ^ k) * cap, cap), cap) if relative else pl.ds(k * cap, cap)
        scores_ref[spot, :] = total[k * cap : (k + 1) * cap, :]


def score(ids_row, rows, pieces, gaps, relative, tokens):
    slots = rows[0].shape[0] * len(rows)
    queries = ids_row.shape[1]
    size, feats = pieces[0].shape
    flops = 6 * slots * size * len(gaps) * feats
    return pl.pallas_call(
        functools.partial(score_kernel, len(rows), gaps, relative),
        in_specs=[pl.BlockSpec(memory_space=pltpu.VMEM)] * (1 + len(rows) + len(pieces))
        + [pl.BlockSpec(memory_space=pl.ANY)] * len(tokens),
        out_shape=jax.ShapeDtypeStruct((slots, queries), F32),
        compiler_params=params(24),
        cost_estimate=cost(flops, 4 * size * len(gaps) * feats),
    )(ids_row, *rows, *pieces, *tokens)


def place_kernel(*refs):
    rows, store_ref = refs[:-1], refs[-1]
    me = lax.axis_index("dp")
    cap = rows[0].shape[0]
    for k, row in enumerate(rows):
        store_ref[pl.ds(pl.multiple_of((me ^ k) * cap, cap), cap), :] = row[...]


def place(rows):
    slots, feats = rows[0].shape[0] * len(rows), rows[0].shape[1]
    return pl.pallas_call(
        place_kernel,
        out_shape=jax.ShapeDtypeStruct((slots, feats), F32),
        compiler_params=params(16),
        cost_estimate=cost(0, 8 * slots * feats),
    )(*rows)


def swap(x, axis, gap):
    return lax.ppermute(x, axis, [(i, i ^ gap) for i in range(lax.axis_size(axis))])


def gather_pieces(piece):
    pieces, gaps = [piece], [0]
    bit = lax.axis_size("dp") // 2
    while bit > 1:
        pieces, gaps = pieces + [swap(p, "dp", bit) for p in pieces], gaps + [g ^ bit for g in gaps]
        bit //= 2
    return pieces, gaps


def local(
    activations, out_grads, proj_in, proj_out, doc_lengths, doc_owner, query_grads, query_ids
):
    tensor_size = lax.axis_size("tensor")
    data_size = lax.axis_size("dp")
    tokens = activations.shape[0]
    rank = proj_in.shape[1]
    width = rank // tensor_size
    docs = doc_owner.shape[0]
    cap = max(2, 2 * docs // data_size)
    direct = data_size <= MOST_DIRECT

    if direct:
        pieces, gaps = gather_pieces(query_grads)
        mate = swap(query_grads, "dp", 1)
        passed = [swap(piece, "dp", 1) for piece in pieces[1:]]
    else:
        pieces, gaps = [lax.all_gather(query_grads, "dp", axis=0, tiled=True)], [0]

    mask = dispatch_mask(doc_lengths, doc_owner.T, data_size, cap, activations.shape[0], direct)
    x = project_x(activations, proj_in.T, [token([], FIRST_FLOPS)])
    bit = tensor_size // 2
    x_got = swap(x, "tensor", bit)
    keep, send = project_g(out_grads, proj_out.T, width)
    early = [mask] + ([token(pieces[1:], EARLY_FLOPS)] if direct else [])
    own, gots = [x], [x_got, swap(send, "tensor", bit)]
    while bit > 1:
        bit //= 2
        keep, own = fold(rank, keep, own, gots, early)
        gots = [swap(part, "tensor", bit) for part in own]
    blocks = outer(own, gots, keep, mask, data_size)
    if direct:
        far = [swap(blocks[k], "dp", k) for k in range(data_size - 1, 1, -1)]
        rows = [blocks[0], swap(after(blocks[1], mate), "dp", 1), *far[::-1]]
        late = [token(far, LATE_FLOPS)]
        pieces, gaps = [*pieces, mate, *passed], [*gaps, *(g ^ 1 for g in gaps)]
        store = place(rows)
    else:
        rows = [lax.all_to_all(jnp.stack(blocks), "dp", 0, 0, tiled=True).reshape(-1, width * rank)]
        store, late = rows[0], []
    scores = score(query_ids[None, :], rows, pieces, gaps, direct, late)
    bit = 1
    while bit < tensor_size:
        scores = scores + swap(scores, "tensor", bit)
        bit *= 2
    return store, scores * (1.0 / (rank * rank))


def solution(mesh):
    return jax.shard_map(
        local,
        mesh=mesh,
        in_specs=(
            P(("groups", "dp"), "tensor"),
            P(("groups", "dp"), "tensor"),
            P("tensor", None),
            P("tensor", None),
            P(("groups", "dp"), None),
            P(("groups", "dp"), None),
            P(("groups", "dp"), "tensor"),
            P("groups"),
        ),
        out_specs=(P(("groups", "dp"), "tensor"), P(("groups", "dp"), None)),
        check_vma=False,
    )
```

```python
import functools

import jax
import jax.numpy as jnp
from jax import lax
from jax.experimental import pallas as pl
from jax.experimental.pallas import tpu as pltpu
from jax.sharding import PartitionSpec as P

F32 = jnp.float32
BF16 = jnp.bfloat16
MIB = 1024 * 1024
NT = (((1,), (1,)), ((), ()))
MOST_DIRECT = 8
GROUP = 4
FIRST_FLOPS = 10 * 10**8
X_FLOPS = 6 * 10**8
MASK_FLOPS = 2 * 10**8
EARLY_FLOPS = 3 * 10**8
LATE_FLOPS = 10**8


def params(mib):
    return pltpu.CompilerParams(vmem_limit_bytes=mib * MIB)


def cost(flops, nbytes):
    return pl.CostEstimate(flops=flops, bytes_accessed=nbytes, transcendentals=0)


def halves(x):
    high = x.astype(BF16)
    return high, (x - high.astype(F32)).astype(BF16)


def mm(a, b, dims=(((1,), (0,)), ((), ()))):
    return lax.dot_general(a, b, dims, preferred_element_type=F32)


def slot_mask(owners, relative, cap, lengths, owner, slots, tokens):
    docs = lengths.shape[1]
    row = lax.broadcasted_iota(jnp.int32, (docs, docs), 0)
    col = lax.broadcasted_iota(jnp.int32, (docs, docs), 1)
    len_row = lengths.astype(F32)
    place_row = lax.rem(owner - lax.axis_index("dp") + 2 * owners - 1, owners) if relative else owner
    own_row = place_row.astype(F32)

    def column(values):
        return jnp.sum(jnp.where(row == col, values, 0.0), axis=1, keepdims=True)

    ends = jnp.sum(jnp.where(row <= col, column(len_row), 0.0), axis=0, keepdims=True)
    rank = jnp.sum(
        jnp.where((row < col) & (column(own_row) == own_row), 1.0, 0.0), axis=0, keepdims=True
    )
    slot = lax.broadcasted_iota(jnp.int32, (slots, docs), 0).astype(F32)
    hot = slot == own_row * cap + rank
    first = jnp.sum(jnp.where(hot, ends - len_row, 0.0), axis=1, keepdims=True)
    last = jnp.sum(jnp.where(hot, ends, 0.0), axis=1, keepdims=True)
    token = lax.broadcasted_iota(jnp.int32, (slots, tokens), 1).astype(F32)
    return jnp.where((token >= first) & (token < last), 1.0, 0.0)


def mask_kernel(owners, relative, cap, lengths_ref, owner_ref, mask_ref):
    mask_ref[...] = slot_mask(owners, relative, cap, lengths_ref[...], owner_ref[...], *mask_ref.shape)


def dispatch_mask(lengths, owner_row, owners, cap, tokens, relative):
    return pl.pallas_call(
        functools.partial(mask_kernel, owners, relative, cap),
        out_shape=jax.ShapeDtypeStruct((owners * cap, tokens), F32),
        compiler_params=params(8),
        cost_estimate=cost(MASK_FLOPS, 0),
    )(lengths, owner_row)


def put_projection(out_ref, proj_ref, act_ref):
    half = act_ref.shape[0] // 2
    out_ref[:, :half] = mm(proj_ref[...], act_ref[:half, :], NT)
    out_ref[:, half:] = mm(act_ref[half:, :], proj_ref[...], NT).T


def x_kernel(act_ref, proj_ref, *refs):
    put_projection(refs[-1], proj_ref, act_ref)


def project_x(act, in_t, tokens):
    return pl.pallas_call(
        x_kernel,
        in_specs=[pl.BlockSpec(memory_space=pltpu.VMEM)] * 2
        + [pl.BlockSpec(memory_space=pl.ANY)] * len(tokens),
        out_shape=jax.ShapeDtypeStruct((in_t.shape[0], act.shape[0]), F32),
        compiler_params=params(8),
        cost_estimate=cost(X_FLOPS, 0),
    )(act, in_t, *tokens)


def g_kernel(width, grad_ref, proj_ref, keep_ref, send_ref, full):
    put_projection(full, proj_ref, grad_ref)
    me = lax.axis_index("tensor")
    count = full.shape[0] // width
    for apart in range(count):
        block = pl.ds(pl.multiple_of((me ^ apart) * width, width), width)
        ref, spot = (keep_ref, apart) if apart < count // 2 else (send_ref, apart - count // 2)
        ref[spot * width : (spot + 1) * width, :] = full[block, :]


def project_g(grad, out_t, width):
    tokens, rank = grad.shape[0], out_t.shape[0]
    part = jax.ShapeDtypeStruct((rank // 2, tokens), F32)
    return pl.pallas_call(
        functools.partial(g_kernel, width),
        out_shape=[part, part],
        scratch_shapes=[pltpu.VMEM((rank, tokens), F32)],
        compiler_params=params(24),
        cost_estimate=cost(0, 0),
    )(grad, out_t)


def stack(refs):
    return jnp.concatenate([r[...] for r in refs], axis=0)


def fold_kernel(rank, owned, came, keep_ref, *refs):
    first_ref, second_ref, kept_ref = refs[-3:]
    got = stack(refs[owned : owned + came])
    total = keep_ref[...] + got[rank:]
    kept = kept_ref.shape[0]
    kept_ref[...] = total[:kept]
    x = stack(refs[:owned])[:rank] + got[:rank]
    sent = jnp.concatenate([x, total[kept:]], axis=0)
    cut = first_ref.shape[0]
    first_ref[...] = sent[:cut]
    second_ref[...] = sent[cut:]


def fold(rank, keep, own, gots, pieces):
    tokens = keep.shape[1]
    kept = keep.shape[0] // 2
    cut = (rank + kept) // 16 * 8
    *sent, keep = pl.pallas_call(
        functools.partial(fold_kernel, rank, len(own), len(gots)),
        in_specs=[pl.BlockSpec(memory_space=pltpu.VMEM)] * (1 + len(own) + len(gots))
        + [pl.BlockSpec(memory_space=pl.ANY)] * len(pieces),
        out_shape=[
            jax.ShapeDtypeStruct((rows, tokens), F32) for rows in (cut, rank + kept - cut, kept)
        ],
        compiler_params=params(16),
        cost_estimate=cost(0, 0),
    )(keep, *own, *gots, *pieces)
    return keep, sent


def outer_kernel(owners, sent, g_ref, mask_ref, *refs):
    blocks = refs[-owners:]
    width = g_ref.shape[0]
    own, got = stack(refs[:sent]), stack(refs[sent : 2 * sent])
    rank = got.shape[0] - width
    x_full = own[:rank] + got[:rank]
    g_full = g_ref[...] + got[rank:]
    x_both = jnp.concatenate(halves(x_full), axis=0)
    g_high = g_full.astype(BF16).astype(F32)
    g_low = g_full - g_high
    mask = mask_ref[...]
    cap = blocks[0].shape[0]

    slots = mask.shape[0]
    group = min(width, GROUP)
    for i in range(0, width, group):
        rows = [mask * g[j : j + 1, :] for j in range(i, i + group) for g in (g_high, g_low)]
        both = mm(jnp.concatenate([r.astype(BF16) for r in rows], axis=0), x_both, NT)
        columns = []
        for j in range(group):
            high = both[2 * j * slots : (2 * j + 1) * slots]
            low = both[(2 * j + 1) * slots : (2 * j + 2) * slots]
            columns.append(high[:, :rank] + high[:, rank:] + low[:, :rank])
        out = jnp.concatenate(columns, axis=1)
        for k, block in enumerate(blocks):
            block[:, i * rank : (i + group) * rank] = out[k * cap : (k + 1) * cap, :]


def outer(sent, gots, g, mask, owners):
    slots, tokens = mask.shape
    width = g.shape[0]
    rank = sum(p.shape[0] for p in sent) - width
    cap = slots // owners
    return pl.pallas_call(
        functools.partial(outer_kernel, owners, len(sent)),
        out_shape=[jax.ShapeDtypeStruct((cap, width * rank), F32)] * owners,
        compiler_params=params(24),
        cost_estimate=cost(8 * slots * width * tokens * rank, 4 * slots * width * rank),
    )(g, mask, *sent, *gots)


def token_kernel(*refs):
    refs[-1][...] = jnp.zeros_like(refs[-1])


def token(arrays, flops):
    return pl.pallas_call(
        token_kernel,
        in_specs=[pl.BlockSpec(memory_space=pl.ANY)] * len(arrays),
        out_shape=jax.ShapeDtypeStruct((8, 128), F32),
        compiler_params=params(4),
        cost_estimate=cost(flops, 0),
    )(*arrays)


def after_kernel(block_ref, piece, out_ref):
    out_ref[...] = block_ref[...]


def after(block, piece):
    return pl.pallas_call(
        after_kernel,
        in_specs=[pl.BlockSpec(memory_space=pltpu.VMEM), pl.BlockSpec(memory_space=pl.ANY)],
        out_shape=jax.ShapeDtypeStruct(block.shape, F32),
        compiler_params=params(4),
        cost_estimate=cost(0, 0),
    )(block, piece)


def score_kernel(count, gaps, relative, ids_ref, *refs):
    rows, pieces, scores_ref = refs[:count], refs[count : count + len(gaps)], refs[-1]
    queries = ids_ref.shape[1]
    me = lax.axis_index("dp")
    cap = rows[0].shape[0]
    high, low = halves(stack(rows))
    slots = high.shape[0]
    both = jnp.concatenate([high, low], axis=0)
    held = pieces[0].shape[0]
    pool = stack(pieces)
    products = mm(both, jnp.concatenate(halves(pool), axis=0), NT)
    split = pool.shape[0]
    part = products[:slots, :split] + products[:slots, split:] + products[slots:, :split]
    row = lax.broadcasted_iota(jnp.int32, (held, queries), 0)
    places = [row + ((me ^ gap) * held if len(gaps) > 1 else 0) for gap in gaps]
    hot = (jnp.concatenate(places, axis=0) == ids_ref[...]).astype(F32).astype(BF16)
    top, rest = halves(part)
    last = (part - top.astype(F32) - rest.astype(F32)).astype(BF16)
    picked = mm(jnp.concatenate([top, rest, last], axis=0), hot)
    total = picked[:slots] + picked[slots : 2 * slots] + picked[2 * slots :]
    for k in range(count):
        source = lax.rem(me - k + count, count) if relative else k
        spot = pl.ds(pl.multiple_of(source * cap, cap), cap)
        scores_ref[spot, :] = total[k * cap : (k + 1) * cap, :]


def score(ids_row, rows, pieces, gaps, relative, tokens):
    slots = rows[0].shape[0] * len(rows)
    queries = ids_row.shape[1]
    size, feats = pieces[0].shape
    flops = 6 * slots * size * len(gaps) * feats
    return pl.pallas_call(
        functools.partial(score_kernel, len(rows), gaps, relative),
        in_specs=[pl.BlockSpec(memory_space=pltpu.VMEM)] * (1 + len(rows) + len(pieces))
        + [pl.BlockSpec(memory_space=pl.ANY)] * len(tokens),
        out_shape=jax.ShapeDtypeStruct((slots, queries), F32),
        compiler_params=params(24),
        cost_estimate=cost(flops, 4 * size * len(gaps) * feats),
    )(ids_row, *rows, *pieces, *tokens)


def place_kernel(*refs):
    rows, store_ref = refs[:-1], refs[-1]
    me = lax.axis_index("dp")
    cap = rows[0].shape[0]
    for k, row in enumerate(rows):
        source = lax.rem(me - k + len(rows), len(rows))
        store_ref[pl.ds(pl.multiple_of(source * cap, cap), cap), :] = row[...]


def place(rows):
    slots, feats = rows[0].shape[0] * len(rows), rows[0].shape[1]
    return pl.pallas_call(
        place_kernel,
        out_shape=jax.ShapeDtypeStruct((slots, feats), F32),
        compiler_params=params(16),
        cost_estimate=cost(0, 8 * slots * feats),
    )(*rows)


def swap(x, axis, gap):
    return lax.ppermute(x, axis, [(i, i ^ gap) for i in range(lax.axis_size(axis))])


def shift(x, axis, by):
    size = lax.axis_size(axis)
    return lax.ppermute(x, axis, [(i, (i + by) % size) for i in range(size)])


def gather_pieces(piece):
    pieces, gaps = [piece], [0]
    bit = lax.axis_size("dp") // 2
    while bit > 1:
        pieces, gaps = pieces + [swap(p, "dp", bit) for p in pieces], gaps + [g ^ bit for g in gaps]
        bit //= 2
    return pieces, gaps


def local(
    activations, out_grads, proj_in, proj_out, doc_lengths, doc_owner, query_grads, query_ids
):
    tensor_size = lax.axis_size("tensor")
    data_size = lax.axis_size("dp")
    tokens = activations.shape[0]
    rank = proj_in.shape[1]
    width = rank // tensor_size
    docs = doc_owner.shape[0]
    cap = max(2, 2 * docs // data_size)
    direct = data_size <= MOST_DIRECT

    if direct:
        pieces, gaps = gather_pieces(query_grads)
        mate = swap(query_grads, "dp", 1)
        passed = [swap(piece, "dp", 1) for piece in pieces[1:]]
    else:
        pieces, gaps = [lax.all_gather(query_grads, "dp", axis=0, tiled=True)], [0]

    mask = dispatch_mask(doc_lengths, doc_owner.T, data_size, cap, activations.shape[0], direct)
    x = project_x(activations, proj_in.T, [token([], FIRST_FLOPS)])
    bit = tensor_size // 2
    x_got = swap(x, "tensor", bit)
    keep, send = project_g(out_grads, proj_out.T, width)
    early = [mask] + ([token(pieces[1:], EARLY_FLOPS)] if direct else [])
    own, gots = [x], [x_got, swap(send, "tensor", bit)]
    while bit > 1:
        bit //= 2
        keep, own = fold(rank, keep, own, gots, early)
        gots = [swap(part, "tensor", bit) for part in own]
    blocks = outer(own, gots, keep, mask, data_size)
    if direct:
        *sent, kept = blocks
        sent[-1] = after(sent[-1], mate)
        rows = [kept] + [shift(block, "dp", k) for k, block in enumerate(sent, 1)]
        late = []
        for row in rows[1:-1]:
            late = [token([row, *late], LATE_FLOPS)]
        pieces, gaps = [*pieces, mate, *passed], [*gaps, *(g ^ 1 for g in gaps)]
        store = place(rows)
    else:
        rows = [lax.all_to_all(jnp.stack(blocks), "dp", 0, 0, tiled=True).reshape(-1, width * rank)]
        store, late = rows[0], []
    scores = score(query_ids[None, :], rows, pieces, gaps, direct, late)
    bit = 1
    while bit < tensor_size:
        scores = scores + swap(scores, "tensor", bit)
        bit *= 2
    return store, scores * (1.0 / (rank * rank))


def solution(mesh):
    return jax.shard_map(
        local,
        mesh=mesh,
        in_specs=(
            P(("groups", "dp"), "tensor"),
            P(("groups", "dp"), "tensor"),
            P("tensor", None),
            P("tensor", None),
            P(("groups", "dp"), None),
            P(("groups", "dp"), None),
            P(("groups", "dp"), "tensor"),
            P("groups"),
        ),
        out_specs=(P(("groups", "dp"), "tensor"), P(("groups", "dp"), None)),
        check_vma=False,
    )
```

```python
import functools

import jax
import jax.numpy as jnp
from jax import lax
from jax.experimental import pallas as pl
from jax.experimental.pallas import tpu as pltpu
from jax.sharding import PartitionSpec as P

F32 = jnp.float32
BF16 = jnp.bfloat16
MIB = 1024 * 1024
NT = (((1,), (1,)), ((), ()))
MOST_DIRECT = 8
GROUP = 4
FIRST_FLOPS = 10 * 10**8
X_FLOPS = 6 * 10**8
MASK_FLOPS = 2 * 10**8
EARLY_FLOPS = 3 * 10**8
LATE_FLOPS = 10**8


def params(mib):
    return pltpu.CompilerParams(vmem_limit_bytes=mib * MIB)


def cost(flops, nbytes):
    return pl.CostEstimate(flops=flops, bytes_accessed=nbytes, transcendentals=0)


def halves(x):
    high = x.astype(BF16)
    return high, (x - high.astype(F32)).astype(BF16)


def mm(a, b, dims=(((1,), (0,)), ((), ()))):
    return lax.dot_general(a, b, dims, preferred_element_type=F32)


def slot_mask(owners, relative, cap, lengths, owner, slots, tokens):
    docs = lengths.shape[1]
    row = lax.broadcasted_iota(jnp.int32, (docs, docs), 0)
    col = lax.broadcasted_iota(jnp.int32, (docs, docs), 1)
    len_row = lengths.astype(F32)
    place_row = lax.rem(owner - lax.axis_index("dp") + 2 * owners - 1, owners) if relative else owner
    own_row = place_row.astype(F32)

    def column(values):
        return jnp.sum(jnp.where(row == col, values, 0.0), axis=1, keepdims=True)

    ends = jnp.sum(jnp.where(row <= col, column(len_row), 0.0), axis=0, keepdims=True)
    rank = jnp.sum(
        jnp.where((row < col) & (column(own_row) == own_row), 1.0, 0.0), axis=0, keepdims=True
    )
    slot = lax.broadcasted_iota(jnp.int32, (slots, docs), 0).astype(F32)
    hot = slot == own_row * cap + rank
    first = jnp.sum(jnp.where(hot, ends - len_row, 0.0), axis=1, keepdims=True)
    last = jnp.sum(jnp.where(hot, ends, 0.0), axis=1, keepdims=True)
    token = lax.broadcasted_iota(jnp.int32, (slots, tokens), 1).astype(F32)
    return jnp.where((token >= first) & (token < last), 1.0, 0.0)


def mask_kernel(owners, relative, cap, lengths_ref, owner_ref, mask_ref):
    mask_ref[...] = slot_mask(owners, relative, cap, lengths_ref[...], owner_ref[...], *mask_ref.shape)


def dispatch_mask(lengths, owner_row, owners, cap, tokens, relative):
    return pl.pallas_call(
        functools.partial(mask_kernel, owners, relative, cap),
        out_shape=jax.ShapeDtypeStruct((owners * cap, tokens), F32),
        compiler_params=params(8),
        cost_estimate=cost(MASK_FLOPS, 0),
    )(lengths, owner_row)


def put_projection(out_ref, proj_ref, act_ref):
    half = act_ref.shape[0] // 2
    out_ref[:, :half] = mm(proj_ref[...], act_ref[:half, :], NT)
    out_ref[:, half:] = mm(act_ref[half:, :], proj_ref[...], NT).T


def x_kernel(act_ref, proj_ref, *refs):
    put_projection(refs[-1], proj_ref, act_ref)


def project_x(act, in_t, tokens):
    return pl.pallas_call(
        x_kernel,
        in_specs=[pl.BlockSpec(memory_space=pltpu.VMEM)] * 2
        + [pl.BlockSpec(memory_space=pl.ANY)] * len(tokens),
        out_shape=jax.ShapeDtypeStruct((in_t.shape[0], act.shape[0]), F32),
        compiler_params=params(8),
        cost_estimate=cost(X_FLOPS, 0),
    )(act, in_t, *tokens)


def g_kernel(width, grad_ref, proj_ref, keep_ref, send_ref, full):
    put_projection(full, proj_ref, grad_ref)
    me = lax.axis_index("tensor")
    count = full.shape[0] // width
    for apart in range(count):
        block = pl.ds(pl.multiple_of((me ^ apart) * width, width), width)
        ref, spot = (keep_ref, apart) if apart < count // 2 else (send_ref, apart - count // 2)
        ref[spot * width : (spot + 1) * width, :] = full[block, :]


def project_g(grad, out_t, width):
    tokens, rank = grad.shape[0], out_t.shape[0]
    part = jax.ShapeDtypeStruct((rank // 2, tokens), F32)
    return pl.pallas_call(
        functools.partial(g_kernel, width),
        out_shape=[part, part],
        scratch_shapes=[pltpu.VMEM((rank, tokens), F32)],
        compiler_params=params(24),
        cost_estimate=cost(0, 0),
    )(grad, out_t)


def stack(refs):
    return jnp.concatenate([r[...] for r in refs], axis=0)


def fold_kernel(rank, owned, came, keep_ref, *refs):
    first_ref, second_ref, kept_ref = refs[-3:]
    got = stack(refs[owned : owned + came])
    total = keep_ref[...] + got[rank:]
    kept = kept_ref.shape[0]
    kept_ref[...] = total[:kept]
    x = stack(refs[:owned])[:rank] + got[:rank]
    sent = jnp.concatenate([x, total[kept:]], axis=0)
    cut = first_ref.shape[0]
    first_ref[...] = sent[:cut]
    second_ref[...] = sent[cut:]


def fold(rank, keep, own, gots, pieces):
    tokens = keep.shape[1]
    kept = keep.shape[0] // 2
    cut = (rank + kept) // 16 * 8
    *sent, keep = pl.pallas_call(
        functools.partial(fold_kernel, rank, len(own), len(gots)),
        in_specs=[pl.BlockSpec(memory_space=pltpu.VMEM)] * (1 + len(own) + len(gots))
        + [pl.BlockSpec(memory_space=pl.ANY)] * len(pieces),
        out_shape=[
            jax.ShapeDtypeStruct((rows, tokens), F32) for rows in (cut, rank + kept - cut, kept)
        ],
        compiler_params=params(16),
        cost_estimate=cost(0, 0),
    )(keep, *own, *gots, *pieces)
    return keep, sent


def outer_kernel(owners, sent, g_ref, mask_ref, *refs):
    blocks = refs[-owners:]
    width = g_ref.shape[0]
    own, got = stack(refs[:sent]), stack(refs[sent : 2 * sent])
    rank = got.shape[0] - width
    x_full = own[:rank] + got[:rank]
    g_full = g_ref[...] + got[rank:]
    x_both = jnp.concatenate(halves(x_full), axis=0)
    g_high = g_full.astype(BF16).astype(F32)
    g_low = g_full - g_high
    mask = mask_ref[...]
    cap = blocks[0].shape[0]

    slots = mask.shape[0]
    group = min(width, GROUP)
    for i in range(0, width, group):
        rows = [mask * g[j : j + 1, :] for j in range(i, i + group) for g in (g_high, g_low)]
        both = mm(jnp.concatenate([r.astype(BF16) for r in rows], axis=0), x_both, NT)
        columns = []
        for j in range(group):
            high = both[2 * j * slots : (2 * j + 1) * slots]
            low = both[(2 * j + 1) * slots : (2 * j + 2) * slots]
            columns.append(high[:, :rank] + high[:, rank:] + low[:, :rank])
        out = jnp.concatenate(columns, axis=1)
        for k, block in enumerate(blocks):
            block[:, i * rank : (i + group) * rank] = out[k * cap : (k + 1) * cap, :]


def outer(sent, gots, g, mask, owners):
    slots, tokens = mask.shape
    width = g.shape[0]
    rank = sum(p.shape[0] for p in sent) - width
    cap = slots // owners
    return pl.pallas_call(
        functools.partial(outer_kernel, owners, len(sent)),
        out_shape=[jax.ShapeDtypeStruct((cap, width * rank), F32)] * owners,
        compiler_params=params(24),
        cost_estimate=cost(8 * slots * width * tokens * rank, 4 * slots * width * rank),
    )(g, mask, *sent, *gots)


def token_kernel(*refs):
    refs[-1][...] = jnp.zeros_like(refs[-1])


def token(arrays, flops):
    return pl.pallas_call(
        token_kernel,
        in_specs=[pl.BlockSpec(memory_space=pl.ANY)] * len(arrays),
        out_shape=jax.ShapeDtypeStruct((8, 128), F32),
        compiler_params=params(4),
        cost_estimate=cost(flops, 0),
    )(*arrays)


def after_kernel(block_ref, *refs):
    refs[-1][...] = block_ref[...]


def after(block, pieces):
    return pl.pallas_call(
        after_kernel,
        in_specs=[pl.BlockSpec(memory_space=pltpu.VMEM)]
        + [pl.BlockSpec(memory_space=pl.ANY)] * len(pieces),
        out_shape=jax.ShapeDtypeStruct(block.shape, F32),
        compiler_params=params(4),
        cost_estimate=cost(0, 0),
    )(block, *pieces)


def score_kernel(count, gaps, relative, ids_ref, *refs):
    rows, pieces, scores_ref = refs[:count], refs[count : count + len(gaps)], refs[-1]
    queries = ids_ref.shape[1]
    me = lax.axis_index("dp")
    cap = rows[0].shape[0]
    high, low = halves(stack(rows))
    slots = high.shape[0]
    both = jnp.concatenate([high, low], axis=0)
    held = pieces[0].shape[0]
    pool = stack(pieces)
    products = mm(both, jnp.concatenate(halves(pool), axis=0), NT)
    split = pool.shape[0]
    part = products[:slots, :split] + products[:slots, split:] + products[slots:, :split]
    row = lax.broadcasted_iota(jnp.int32, (held, queries), 0)
    places = [row + ((me ^ gap) * held if len(gaps) > 1 else 0) for gap in gaps]
    hot = (jnp.concatenate(places, axis=0) == ids_ref[...]).astype(F32).astype(BF16)
    top, rest = halves(part)
    last = (part - top.astype(F32) - rest.astype(F32)).astype(BF16)
    picked = mm(jnp.concatenate([top, rest, last], axis=0), hot)
    total = picked[:slots] + picked[slots : 2 * slots] + picked[2 * slots :]
    for k in range(count):
        source = lax.rem(me - k + count, count) if relative else k
        spot = pl.ds(pl.multiple_of(source * cap, cap), cap)
        scores_ref[spot, :] = total[k * cap : (k + 1) * cap, :]


def score(ids_row, rows, pieces, gaps, relative, tokens):
    slots = rows[0].shape[0] * len(rows)
    queries = ids_row.shape[1]
    size, feats = pieces[0].shape
    flops = 6 * slots * size * len(gaps) * feats
    return pl.pallas_call(
        functools.partial(score_kernel, len(rows), gaps, relative),
        in_specs=[pl.BlockSpec(memory_space=pltpu.VMEM)] * (1 + len(rows) + len(pieces))
        + [pl.BlockSpec(memory_space=pl.ANY)] * len(tokens),
        out_shape=jax.ShapeDtypeStruct((slots, queries), F32),
        compiler_params=params(24),
        cost_estimate=cost(flops, 4 * size * len(gaps) * feats),
    )(ids_row, *rows, *pieces, *tokens)


def place_kernel(*refs):
    rows, store_ref = refs[:-1], refs[-1]
    me = lax.axis_index("dp")
    cap = rows[0].shape[0]
    for k, row in enumerate(rows):
        source = lax.rem(me - k + len(rows), len(rows))
        store_ref[pl.ds(pl.multiple_of(source * cap, cap), cap), :] = row[...]


def place(rows):
    slots, feats = rows[0].shape[0] * len(rows), rows[0].shape[1]
    return pl.pallas_call(
        place_kernel,
        out_shape=jax.ShapeDtypeStruct((slots, feats), F32),
        compiler_params=params(16),
        cost_estimate=cost(0, 8 * slots * feats),
    )(*rows)


def swap(x, axis, gap):
    return lax.ppermute(x, axis, [(i, i ^ gap) for i in range(lax.axis_size(axis))])


def shift(x, axis, by):
    size = lax.axis_size(axis)
    return lax.ppermute(x, axis, [(i, (i + by) % size) for i in range(size)])


def gather_pieces(piece):
    pieces, gaps = [piece], [0]
    bit = lax.axis_size("dp") // 2
    while bit > 1:
        pieces, gaps = pieces + [swap(p, "dp", bit) for p in pieces], gaps + [g ^ bit for g in gaps]
        bit //= 2
    return pieces, gaps


def local(
    activations, out_grads, proj_in, proj_out, doc_lengths, doc_owner, query_grads, query_ids
):
    tensor_size = lax.axis_size("tensor")
    data_size = lax.axis_size("dp")
    tokens = activations.shape[0]
    rank = proj_in.shape[1]
    width = rank // tensor_size
    docs = doc_owner.shape[0]
    cap = max(2, 2 * docs // data_size)
    direct = data_size <= MOST_DIRECT

    if direct:
        pieces, gaps = gather_pieces(query_grads)
        mate = swap(query_grads, "dp", 1)
        passed = [swap(piece, "dp", 1) for piece in pieces[1:]]
    else:
        pieces, gaps = [lax.all_gather(query_grads, "dp", axis=0, tiled=True)], [0]

    mask = dispatch_mask(doc_lengths, doc_owner.T, data_size, cap, activations.shape[0], direct)
    x = project_x(activations, proj_in.T, [token([], FIRST_FLOPS)])
    bit = tensor_size // 2
    x_got = swap(x, "tensor", bit)
    keep, send = project_g(out_grads, proj_out.T, width)
    early = [mask] + ([token(pieces[1:], EARLY_FLOPS)] if direct else [])
    own, gots = [x], [x_got, swap(send, "tensor", bit)]
    while bit > 1:
        bit //= 2
        keep, own = fold(rank, keep, own, gots, early)
        gots = [swap(part, "tensor", bit) for part in own]
    blocks = outer(own, gots, keep, mask, data_size)
    if direct:
        *sent, kept = blocks
        sent[-1] = after(sent[-1], [mate, *passed])
        rows = [kept] + [shift(block, "dp", k) for k, block in enumerate(sent, 1)]
        late = []
        for row in rows[1:-1]:
            late = [token([row, *late], LATE_FLOPS)]
        pieces, gaps = [*pieces, mate, *passed], [*gaps, *(g ^ 1 for g in gaps)]
        store = place(rows)
    else:
        rows = [lax.all_to_all(jnp.stack(blocks), "dp", 0, 0, tiled=True).reshape(-1, width * rank)]
        store, late = rows[0], []
    scores = score(query_ids[None, :], rows, pieces, gaps, direct, late)
    bit = 1
    while bit < tensor_size:
        scores = scores + swap(scores, "tensor", bit)
        bit *= 2
    return store, scores * (1.0 / (rank * rank))


def solution(mesh):
    return jax.shard_map(
        local,
        mesh=mesh,
        in_specs=(
            P(("groups", "dp"), "tensor"),
            P(("groups", "dp"), "tensor"),
            P("tensor", None),
            P("tensor", None),
            P(("groups", "dp"), None),
            P(("groups", "dp"), None),
            P(("groups", "dp"), "tensor"),
            P("groups"),
        ),
        out_specs=(P(("groups", "dp"), "tensor"), P(("groups", "dp"), None)),
        check_vma=False,
    )
```

```python
import functools

import jax
import jax.numpy as jnp
from jax import lax
from jax.experimental import pallas as pl
from jax.experimental.pallas import tpu as pltpu
from jax.sharding import PartitionSpec as P

F32 = jnp.float32
BF16 = jnp.bfloat16
MIB = 1024 * 1024
NT = (((1,), (1,)), ((), ()))
MOST_DIRECT = 8
GROUP = 4
FIRST_FLOPS = 10 * 10**8
X_FLOPS = 6 * 10**8
MASK_FLOPS = 2 * 10**8
EARLY_FLOPS = 3 * 10**8
AFTER_FLOPS = 6 * 10**8
LATE_FLOPS = 10**8


def params(mib):
    return pltpu.CompilerParams(vmem_limit_bytes=mib * MIB)


def cost(flops, nbytes):
    return pl.CostEstimate(flops=flops, bytes_accessed=nbytes, transcendentals=0)


def halves(x):
    high = x.astype(BF16)
    return high, (x - high.astype(F32)).astype(BF16)


def mm(a, b, dims=(((1,), (0,)), ((), ()))):
    return lax.dot_general(a, b, dims, preferred_element_type=F32)


def slot_mask(owners, relative, cap, lengths, owner, slots, tokens):
    docs = lengths.shape[1]
    row = lax.broadcasted_iota(jnp.int32, (docs, docs), 0)
    col = lax.broadcasted_iota(jnp.int32, (docs, docs), 1)
    len_row = lengths.astype(F32)
    place_row = lax.rem(owner - lax.axis_index("dp") + 2 * owners - 1, owners) if relative else owner
    own_row = place_row.astype(F32)

    def column(values):
        return jnp.sum(jnp.where(row == col, values, 0.0), axis=1, keepdims=True)

    ends = jnp.sum(jnp.where(row <= col, column(len_row), 0.0), axis=0, keepdims=True)
    rank = jnp.sum(
        jnp.where((row < col) & (column(own_row) == own_row), 1.0, 0.0), axis=0, keepdims=True
    )
    slot = lax.broadcasted_iota(jnp.int32, (slots, docs), 0).astype(F32)
    hot = slot == own_row * cap + rank
    first = jnp.sum(jnp.where(hot, ends - len_row, 0.0), axis=1, keepdims=True)
    last = jnp.sum(jnp.where(hot, ends, 0.0), axis=1, keepdims=True)
    token = lax.broadcasted_iota(jnp.int32, (slots, tokens), 1).astype(F32)
    return jnp.where((token >= first) & (token < last), 1.0, 0.0)


def mask_kernel(owners, relative, cap, lengths_ref, owner_ref, mask_ref):
    mask_ref[...] = slot_mask(owners, relative, cap, lengths_ref[...], owner_ref[...], *mask_ref.shape)


def dispatch_mask(lengths, owner_row, owners, cap, tokens, relative):
    return pl.pallas_call(
        functools.partial(mask_kernel, owners, relative, cap),
        out_shape=jax.ShapeDtypeStruct((owners * cap, tokens), F32),
        compiler_params=params(8),
        cost_estimate=cost(MASK_FLOPS, 0),
    )(lengths, owner_row)


def put_projection(out_ref, proj_ref, act_ref):
    half = act_ref.shape[0] // 2
    out_ref[:, :half] = mm(proj_ref[...], act_ref[:half, :], NT)
    out_ref[:, half:] = mm(act_ref[half:, :], proj_ref[...], NT).T


def x_kernel(act_ref, proj_ref, *refs):
    put_projection(refs[-1], proj_ref, act_ref)


def project_x(act, in_t, tokens):
    return pl.pallas_call(
        x_kernel,
        in_specs=[pl.BlockSpec(memory_space=pltpu.VMEM)] * 2
        + [pl.BlockSpec(memory_space=pl.ANY)] * len(tokens),
        out_shape=jax.ShapeDtypeStruct((in_t.shape[0], act.shape[0]), F32),
        compiler_params=params(8),
        cost_estimate=cost(X_FLOPS, 0),
    )(act, in_t, *tokens)


def g_kernel(width, grad_ref, proj_ref, keep_ref, send_ref, full):
    put_projection(full, proj_ref, grad_ref)
    me = lax.axis_index("tensor")
    count = full.shape[0] // width
    for apart in range(count):
        block = pl.ds(pl.multiple_of((me ^ apart) * width, width), width)
        ref, spot = (keep_ref, apart) if apart < count // 2 else (send_ref, apart - count // 2)
        ref[spot * width : (spot + 1) * width, :] = full[block, :]


def project_g(grad, out_t, width):
    tokens, rank = grad.shape[0], out_t.shape[0]
    part = jax.ShapeDtypeStruct((rank // 2, tokens), F32)
    return pl.pallas_call(
        functools.partial(g_kernel, width),
        out_shape=[part, part],
        scratch_shapes=[pltpu.VMEM((rank, tokens), F32)],
        compiler_params=params(24),
        cost_estimate=cost(0, 0),
    )(grad, out_t)


def stack(refs):
    return jnp.concatenate([r[...] for r in refs], axis=0)


def fold_kernel(rank, owned, came, keep_ref, *refs):
    first_ref, second_ref, kept_ref = refs[-3:]
    got = stack(refs[owned : owned + came])
    total = keep_ref[...] + got[rank:]
    kept = kept_ref.shape[0]
    kept_ref[...] = total[:kept]
    x = stack(refs[:owned])[:rank] + got[:rank]
    sent = jnp.concatenate([x, total[kept:]], axis=0)
    cut = first_ref.shape[0]
    first_ref[...] = sent[:cut]
    second_ref[...] = sent[cut:]


def fold(rank, keep, own, gots, pieces):
    tokens = keep.shape[1]
    kept = keep.shape[0] // 2
    cut = (rank + kept) // 16 * 8
    *sent, keep = pl.pallas_call(
        functools.partial(fold_kernel, rank, len(own), len(gots)),
        in_specs=[pl.BlockSpec(memory_space=pltpu.VMEM)] * (1 + len(own) + len(gots))
        + [pl.BlockSpec(memory_space=pl.ANY)] * len(pieces),
        out_shape=[
            jax.ShapeDtypeStruct((rows, tokens), F32) for rows in (cut, rank + kept - cut, kept)
        ],
        compiler_params=params(16),
        cost_estimate=cost(0, 0),
    )(keep, *own, *gots, *pieces)
    return keep, sent


def outer_kernel(owners, sent, g_ref, mask_ref, *refs):
    blocks = refs[-owners:]
    width = g_ref.shape[0]
    own, got = stack(refs[:sent]), stack(refs[sent : 2 * sent])
    rank = got.shape[0] - width
    x_full = own[:rank] + got[:rank]
    g_full = g_ref[...] + got[rank:]
    x_both = jnp.concatenate(halves(x_full), axis=0)
    g_high = g_full.astype(BF16).astype(F32)
    g_low = g_full - g_high
    mask = mask_ref[...]
    cap = blocks[0].shape[0]

    slots = mask.shape[0]
    group = min(width, GROUP)
    for i in range(0, width, group):
        rows = [mask * g[j : j + 1, :] for j in range(i, i + group) for g in (g_high, g_low)]
        both = mm(jnp.concatenate([r.astype(BF16) for r in rows], axis=0), x_both, NT)
        columns = []
        for j in range(group):
            high = both[2 * j * slots : (2 * j + 1) * slots]
            low = both[(2 * j + 1) * slots : (2 * j + 2) * slots]
            columns.append(high[:, :rank] + high[:, rank:] + low[:, :rank])
        out = jnp.concatenate(columns, axis=1)
        for k, block in enumerate(blocks):
            block[:, i * rank : (i + group) * rank] = out[k * cap : (k + 1) * cap, :]


def outer(sent, gots, g, mask, owners):
    slots, tokens = mask.shape
    width = g.shape[0]
    rank = sum(p.shape[0] for p in sent) - width
    cap = slots // owners
    return pl.pallas_call(
        functools.partial(outer_kernel, owners, len(sent)),
        out_shape=[jax.ShapeDtypeStruct((cap, width * rank), F32)] * owners,
        compiler_params=params(24),
        cost_estimate=cost(8 * slots * width * tokens * rank, 4 * slots * width * rank),
    )(g, mask, *sent, *gots)


def token_kernel(*refs):
    refs[-1][...] = jnp.zeros_like(refs[-1])


def token(arrays, flops):
    return pl.pallas_call(
        token_kernel,
        in_specs=[pl.BlockSpec(memory_space=pl.ANY)] * len(arrays),
        out_shape=jax.ShapeDtypeStruct((8, 128), F32),
        compiler_params=params(4),
        cost_estimate=cost(flops, 0),
    )(*arrays)


def after_kernel(count, *refs):
    for block_ref, out_ref in zip(refs[:count], refs[-count:]):
        out_ref[...] = block_ref[...]


def after(blocks, pieces):
    count = len(blocks)
    return pl.pallas_call(
        functools.partial(after_kernel, count),
        in_specs=[pl.BlockSpec(memory_space=pltpu.VMEM)] * count
        + [pl.BlockSpec(memory_space=pl.ANY)] * len(pieces),
        out_shape=[jax.ShapeDtypeStruct(block.shape, F32) for block in blocks],
        compiler_params=params(4),
        cost_estimate=cost(AFTER_FLOPS, 0),
    )(*blocks, *pieces)


def score_kernel(arrivals, gaps, relative, ids_ref, *refs):
    scores_ref = refs[-1]
    rows = arrived(arrivals, refs)
    pieces = refs[sum(arrivals) : sum(arrivals) + len(gaps)]
    count = len(rows)
    queries = ids_ref.shape[1]
    me = lax.axis_index("dp")
    cap = rows[0].shape[0]
    high, low = halves(jnp.concatenate(rows, axis=0))
    slots = high.shape[0]
    both = jnp.concatenate([high, low], axis=0)
    held = pieces[0].shape[0]
    pool = stack(pieces)
    products = mm(both, jnp.concatenate(halves(pool), axis=0), NT)
    split = pool.shape[0]
    part = products[:slots, :split] + products[:slots, split:] + products[slots:, :split]
    row = lax.broadcasted_iota(jnp.int32, (held, queries), 0)
    places = [row + ((me ^ gap) * held if len(gaps) > 1 else 0) for gap in gaps]
    hot = (jnp.concatenate(places, axis=0) == ids_ref[...]).astype(F32).astype(BF16)
    top, rest = halves(part)
    last = (part - top.astype(F32) - rest.astype(F32)).astype(BF16)
    picked = mm(jnp.concatenate([top, rest, last], axis=0), hot)
    total = picked[:slots] + picked[slots : 2 * slots] + picked[2 * slots :]
    for k in range(count):
        source = lax.rem(me - k + count, count) if relative else k
        spot = pl.ds(pl.multiple_of(source * cap, cap), cap)
        scores_ref[spot, :] = total[k * cap : (k + 1) * cap, :]


def arrived(arrivals, refs):
    rows, at = [], 0
    for count in arrivals:
        row = refs[at][...]
        for ref in refs[at + 1 : at + count]:
            row = row + ref[...]
        rows.append(row)
        at += count
    return rows


def score(ids_row, rows, pieces, gaps, relative, tokens):
    slots = rows[0][0].shape[0] * len(rows)
    queries = ids_row.shape[1]
    size, feats = pieces[0].shape
    flops = 6 * slots * size * len(gaps) * feats
    arrivals = tuple(len(row) for row in rows)
    arrays = [array for row in rows for array in row]
    return pl.pallas_call(
        functools.partial(score_kernel, arrivals, gaps, relative),
        in_specs=[pl.BlockSpec(memory_space=pltpu.VMEM)] * (1 + len(arrays) + len(pieces))
        + [pl.BlockSpec(memory_space=pl.ANY)] * len(tokens),
        out_shape=jax.ShapeDtypeStruct((slots, queries), F32),
        compiler_params=params(24),
        cost_estimate=cost(flops, 4 * size * len(gaps) * feats),
    )(ids_row, *arrays, *pieces, *tokens)


def place_kernel(arrivals, *refs):
    store_ref = refs[-1]
    me = lax.axis_index("dp")
    for k, row in enumerate(arrived(arrivals, refs)):
        cap, count = row.shape[0], len(arrivals)
        source = lax.rem(me - k + count, count)
        store_ref[pl.ds(pl.multiple_of(source * cap, cap), cap), :] = row


def place(rows):
    slots, feats = rows[0][0].shape[0] * len(rows), rows[0][0].shape[1]
    arrivals = tuple(len(row) for row in rows)
    return pl.pallas_call(
        functools.partial(place_kernel, arrivals),
        out_shape=jax.ShapeDtypeStruct((slots, feats), F32),
        compiler_params=params(16),
        cost_estimate=cost(0, 8 * slots * feats),
    )(*(array for row in rows for array in row))


def swap(x, axis, gap):
    return lax.ppermute(x, axis, [(i, i ^ gap) for i in range(lax.axis_size(axis))])


def shift(x, axis, by, first):
    size = lax.axis_size(axis)
    return lax.ppermute(x, axis, [(i, (i + by) % size) for i in range(size) if (i == 0) == first])


def gather_pieces(piece):
    pieces, gaps = [piece], [0]
    bit = lax.axis_size("dp") // 2
    while bit > 1:
        pieces, gaps = pieces + [swap(p, "dp", bit) for p in pieces], gaps + [g ^ bit for g in gaps]
        bit //= 2
    return pieces, gaps


def local(
    activations, out_grads, proj_in, proj_out, doc_lengths, doc_owner, query_grads, query_ids
):
    tensor_size = lax.axis_size("tensor")
    data_size = lax.axis_size("dp")
    tokens = activations.shape[0]
    rank = proj_in.shape[1]
    width = rank // tensor_size
    docs = doc_owner.shape[0]
    cap = max(2, 2 * docs // data_size)
    direct = data_size <= MOST_DIRECT

    if direct:
        pieces, gaps = gather_pieces(query_grads)
        mate = swap(query_grads, "dp", 1)
        passed = [swap(piece, "dp", 1) for piece in pieces[1:]]
    else:
        pieces, gaps = [lax.all_gather(query_grads, "dp", axis=0, tiled=True)], [0]

    mask = dispatch_mask(doc_lengths, doc_owner.T, data_size, cap, activations.shape[0], direct)
    x = project_x(activations, proj_in.T, [token([], FIRST_FLOPS)])
    bit = tensor_size // 2
    x_got = swap(x, "tensor", bit)
    keep, send = project_g(out_grads, proj_out.T, width)
    early = [mask] + ([token(pieces[1:], EARLY_FLOPS)] if direct else [])
    own, gots = [x], [x_got, swap(send, "tensor", bit)]
    while bit > 1:
        bit //= 2
        keep, own = fold(rank, keep, own, gots, early)
        gots = [swap(part, "tensor", bit) for part in own]
    blocks = outer(own, gots, keep, mask, data_size)
    if direct:
        *sent, kept = blocks
        most = [shift(block, "dp", k, False) for k, block in enumerate(sent, 1)]
        held = after(sent, [mate, *passed])
        rest = [shift(block, "dp", k, True) for k, block in enumerate(held, 1)]
        rows = [(kept,), *zip(most, rest)]
        late = [token(most, LATE_FLOPS)]
        pieces, gaps = [*pieces, mate, *passed], [*gaps, *(g ^ 1 for g in gaps)]
        store = place(rows)
    else:
        rows = [lax.all_to_all(jnp.stack(blocks), "dp", 0, 0, tiled=True).reshape(-1, width * rank)]
        store, late = rows[0], []
        rows = [(store,)]
    scores = score(query_ids[None, :], rows, pieces, gaps, direct, late)
    bit = 1
    while bit < tensor_size:
        scores = scores + swap(scores, "tensor", bit)
        bit *= 2
    return store, scores * (1.0 / (rank * rank))


def solution(mesh):
    return jax.shard_map(
        local,
        mesh=mesh,
        in_specs=(
            P(("groups", "dp"), "tensor"),
            P(("groups", "dp"), "tensor"),
            P("tensor", None),
            P("tensor", None),
            P(("groups", "dp"), None),
            P(("groups", "dp"), None),
            P(("groups", "dp"), "tensor"),
            P("groups"),
        ),
        out_specs=(P(("groups", "dp"), "tensor"), P(("groups", "dp"), None)),
        check_vma=False,
    )
```

```python
import functools

import jax
import jax.numpy as jnp
from jax import lax
from jax.experimental import pallas as pl
from jax.experimental.pallas import tpu as pltpu
from jax.sharding import PartitionSpec as P

F32 = jnp.float32
BF16 = jnp.bfloat16
MIB = 1024 * 1024
NT = (((1,), (1,)), ((), ()))
MOST_DIRECT = 8
GROUP = 8
ROWS = 16
FIRST_FLOPS = 10 * 10**8
X_FLOPS = 6 * 10**8
MASK_FLOPS = 2 * 10**8
EARLY_FLOPS = 3 * 10**8
LATE_FLOPS = 10**8
SCORE_FLOPS = 0


def params(mib):
    return pltpu.CompilerParams(vmem_limit_bytes=mib * MIB)


def cost(flops, nbytes):
    return pl.CostEstimate(flops=flops, bytes_accessed=nbytes, transcendentals=0)


def halves(x):
    high = x.astype(BF16)
    return high, (x - high.astype(F32)).astype(BF16)


def mm(a, b, dims=(((1,), (0,)), ((), ()))):
    return lax.dot_general(a, b, dims, preferred_element_type=F32)


def slot_mask(owners, relative, cap, lengths, owner, slots, tokens):
    docs = lengths.shape[1]
    row = lax.broadcasted_iota(jnp.int32, (docs, docs), 0)
    col = lax.broadcasted_iota(jnp.int32, (docs, docs), 1)
    len_row = lengths.astype(F32)
    place_row = lax.rem(owner - lax.axis_index("dp") + 2 * owners - 1, owners) if relative else owner
    own_row = place_row.astype(F32)

    def column(values):
        return jnp.sum(jnp.where(row == col, values, 0.0), axis=1, keepdims=True)

    ends = jnp.sum(jnp.where(row <= col, column(len_row), 0.0), axis=0, keepdims=True)
    rank = jnp.sum(
        jnp.where((row < col) & (column(own_row) == own_row), 1.0, 0.0), axis=0, keepdims=True
    )
    slot = lax.broadcasted_iota(jnp.int32, (slots, docs), 0).astype(F32)
    hot = slot == own_row * cap + rank
    first = jnp.sum(jnp.where(hot, ends - len_row, 0.0), axis=1, keepdims=True)
    last = jnp.sum(jnp.where(hot, ends, 0.0), axis=1, keepdims=True)
    token = lax.broadcasted_iota(jnp.int32, (slots, tokens), 1).astype(F32)
    return jnp.where((token >= first) & (token < last), 1.0, 0.0).astype(BF16)


def mask_kernel(owners, relative, cap, lengths_ref, owner_ref, mask_ref):
    mask_ref[...] = slot_mask(owners, relative, cap, lengths_ref[...], owner_ref[...], *mask_ref.shape)


def dispatch_mask(lengths, owner_row, owners, cap, tokens, relative):
    return pl.pallas_call(
        functools.partial(mask_kernel, owners, relative, cap),
        out_shape=jax.ShapeDtypeStruct((owners * cap, tokens), BF16),
        compiler_params=params(8),
        cost_estimate=cost(MASK_FLOPS, 0),
    )(lengths, owner_row)


def put_projection(out_ref, proj_ref, act_ref):
    half = act_ref.shape[0] // 2
    out_ref[:, :half] = mm(proj_ref[...], act_ref[:half, :], NT)
    out_ref[:, half:] = mm(act_ref[half:, :], proj_ref[...], NT).T


def x_kernel(act_ref, proj_ref, *refs):
    put_projection(refs[-1], proj_ref, act_ref)


def project_x(act, in_t, tokens):
    return pl.pallas_call(
        x_kernel,
        in_specs=[pl.BlockSpec(memory_space=pltpu.VMEM)] * 2
        + [pl.BlockSpec(memory_space=pl.ANY)] * len(tokens),
        out_shape=jax.ShapeDtypeStruct((in_t.shape[0], act.shape[0]), F32),
        compiler_params=params(8),
        cost_estimate=cost(X_FLOPS, 0),
    )(act, in_t, *tokens)


def g_kernel(width, grad_ref, proj_ref, keep_ref, send_ref, full):
    put_projection(full, proj_ref, grad_ref)
    me = lax.axis_index("tensor")
    count = full.shape[0] // width
    for apart in range(count):
        block = pl.ds(pl.multiple_of((me ^ apart) * width, width), width)
        ref, spot = (keep_ref, apart) if apart < count // 2 else (send_ref, apart - count // 2)
        ref[spot * width : (spot + 1) * width, :] = full[block, :]


def project_g(grad, out_t, width):
    tokens, rank = grad.shape[0], out_t.shape[0]
    part = jax.ShapeDtypeStruct((rank // 2, tokens), F32)
    return pl.pallas_call(
        functools.partial(g_kernel, width),
        out_shape=[part, part],
        scratch_shapes=[pltpu.VMEM((rank, tokens), F32)],
        compiler_params=params(24),
        cost_estimate=cost(0, 0),
    )(grad, out_t)


def stack(refs):
    return jnp.concatenate([r[...] for r in refs], axis=0)


def fold_kernel(rank, owned, came, keep_ref, *refs):
    first_ref, second_ref, kept_ref = refs[-3:]
    got = stack(refs[owned : owned + came])
    total = keep_ref[...] + got[rank:]
    kept = kept_ref.shape[0]
    kept_ref[...] = total[:kept]
    x = stack(refs[:owned])[:rank] + got[:rank]
    sent = jnp.concatenate([x, total[kept:]], axis=0)
    cut = first_ref.shape[0]
    first_ref[...] = sent[:cut]
    second_ref[...] = sent[cut:]


def fold(rank, keep, own, gots, pieces):
    tokens = keep.shape[1]
    kept = keep.shape[0] // 2
    cut = (rank + kept) // 16 * 8
    *sent, keep = pl.pallas_call(
        functools.partial(fold_kernel, rank, len(own), len(gots)),
        in_specs=[pl.BlockSpec(memory_space=pltpu.VMEM)] * (1 + len(own) + len(gots))
        + [pl.BlockSpec(memory_space=pl.ANY)] * len(pieces),
        out_shape=[
            jax.ShapeDtypeStruct((rows, tokens), F32) for rows in (cut, rank + kept - cut, kept)
        ],
        compiler_params=params(16),
        cost_estimate=cost(0, 0),
    )(keep, *own, *gots, *pieces)
    return keep, sent


def outer_kernel(first, owners, sent, g_ref, mask_ref, *refs):
    blocks = refs[-owners:]
    width = g_ref.shape[0]
    own, got = stack(refs[:sent]), stack(refs[sent : 2 * sent])
    rank = got.shape[0] - width
    x_full = own[:rank] + got[:rank]
    g_full = g_ref[...] + got[rank:]
    x_both = jnp.concatenate(halves(x_full), axis=0)
    g_high = g_full.astype(BF16).astype(F32)
    g_low = g_full - g_high
    cap = blocks[0].shape[0]
    slots = owners * cap
    mask = mask_ref[first * cap : first * cap + slots, :]
    tokens = mask.shape[1]

    def masked(row):
        wide = jnp.broadcast_to(row, (ROWS, tokens)).astype(BF16)
        return [mask[i : i + ROWS] * wide for i in range(0, slots, ROWS)]

    group = min(width, GROUP)
    for i in range(0, width, group):
        rows = [m for j in range(i, i + group) for g in (g_high, g_low) for m in masked(g[j : j + 1])]
        both = mm(jnp.concatenate(rows, axis=0), x_both, NT)
        columns = []
        for j in range(group):
            high = both[2 * j * slots : (2 * j + 1) * slots]
            low = both[(2 * j + 1) * slots : (2 * j + 2) * slots]
            columns.append(high[:, :rank] + high[:, rank:] + low[:, :rank])
        out = jnp.concatenate(columns, axis=1)
        for k, block in enumerate(blocks):
            block[:, i * rank : (i + group) * rank] = out[k * cap : (k + 1) * cap, :]


def outer(sent, gots, g, mask, cap, first, owners):
    width = g.shape[0]
    rank = sum(p.shape[0] for p in sent) - width
    return pl.pallas_call(
        functools.partial(outer_kernel, first, owners, len(sent)),
        out_shape=[jax.ShapeDtypeStruct((cap, width * rank), F32)] * owners,
        compiler_params=params(24),
        cost_estimate=cost(8 * owners * cap * width * mask.shape[1] * rank, 0),
    )(g, mask, *sent, *gots)


def token_kernel(*refs):
    refs[-1][...] = jnp.zeros_like(refs[-1])


def token(arrays, flops):
    return pl.pallas_call(
        token_kernel,
        in_specs=[pl.BlockSpec(memory_space=pl.ANY)] * len(arrays),
        out_shape=jax.ShapeDtypeStruct((8, 128), F32),
        compiler_params=params(4),
        cost_estimate=cost(flops, 0),
    )(*arrays)


def after_kernel(block_ref, *refs):
    refs[-1][...] = block_ref[...]


def after(block, pieces):
    return pl.pallas_call(
        after_kernel,
        in_specs=[pl.BlockSpec(memory_space=pltpu.VMEM)]
        + [pl.BlockSpec(memory_space=pl.ANY)] * len(pieces),
        out_shape=jax.ShapeDtypeStruct(block.shape, F32),
        compiler_params=params(4),
        cost_estimate=cost(0, 0),
    )(block, *pieces)


def pool_kernel(*refs):
    refs[-1][...] = jnp.concatenate(halves(stack(refs[:-1])), axis=0)


def pool_halves(pieces):
    rows, feats = sum(piece.shape[0] for piece in pieces), pieces[0].shape[1]
    return pl.pallas_call(
        pool_kernel,
        out_shape=jax.ShapeDtypeStruct((2 * rows, feats), BF16),
        compiler_params=params(16),
        cost_estimate=cost(0, 0),
    )(*pieces)


def scores_of(rows, ids, pool, gaps):
    me = lax.axis_index("dp")
    high, low = halves(rows)
    slots, split, queries = rows.shape[0], pool.shape[0] // 2, ids.shape[1]
    products = mm(jnp.concatenate([high, low], axis=0), pool, NT)
    part = products[:slots, :split] + products[:slots, split:] + products[slots:, :split]
    held = split // len(gaps)
    row = lax.broadcasted_iota(jnp.int32, (held, queries), 0)
    places = [row + ((me ^ gap) * held if len(gaps) > 1 else 0) for gap in gaps]
    hot = (jnp.concatenate(places, axis=0) == ids).astype(F32).astype(BF16)
    top, rest = halves(part)
    last = (part - top.astype(F32) - rest.astype(F32)).astype(BF16)
    picked = mm(jnp.concatenate([top, rest, last], axis=0), hot)
    return picked[:slots] + picked[slots : 2 * slots] + picked[2 * slots :]


def early_kernel(gaps, ids_ref, pool_ref, *refs):
    refs[-1][...] = scores_of(stack(refs[:-1]), ids_ref[...], pool_ref[...], gaps)


def score_early(ids_row, pool, rows, gaps):
    slots = sum(row.shape[0] for row in rows)
    return pl.pallas_call(
        functools.partial(early_kernel, gaps),
        out_shape=jax.ShapeDtypeStruct((slots, ids_row.shape[1]), F32),
        compiler_params=params(16),
        cost_estimate=cost(SCORE_FLOPS, 0),
    )(ids_row, pool, *rows)


def score_kernel(count, gaps, relative, ids_ref, pool_ref, early_ref, *refs):
    rows, scores_ref = refs[:count], refs[-1]
    me = lax.axis_index("dp")
    cap = rows[0].shape[0]
    total = scores_of(stack(rows), ids_ref[...], pool_ref[...], gaps)
    done = early_ref.shape[0] // cap if relative else 0
    for k in range(done + count):
        part = early_ref if k < done else total
        at = (k if k < done else k - done) * cap
        source = lax.rem(me - k + done + count, done + count) if relative else k
        scores_ref[pl.ds(pl.multiple_of(source * cap, cap), cap), :] = part[at : at + cap, :]


def score(ids_row, pool, early, rows, gaps, relative, tokens):
    slots = sum(row.shape[0] for row in rows) + (early.shape[0] if relative else 0)
    queries = ids_row.shape[1]
    return pl.pallas_call(
        functools.partial(score_kernel, len(rows), gaps, relative),
        in_specs=[pl.BlockSpec(memory_space=pltpu.VMEM)] * (3 + len(rows))
        + [pl.BlockSpec(memory_space=pl.ANY)] * len(tokens),
        out_shape=jax.ShapeDtypeStruct((slots, queries), F32),
        compiler_params=params(24),
        cost_estimate=cost(0, 0),
    )(ids_row, pool, early, *rows, *tokens)


def place_kernel(*refs):
    rows, store_ref = refs[:-1], refs[-1]
    me = lax.axis_index("dp")
    cap = rows[0].shape[0]
    for k, row in enumerate(rows):
        source = lax.rem(me - k + len(rows), len(rows))
        store_ref[pl.ds(pl.multiple_of(source * cap, cap), cap), :] = row[...]


def place(rows):
    slots, feats = rows[0].shape[0] * len(rows), rows[0].shape[1]
    return pl.pallas_call(
        place_kernel,
        out_shape=jax.ShapeDtypeStruct((slots, feats), F32),
        compiler_params=params(16),
        cost_estimate=cost(0, 8 * slots * feats),
    )(*rows)


def swap(x, axis, gap):
    return lax.ppermute(x, axis, [(i, i ^ gap) for i in range(lax.axis_size(axis))])


def shift(x, axis, by):
    size = lax.axis_size(axis)
    return lax.ppermute(x, axis, [(i, (i + by) % size) for i in range(size)])


def gather_pieces(piece):
    pieces, gaps = [piece], [0]
    bit = lax.axis_size("dp") // 2
    while bit > 1:
        pieces, gaps = pieces + [swap(p, "dp", bit) for p in pieces], gaps + [g ^ bit for g in gaps]
        bit //= 2
    return pieces, gaps


def local(
    activations, out_grads, proj_in, proj_out, doc_lengths, doc_owner, query_grads, query_ids
):
    tensor_size = lax.axis_size("tensor")
    data_size = lax.axis_size("dp")
    tokens = activations.shape[0]
    rank = proj_in.shape[1]
    width = rank // tensor_size
    docs = doc_owner.shape[0]
    cap = max(2, 2 * docs // data_size)
    direct = data_size <= MOST_DIRECT

    if direct:
        pieces, gaps = gather_pieces(query_grads)
        mate = swap(query_grads, "dp", 1)
        passed = [swap(piece, "dp", 1) for piece in pieces[1:]]
    else:
        pieces, gaps = [lax.all_gather(query_grads, "dp", axis=0, tiled=True)], [0]

    mask = dispatch_mask(doc_lengths, doc_owner.T, data_size, cap, activations.shape[0], direct)
    x = project_x(activations, proj_in.T, [token([], FIRST_FLOPS)])
    bit = tensor_size // 2
    x_got = swap(x, "tensor", bit)
    keep, send = project_g(out_grads, proj_out.T, width)
    early = [mask] + ([token(pieces[1:], EARLY_FLOPS)] if direct else [])
    own, gots = [x], [x_got, swap(send, "tensor", bit)]
    while bit > 1:
        bit //= 2
        keep, own = fold(rank, keep, own, gots, early)
        gots = [swap(part, "tensor", bit) for part in own]
    ids_row = query_ids[None, :]
    if direct:
        split = max(1, data_size // 2)
        soon = outer(own, gots, keep, mask, cap, 0, split)
        rows = [shift(block, "dp", k) for k, block in enumerate(soon, 1)]
        *sent, kept = outer(own, gots, keep, mask, cap, split, data_size - split)
        sent[-1] = after(sent[-1], [mate, *passed])
        rows = [kept, *rows, *(shift(block, "dp", k) for k, block in enumerate(sent, 1 + split))]
        store = place(rows)
        late = [token(rows[2:-1], LATE_FLOPS)]
        pool = pool_halves([*pieces, mate, *passed])
        gaps = [*gaps, *(g ^ 1 for g in gaps)]
        early = score_early(ids_row, pool, rows[:2], gaps)
        scores = score(ids_row, pool, early, rows[2:], gaps, True, late)
    else:
        blocks = outer(own, gots, keep, mask, cap, 0, data_size)
        store = lax.all_to_all(jnp.stack(blocks), "dp", 0, 0, tiled=True).reshape(-1, width * rank)
        pool = pool_halves(pieces)
        scores = score(ids_row, pool, ids_row, [store], gaps, False, [])
    bit = 1
    while bit < tensor_size:
        scores = scores + swap(scores, "tensor", bit)
        bit *= 2
    return store, scores * (1.0 / (rank * rank))


def solution(mesh):
    return jax.shard_map(
        local,
        mesh=mesh,
        in_specs=(
            P(("groups", "dp"), "tensor"),
            P(("groups", "dp"), "tensor"),
            P("tensor", None),
            P("tensor", None),
            P(("groups", "dp"), None),
            P(("groups", "dp"), None),
            P(("groups", "dp"), "tensor"),
            P("groups"),
        ),
        out_specs=(P(("groups", "dp"), "tensor"), P(("groups", "dp"), None)),
        check_vma=False,
    )
```

```python
import functools

import jax
import jax.numpy as jnp
from jax import lax
from jax.experimental import pallas as pl
from jax.experimental.pallas import tpu as pltpu
from jax.sharding import PartitionSpec as P

F32 = jnp.float32
BF16 = jnp.bfloat16
MIB = 1024 * 1024
NT = (((1,), (1,)), ((), ()))
MOST_DIRECT = 8
GROUP = 8
ROWS = 16
LANES = 128
FIRST_FLOPS = 10 * 10**8
X_FLOPS = 6 * 10**8
MASK_FLOPS = 2 * 10**8
EARLY_FLOPS = 3 * 10**8
LATE_FLOPS = 10**8
SCORE_FLOPS = 0


def params(mib):
    return pltpu.CompilerParams(vmem_limit_bytes=mib * MIB)


def cost(flops, nbytes):
    return pl.CostEstimate(flops=flops, bytes_accessed=nbytes, transcendentals=0)


def halves(x):
    high = x.astype(BF16)
    return high, (x - high.astype(F32)).astype(BF16)


def mm(a, b, dims=(((1,), (0,)), ((), ()))):
    return lax.dot_general(a, b, dims, preferred_element_type=F32)


def slot_mask(owners, relative, cap, lengths, owner, slots, tokens):
    docs = lengths.shape[1]
    row = lax.broadcasted_iota(jnp.int32, (docs, docs), 0)
    col = lax.broadcasted_iota(jnp.int32, (docs, docs), 1)
    len_row = lengths.astype(F32)
    place_row = lax.rem(owner - lax.axis_index("dp") + 2 * owners - 1, owners) if relative else owner
    own_row = place_row.astype(F32)

    def column(values):
        return jnp.sum(jnp.where(row == col, values, 0.0), axis=1, keepdims=True)

    ends = jnp.sum(jnp.where(row <= col, column(len_row), 0.0), axis=0, keepdims=True)
    rank = jnp.sum(
        jnp.where((row < col) & (column(own_row) == own_row), 1.0, 0.0), axis=0, keepdims=True
    )
    slot = lax.broadcasted_iota(jnp.int32, (slots, docs), 0).astype(F32)
    hot = slot == own_row * cap + rank
    first = jnp.sum(jnp.where(hot, ends - len_row, 0.0), axis=1, keepdims=True)
    last = jnp.sum(jnp.where(hot, ends, 0.0), axis=1, keepdims=True)
    token = lax.broadcasted_iota(jnp.int32, (slots, tokens), 1).astype(F32)
    return jnp.where((token >= first) & (token < last), 1.0, 0.0).astype(BF16)


def mask_kernel(owners, relative, cap, lengths_ref, owner_ref, mask_ref):
    mask_ref[...] = slot_mask(owners, relative, cap, lengths_ref[...], owner_ref[...], *mask_ref.shape)


def dispatch_mask(lengths, owner_row, owners, cap, tokens, relative):
    return pl.pallas_call(
        functools.partial(mask_kernel, owners, relative, cap),
        out_shape=jax.ShapeDtypeStruct((owners * cap, tokens), BF16),
        compiler_params=params(8),
        cost_estimate=cost(MASK_FLOPS, 0),
    )(lengths, owner_row)


def put_projection(out_ref, proj_ref, act_ref):
    half = act_ref.shape[0] // 2
    out_ref[:, :half] = mm(proj_ref[...], act_ref[:half, :], NT)
    out_ref[:, half:] = mm(act_ref[half:, :], proj_ref[...], NT).T


def x_kernel(act_ref, proj_ref, *refs):
    put_projection(refs[-1], proj_ref, act_ref)


def project_x(act, in_t, tokens):
    return pl.pallas_call(
        x_kernel,
        in_specs=[pl.BlockSpec(memory_space=pltpu.VMEM)] * 2
        + [pl.BlockSpec(memory_space=pl.ANY)] * len(tokens),
        out_shape=jax.ShapeDtypeStruct((in_t.shape[0], act.shape[0]), F32),
        compiler_params=params(8),
        cost_estimate=cost(X_FLOPS, 0),
    )(act, in_t, *tokens)


def g_kernel(width, grad_ref, proj_ref, keep_ref, send_ref, full):
    put_projection(full, proj_ref, grad_ref)
    me = lax.axis_index("tensor")
    count = full.shape[0] // width
    for apart in range(count):
        block = pl.ds(pl.multiple_of((me ^ apart) * width, width), width)
        ref, spot = (keep_ref, apart) if apart < count // 2 else (send_ref, apart - count // 2)
        ref[spot * width : (spot + 1) * width, :] = full[block, :]


def project_g(grad, out_t, width):
    tokens, rank = grad.shape[0], out_t.shape[0]
    part = jax.ShapeDtypeStruct((rank // 2, tokens), F32)
    return pl.pallas_call(
        functools.partial(g_kernel, width),
        out_shape=[part, part],
        scratch_shapes=[pltpu.VMEM((rank, tokens), F32)],
        compiler_params=params(24),
        cost_estimate=cost(0, 0),
    )(grad, out_t)


def stack(refs):
    return jnp.concatenate([r[...] for r in refs], axis=0)


def fold_kernel(rank, owned, came, keep_ref, *refs):
    first_ref, second_ref, kept_ref = refs[-3:]
    got = stack(refs[owned : owned + came])
    total = keep_ref[...] + got[rank:]
    kept = kept_ref.shape[0]
    kept_ref[...] = total[:kept]
    x = stack(refs[:owned])[:rank] + got[:rank]
    sent = jnp.concatenate([x, total[kept:]], axis=0)
    cut = first_ref.shape[0]
    first_ref[...] = sent[:cut]
    second_ref[...] = sent[cut:]


def fold(rank, keep, own, gots, pieces):
    tokens = keep.shape[1]
    kept = keep.shape[0] // 2
    cut = (rank + kept) // 16 * 8
    *sent, keep = pl.pallas_call(
        functools.partial(fold_kernel, rank, len(own), len(gots)),
        in_specs=[pl.BlockSpec(memory_space=pltpu.VMEM)] * (1 + len(own) + len(gots))
        + [pl.BlockSpec(memory_space=pl.ANY)] * len(pieces),
        out_shape=[
            jax.ShapeDtypeStruct((rows, tokens), F32) for rows in (cut, rank + kept - cut, kept)
        ],
        compiler_params=params(16),
        cost_estimate=cost(0, 0),
    )(keep, *own, *gots, *pieces)
    return keep, sent


def outer_kernel(first, owners, sent, g_ref, mask_ref, *refs):
    blocks = refs[-owners:]
    width = g_ref.shape[0]
    own, got = stack(refs[:sent]), stack(refs[sent : 2 * sent])
    rank = got.shape[0] - width
    x_full = own[:rank] + got[:rank]
    g_full = g_ref[...] + got[rank:]
    x_both = jnp.concatenate(halves(x_full), axis=0)
    g_high = g_full.astype(BF16).astype(F32)
    g_low = g_full - g_high
    cap = blocks[0].shape[0]
    slots = owners * cap
    mask = mask_ref[first * cap : first * cap + slots, :]
    tokens = mask.shape[1]

    def masked(row):
        wide = jnp.broadcast_to(row, (ROWS, tokens)).astype(BF16)
        return [mask[i : i + ROWS] * wide for i in range(0, slots, ROWS)]

    group = min(width, GROUP)
    for i in range(0, width, group):
        rows = [m for j in range(i, i + group) for g in (g_high, g_low) for m in masked(g[j : j + 1])]
        both = mm(jnp.concatenate(rows, axis=0), x_both, NT)
        columns = []
        for j in range(group):
            high = both[2 * j * slots : (2 * j + 1) * slots]
            low = both[(2 * j + 1) * slots : (2 * j + 2) * slots]
            columns.append(high[:, :rank] + high[:, rank:] + low[:, :rank])
        out = jnp.concatenate(columns, axis=1)
        for k, block in enumerate(blocks):
            block[:, i * rank : (i + group) * rank] = out[k * cap : (k + 1) * cap, :]


def outer(sent, gots, g, mask, cap, first, owners):
    width = g.shape[0]
    rank = sum(p.shape[0] for p in sent) - width
    return pl.pallas_call(
        functools.partial(outer_kernel, first, owners, len(sent)),
        out_shape=[jax.ShapeDtypeStruct((cap, width * rank), F32)] * owners,
        compiler_params=params(24),
        cost_estimate=cost(8 * owners * cap * width * mask.shape[1] * rank, 0),
    )(g, mask, *sent, *gots)


def token_kernel(*refs):
    refs[-1][...] = jnp.zeros_like(refs[-1])


def token(arrays, flops):
    return pl.pallas_call(
        token_kernel,
        in_specs=[pl.BlockSpec(memory_space=pl.ANY)] * len(arrays),
        out_shape=jax.ShapeDtypeStruct((8, 128), F32),
        compiler_params=params(4),
        cost_estimate=cost(flops, 0),
    )(*arrays)


def after_kernel(block_ref, *refs):
    refs[-1][...] = block_ref[...]


def after(block, pieces):
    return pl.pallas_call(
        after_kernel,
        in_specs=[pl.BlockSpec(memory_space=pltpu.VMEM)]
        + [pl.BlockSpec(memory_space=pl.ANY)] * len(pieces),
        out_shape=jax.ShapeDtypeStruct(block.shape, F32),
        compiler_params=params(4),
        cost_estimate=cost(0, 0),
    )(block, *pieces)


def pool_kernel(*refs):
    refs[-1][...] = jnp.concatenate(halves(stack(refs[:-1])), axis=0)


def pool_halves(pieces):
    rows, feats = sum(piece.shape[0] for piece in pieces), pieces[0].shape[1]
    return pl.pallas_call(
        pool_kernel,
        out_shape=jax.ShapeDtypeStruct((2 * rows, feats), BF16),
        compiler_params=params(16),
        cost_estimate=cost(0, 0),
    )(*pieces)


def scores_of(rows, ids, pool, gaps):
    me = lax.axis_index("dp")
    high, low = halves(rows)
    slots, split, queries = rows.shape[0], pool.shape[0] // 2, ids.shape[1]
    products = mm(jnp.concatenate([high, low], axis=0), pool, NT)
    part = products[:slots, :split] + products[:slots, split:] + products[slots:, :split]
    held = split // len(gaps)
    if split == LANES and queries == LANES and len(gaps) > 1:
        spot = lax.rem(ids, held)
        for place, gap in enumerate(gaps):
            spot = spot + jnp.where(lax.div(ids, held) == (me ^ gap), place * held, 0)
        return jnp.take_along_axis(part, jnp.broadcast_to(spot, part.shape), axis=1)
    row = lax.broadcasted_iota(jnp.int32, (held, queries), 0)
    places = [row + ((me ^ gap) * held if len(gaps) > 1 else 0) for gap in gaps]
    hot = (jnp.concatenate(places, axis=0) == ids).astype(F32).astype(BF16)
    top, rest = halves(part)
    last = (part - top.astype(F32) - rest.astype(F32)).astype(BF16)
    picked = mm(jnp.concatenate([top, rest, last], axis=0), hot)
    return picked[:slots] + picked[slots : 2 * slots] + picked[2 * slots :]


def early_kernel(gaps, ids_ref, pool_ref, *refs):
    refs[-1][...] = scores_of(stack(refs[:-1]), ids_ref[...], pool_ref[...], gaps)


def score_early(ids_row, pool, rows, gaps):
    slots = sum(row.shape[0] for row in rows)
    return pl.pallas_call(
        functools.partial(early_kernel, gaps),
        out_shape=jax.ShapeDtypeStruct((slots, ids_row.shape[1]), F32),
        compiler_params=params(16),
        cost_estimate=cost(SCORE_FLOPS, 0),
    )(ids_row, pool, *rows)


def score_kernel(count, gaps, relative, ids_ref, pool_ref, early_ref, *refs):
    rows, scores_ref = refs[:count], refs[-1]
    me = lax.axis_index("dp")
    cap = rows[0].shape[0]
    total = scores_of(stack(rows), ids_ref[...], pool_ref[...], gaps)
    done = early_ref.shape[0] // cap if relative else 0
    for k in range(done + count):
        part = early_ref if k < done else total
        at = (k if k < done else k - done) * cap
        source = lax.rem(me - k + done + count, done + count) if relative else k
        scores_ref[pl.ds(pl.multiple_of(source * cap, cap), cap), :] = part[at : at + cap, :]


def score(ids_row, pool, early, rows, gaps, relative, tokens):
    slots = sum(row.shape[0] for row in rows) + (early.shape[0] if relative else 0)
    queries = ids_row.shape[1]
    return pl.pallas_call(
        functools.partial(score_kernel, len(rows), gaps, relative),
        in_specs=[pl.BlockSpec(memory_space=pltpu.VMEM)] * (3 + len(rows))
        + [pl.BlockSpec(memory_space=pl.ANY)] * len(tokens),
        out_shape=jax.ShapeDtypeStruct((slots, queries), F32),
        compiler_params=params(24),
        cost_estimate=cost(0, 0),
    )(ids_row, pool, early, *rows, *tokens)


def place_kernel(*refs):
    rows, store_ref = refs[:-1], refs[-1]
    me = lax.axis_index("dp")
    cap = rows[0].shape[0]
    for k, row in enumerate(rows):
        source = lax.rem(me - k + len(rows), len(rows))
        store_ref[pl.ds(pl.multiple_of(source * cap, cap), cap), :] = row[...]


def place(rows):
    slots, feats = rows[0].shape[0] * len(rows), rows[0].shape[1]
    return pl.pallas_call(
        place_kernel,
        out_shape=jax.ShapeDtypeStruct((slots, feats), F32),
        compiler_params=params(16),
        cost_estimate=cost(0, 8 * slots * feats),
    )(*rows)


def swap(x, axis, gap):
    return lax.ppermute(x, axis, [(i, i ^ gap) for i in range(lax.axis_size(axis))])


def shift(x, axis, by):
    size = lax.axis_size(axis)
    return lax.ppermute(x, axis, [(i, (i + by) % size) for i in range(size)])


def gather_pieces(piece):
    pieces, gaps = [piece], [0]
    bit = lax.axis_size("dp") // 2
    while bit > 1:
        pieces, gaps = pieces + [swap(p, "dp", bit) for p in pieces], gaps + [g ^ bit for g in gaps]
        bit //= 2
    return pieces, gaps


def local(
    activations, out_grads, proj_in, proj_out, doc_lengths, doc_owner, query_grads, query_ids
):
    tensor_size = lax.axis_size("tensor")
    data_size = lax.axis_size("dp")
    tokens = activations.shape[0]
    rank = proj_in.shape[1]
    width = rank // tensor_size
    docs = doc_owner.shape[0]
    cap = max(2, 2 * docs // data_size)
    direct = data_size <= MOST_DIRECT

    if direct:
        pieces, gaps = gather_pieces(query_grads)
        mate = swap(query_grads, "dp", 1)
        passed = [swap(piece, "dp", 1) for piece in pieces[1:]]
    else:
        pieces, gaps = [lax.all_gather(query_grads, "dp", axis=0, tiled=True)], [0]

    mask = dispatch_mask(doc_lengths, doc_owner.T, data_size, cap, activations.shape[0], direct)
    x = project_x(activations, proj_in.T, [token([], FIRST_FLOPS)])
    bit = tensor_size // 2
    x_got = swap(x, "tensor", bit)
    keep, send = project_g(out_grads, proj_out.T, width)
    early = [mask] + ([token(pieces[1:], EARLY_FLOPS)] if direct else [])
    own, gots = [x], [x_got, swap(send, "tensor", bit)]
    while bit > 1:
        bit //= 2
        keep, own = fold(rank, keep, own, gots, early)
        gots = [swap(part, "tensor", bit) for part in own]
    ids_row = query_ids[None, :]
    if direct:
        split = max(1, data_size // 2)
        soon = outer(own, gots, keep, mask, cap, 0, split)
        rows = [shift(block, "dp", k) for k, block in enumerate(soon, 1)]
        *sent, kept = outer(own, gots, keep, mask, cap, split, data_size - split)
        sent[-1] = after(sent[-1], [mate, *passed])
        rows = [kept, *rows, *(shift(block, "dp", k) for k, block in enumerate(sent, 1 + split))]
        store = place(rows)
        late = [token(rows[2:-1], LATE_FLOPS)]
        pool = pool_halves([*pieces, mate, *passed])
        gaps = [*gaps, *(g ^ 1 for g in gaps)]
        early = score_early(ids_row, pool, rows[:2], gaps)
        scores = score(ids_row, pool, early, rows[2:], gaps, True, late)
    else:
        blocks = outer(own, gots, keep, mask, cap, 0, data_size)
        store = lax.all_to_all(jnp.stack(blocks), "dp", 0, 0, tiled=True).reshape(-1, width * rank)
        pool = pool_halves(pieces)
        scores = score(ids_row, pool, ids_row, [store], gaps, False, [])
    bit = 1
    while bit < tensor_size:
        scores = scores + swap(scores, "tensor", bit)
        bit *= 2
    return store, scores * (1.0 / (rank * rank))


def solution(mesh):
    return jax.shard_map(
        local,
        mesh=mesh,
        in_specs=(
            P(("groups", "dp"), "tensor"),
            P(("groups", "dp"), "tensor"),
            P("tensor", None),
            P("tensor", None),
            P(("groups", "dp"), None),
            P(("groups", "dp"), None),
            P(("groups", "dp"), "tensor"),
            P("groups"),
        ),
        out_specs=(P(("groups", "dp"), "tensor"), P(("groups", "dp"), None)),
        check_vma=False,
    )
```

```python
import functools

import jax
import jax.numpy as jnp
from jax import lax
from jax.experimental import pallas as pl
from jax.experimental.pallas import tpu as pltpu
from jax.sharding import PartitionSpec as P

F32 = jnp.float32
BF16 = jnp.bfloat16
MIB = 1024 * 1024
NT = (((1,), (1,)), ((), ()))
MOST_DIRECT = 8
GROUP = 8
ROWS = 16
LANES = 128
FIRST_FLOPS = 10 * 10**8
X_FLOPS = 6 * 10**8
MASK_FLOPS = 2 * 10**8
EARLY_FLOPS = 3 * 10**8
LATE_FLOPS = 10**8
SCORE_FLOPS = 0


def params(mib):
    return pltpu.CompilerParams(vmem_limit_bytes=mib * MIB)


def cost(flops, nbytes):
    return pl.CostEstimate(flops=flops, bytes_accessed=nbytes, transcendentals=0)


def halves(x):
    high = x.astype(BF16)
    return high, (x - high.astype(F32)).astype(BF16)


def mm(a, b, dims=(((1,), (0,)), ((), ()))):
    return lax.dot_general(a, b, dims, preferred_element_type=F32)


def slot_mask(owners, relative, cap, lengths, owner, slots, tokens):
    docs = lengths.shape[1]
    row = lax.broadcasted_iota(jnp.int32, (docs, docs), 0)
    col = lax.broadcasted_iota(jnp.int32, (docs, docs), 1)
    len_row = lengths.astype(F32)
    place_row = lax.rem(owner - lax.axis_index("dp") + 2 * owners - 1, owners) if relative else owner
    own_row = place_row.astype(F32)

    def column(values):
        return jnp.sum(jnp.where(row == col, values, 0.0), axis=1, keepdims=True)

    ends = jnp.sum(jnp.where(row <= col, column(len_row), 0.0), axis=0, keepdims=True)
    rank = jnp.sum(
        jnp.where((row < col) & (column(own_row) == own_row), 1.0, 0.0), axis=0, keepdims=True
    )
    slot = lax.broadcasted_iota(jnp.int32, (slots, docs), 0).astype(F32)
    hot = slot == own_row * cap + rank
    first = jnp.sum(jnp.where(hot, ends - len_row, 0.0), axis=1, keepdims=True)
    last = jnp.sum(jnp.where(hot, ends, 0.0), axis=1, keepdims=True)
    token = lax.broadcasted_iota(jnp.int32, (slots, tokens), 1).astype(F32)
    return jnp.where((token >= first) & (token < last), 1.0, 0.0).astype(BF16)


def mask_kernel(owners, relative, cap, lengths_ref, owner_ref, mask_ref):
    mask_ref[...] = slot_mask(owners, relative, cap, lengths_ref[...], owner_ref[...], *mask_ref.shape)


def dispatch_mask(lengths, owner_row, owners, cap, tokens, relative):
    return pl.pallas_call(
        functools.partial(mask_kernel, owners, relative, cap),
        out_shape=jax.ShapeDtypeStruct((owners * cap, tokens), BF16),
        compiler_params=params(8),
        cost_estimate=cost(MASK_FLOPS, 0),
    )(lengths, owner_row)


def put_projection(out_ref, proj_ref, act_ref):
    half = act_ref.shape[0] // 2
    out_ref[:, :half] = mm(proj_ref[...], act_ref[:half, :], NT)
    out_ref[:, half:] = mm(act_ref[half:, :], proj_ref[...], NT).T


def x_kernel(act_ref, proj_ref, *refs):
    put_projection(refs[-1], proj_ref, act_ref)


def project_x(act, in_t, tokens):
    return pl.pallas_call(
        x_kernel,
        in_specs=[pl.BlockSpec(memory_space=pltpu.VMEM)] * 2
        + [pl.BlockSpec(memory_space=pl.ANY)] * len(tokens),
        out_shape=jax.ShapeDtypeStruct((in_t.shape[0], act.shape[0]), F32),
        compiler_params=params(8),
        cost_estimate=cost(X_FLOPS, 0),
    )(act, in_t, *tokens)


def g_kernel(width, grad_ref, proj_ref, keep_ref, send_ref, full):
    put_projection(full, proj_ref, grad_ref)
    me = lax.axis_index("tensor")
    count = full.shape[0] // width
    for apart in range(count):
        block = pl.ds(pl.multiple_of((me ^ apart) * width, width), width)
        ref, spot = (keep_ref, apart) if apart < count // 2 else (send_ref, apart - count // 2)
        ref[spot * width : (spot + 1) * width, :] = full[block, :]


def project_g(grad, out_t, width):
    tokens, rank = grad.shape[0], out_t.shape[0]
    part = jax.ShapeDtypeStruct((rank // 2, tokens), F32)
    return pl.pallas_call(
        functools.partial(g_kernel, width),
        out_shape=[part, part],
        scratch_shapes=[pltpu.VMEM((rank, tokens), F32)],
        compiler_params=params(24),
        cost_estimate=cost(0, 0),
    )(grad, out_t)


def stack(refs):
    return jnp.concatenate([r[...] for r in refs], axis=0)


def fold_kernel(rank, owned, came, keep_ref, *refs):
    first_ref, second_ref, kept_ref = refs[-3:]
    got = stack(refs[owned : owned + came])
    total = keep_ref[...] + got[rank:]
    kept = kept_ref.shape[0]
    kept_ref[...] = total[:kept]
    x = stack(refs[:owned])[:rank] + got[:rank]
    sent = jnp.concatenate([x, total[kept:]], axis=0)
    cut = first_ref.shape[0]
    first_ref[...] = sent[:cut]
    second_ref[...] = sent[cut:]


def fold(rank, keep, own, gots, pieces):
    tokens = keep.shape[1]
    kept = keep.shape[0] // 2
    cut = (rank + kept) // 16 * 8
    *sent, keep = pl.pallas_call(
        functools.partial(fold_kernel, rank, len(own), len(gots)),
        in_specs=[pl.BlockSpec(memory_space=pltpu.VMEM)] * (1 + len(own) + len(gots))
        + [pl.BlockSpec(memory_space=pl.ANY)] * len(pieces),
        out_shape=[
            jax.ShapeDtypeStruct((rows, tokens), F32) for rows in (cut, rank + kept - cut, kept)
        ],
        compiler_params=params(16),
        cost_estimate=cost(0, 0),
    )(keep, *own, *gots, *pieces)
    return keep, sent


def outer_kernel(first, owners, sent, g_ref, mask_ref, *refs):
    blocks = refs[-owners:]
    width = g_ref.shape[0]
    own, got = stack(refs[:sent]), stack(refs[sent : 2 * sent])
    rank = got.shape[0] - width
    x_full = own[:rank] + got[:rank]
    g_full = g_ref[...] + got[rank:]
    x_high, x_low = halves(x_full)
    x_both = jnp.concatenate(
        [
            jnp.concatenate([x_high, x_high], axis=1),
            jnp.concatenate([x_low, jnp.zeros_like(x_low)], axis=1),
        ],
        axis=0,
    )
    g_high = g_full.astype(BF16).astype(F32)
    g_low = g_full - g_high
    cap = blocks[0].shape[0]
    slots = owners * cap
    mask = mask_ref[first * cap : first * cap + slots, :]
    tokens = mask.shape[1]

    def masked(row):
        wide = jnp.broadcast_to(row, (ROWS, tokens)).astype(BF16)
        return [mask[i : i + ROWS] * wide for i in range(0, slots, ROWS)]

    group = min(width, GROUP)
    for i in range(0, width, group):
        rows = [
            jnp.concatenate([m for j in range(i, i + group) for m in masked(g[j : j + 1])], axis=0)
            for g in (g_high, g_low)
        ]
        both = mm(jnp.concatenate(rows, axis=1), x_both, NT)
        columns = []
        for j in range(group):
            part = both[j * slots : (j + 1) * slots]
            columns.append(part[:, :rank] + part[:, rank:])
        out = jnp.concatenate(columns, axis=1)
        for k, block in enumerate(blocks):
            block[:, i * rank : (i + group) * rank] = out[k * cap : (k + 1) * cap, :]


def outer(sent, gots, g, mask, cap, first, owners):
    width = g.shape[0]
    rank = sum(p.shape[0] for p in sent) - width
    return pl.pallas_call(
        functools.partial(outer_kernel, first, owners, len(sent)),
        out_shape=[jax.ShapeDtypeStruct((cap, width * rank), F32)] * owners,
        compiler_params=params(24),
        cost_estimate=cost(8 * owners * cap * width * mask.shape[1] * rank, 0),
    )(g, mask, *sent, *gots)


def token_kernel(*refs):
    refs[-1][...] = jnp.zeros_like(refs[-1])


def token(arrays, flops):
    return pl.pallas_call(
        token_kernel,
        in_specs=[pl.BlockSpec(memory_space=pl.ANY)] * len(arrays),
        out_shape=jax.ShapeDtypeStruct((8, 128), F32),
        compiler_params=params(4),
        cost_estimate=cost(flops, 0),
    )(*arrays)


def after_kernel(block_ref, *refs):
    refs[-1][...] = block_ref[...]


def after(block, pieces):
    return pl.pallas_call(
        after_kernel,
        in_specs=[pl.BlockSpec(memory_space=pltpu.VMEM)]
        + [pl.BlockSpec(memory_space=pl.ANY)] * len(pieces),
        out_shape=jax.ShapeDtypeStruct(block.shape, F32),
        compiler_params=params(4),
        cost_estimate=cost(0, 0),
    )(block, *pieces)


def pool_kernel(*refs):
    refs[-1][...] = jnp.concatenate(halves(stack(refs[:-1])), axis=0)


def pool_halves(pieces):
    rows, feats = sum(piece.shape[0] for piece in pieces), pieces[0].shape[1]
    return pl.pallas_call(
        pool_kernel,
        out_shape=jax.ShapeDtypeStruct((2 * rows, feats), BF16),
        compiler_params=params(16),
        cost_estimate=cost(0, 0),
    )(*pieces)


def scores_of(rows, ids, pool, gaps):
    me = lax.axis_index("dp")
    high, low = halves(rows)
    slots, split, queries = rows.shape[0], pool.shape[0] // 2, ids.shape[1]
    products = mm(jnp.concatenate([high, low], axis=0), pool, NT)
    part = products[:slots, :split] + products[:slots, split:] + products[slots:, :split]
    held = split // len(gaps)
    if split == LANES and queries == LANES and len(gaps) > 1:
        spot = lax.rem(ids, held)
        for place, gap in enumerate(gaps):
            spot = spot + jnp.where(lax.div(ids, held) == (me ^ gap), place * held, 0)
        return jnp.take_along_axis(part, jnp.broadcast_to(spot, part.shape), axis=1)
    row = lax.broadcasted_iota(jnp.int32, (held, queries), 0)
    places = [row + ((me ^ gap) * held if len(gaps) > 1 else 0) for gap in gaps]
    hot = (jnp.concatenate(places, axis=0) == ids).astype(F32).astype(BF16)
    top, rest = halves(part)
    last = (part - top.astype(F32) - rest.astype(F32)).astype(BF16)
    picked = mm(jnp.concatenate([top, rest, last], axis=0), hot)
    return picked[:slots] + picked[slots : 2 * slots] + picked[2 * slots :]


def early_kernel(gaps, ids_ref, pool_ref, *refs):
    refs[-1][...] = scores_of(stack(refs[:-1]), ids_ref[...], pool_ref[...], gaps)


def score_early(ids_row, pool, rows, gaps):
    slots = sum(row.shape[0] for row in rows)
    return pl.pallas_call(
        functools.partial(early_kernel, gaps),
        out_shape=jax.ShapeDtypeStruct((slots, ids_row.shape[1]), F32),
        compiler_params=params(16),
        cost_estimate=cost(SCORE_FLOPS, 0),
    )(ids_row, pool, *rows)


def score_kernel(count, gaps, relative, ids_ref, pool_ref, early_ref, *refs):
    rows, scores_ref = refs[:count], refs[-1]
    me = lax.axis_index("dp")
    cap = rows[0].shape[0]
    total = scores_of(stack(rows), ids_ref[...], pool_ref[...], gaps)
    done = early_ref.shape[0] // cap if relative else 0
    for k in range(done + count):
        part = early_ref if k < done else total
        at = (k if k < done else k - done) * cap
        source = lax.rem(me - k + done + count, done + count) if relative else k
        scores_ref[pl.ds(pl.multiple_of(source * cap, cap), cap), :] = part[at : at + cap, :]


def score(ids_row, pool, early, rows, gaps, relative, tokens):
    slots = sum(row.shape[0] for row in rows) + (early.shape[0] if relative else 0)
    queries = ids_row.shape[1]
    return pl.pallas_call(
        functools.partial(score_kernel, len(rows), gaps, relative),
        in_specs=[pl.BlockSpec(memory_space=pltpu.VMEM)] * (3 + len(rows))
        + [pl.BlockSpec(memory_space=pl.ANY)] * len(tokens),
        out_shape=jax.ShapeDtypeStruct((slots, queries), F32),
        compiler_params=params(24),
        cost_estimate=cost(0, 0),
    )(ids_row, pool, early, *rows, *tokens)


def place_kernel(*refs):
    rows, store_ref = refs[:-1], refs[-1]
    me = lax.axis_index("dp")
    cap = rows[0].shape[0]
    for k, row in enumerate(rows):
        source = lax.rem(me - k + len(rows), len(rows))
        store_ref[pl.ds(pl.multiple_of(source * cap, cap), cap), :] = row[...]


def place(rows):
    slots, feats = rows[0].shape[0] * len(rows), rows[0].shape[1]
    return pl.pallas_call(
        place_kernel,
        out_shape=jax.ShapeDtypeStruct((slots, feats), F32),
        compiler_params=params(16),
        cost_estimate=cost(0, 8 * slots * feats),
    )(*rows)


def swap(x, axis, gap):
    return lax.ppermute(x, axis, [(i, i ^ gap) for i in range(lax.axis_size(axis))])


def shift(x, axis, by):
    size = lax.axis_size(axis)
    return lax.ppermute(x, axis, [(i, (i + by) % size) for i in range(size)])


def gather_pieces(piece):
    pieces, gaps = [piece], [0]
    bit = lax.axis_size("dp") // 2
    while bit > 1:
        pieces, gaps = pieces + [swap(p, "dp", bit) for p in pieces], gaps + [g ^ bit for g in gaps]
        bit //= 2
    return pieces, gaps


def local(
    activations, out_grads, proj_in, proj_out, doc_lengths, doc_owner, query_grads, query_ids
):
    tensor_size = lax.axis_size("tensor")
    data_size = lax.axis_size("dp")
    tokens = activations.shape[0]
    rank = proj_in.shape[1]
    width = rank // tensor_size
    docs = doc_owner.shape[0]
    cap = max(2, 2 * docs // data_size)
    direct = data_size <= MOST_DIRECT

    if direct:
        pieces, gaps = gather_pieces(query_grads)
        mate = swap(query_grads, "dp", 1)
        passed = [swap(piece, "dp", 1) for piece in pieces[1:]]
    else:
        pieces, gaps = [lax.all_gather(query_grads, "dp", axis=0, tiled=True)], [0]

    mask = dispatch_mask(doc_lengths, doc_owner.T, data_size, cap, activations.shape[0], direct)
    x = project_x(activations, proj_in.T, [token([], FIRST_FLOPS)])
    bit = tensor_size // 2
    x_got = swap(x, "tensor", bit)
    keep, send = project_g(out_grads, proj_out.T, width)
    early = [mask] + ([token(pieces[1:], EARLY_FLOPS)] if direct else [])
    own, gots = [x], [x_got, swap(send, "tensor", bit)]
    while bit > 1:
        bit //= 2
        keep, own = fold(rank, keep, own, gots, early)
        gots = [swap(part, "tensor", bit) for part in own]
    ids_row = query_ids[None, :]
    if direct:
        split = max(1, data_size // 2)
        soon = outer(own, gots, keep, mask, cap, 0, split)
        rows = [shift(block, "dp", k) for k, block in enumerate(soon, 1)]
        *sent, kept = outer(own, gots, keep, mask, cap, split, data_size - split)
        sent[-1] = after(sent[-1], [mate, *passed])
        rows = [kept, *rows, *(shift(block, "dp", k) for k, block in enumerate(sent, 1 + split))]
        store = place(rows)
        late = [token(rows[2:-1], LATE_FLOPS)]
        pool = pool_halves([*pieces, mate, *passed])
        gaps = [*gaps, *(g ^ 1 for g in gaps)]
        early = score_early(ids_row, pool, rows[:2], gaps)
        scores = score(ids_row, pool, early, rows[2:], gaps, True, late)
    else:
        blocks = outer(own, gots, keep, mask, cap, 0, data_size)
        store = lax.all_to_all(jnp.stack(blocks), "dp", 0, 0, tiled=True).reshape(-1, width * rank)
        pool = pool_halves(pieces)
        scores = score(ids_row, pool, ids_row, [store], gaps, False, [])
    bit = 1
    while bit < tensor_size:
        scores = scores + swap(scores, "tensor", bit)
        bit *= 2
    return store, scores * (1.0 / (rank * rank))


def solution(mesh):
    return jax.shard_map(
        local,
        mesh=mesh,
        in_specs=(
            P(("groups", "dp"), "tensor"),
            P(("groups", "dp"), "tensor"),
            P("tensor", None),
            P("tensor", None),
            P(("groups", "dp"), None),
            P(("groups", "dp"), None),
            P(("groups", "dp"), "tensor"),
            P("groups"),
        ),
        out_specs=(P(("groups", "dp"), "tensor"), P(("groups", "dp"), None)),
        check_vma=False,
    )
```

```python
import functools

import jax
import jax.numpy as jnp
from jax import lax
from jax.experimental import pallas as pl
from jax.experimental.pallas import tpu as pltpu
from jax.sharding import PartitionSpec as P

F32 = jnp.float32
BF16 = jnp.bfloat16
MIB = 1024 * 1024
NT = (((1,), (1,)), ((), ()))
MOST_DIRECT = 8
GROUP = 16
ROWS = 16
LANES = 128
FIRST_FLOPS = 10 * 10**8
X_FLOPS = 6 * 10**8
MASK_FLOPS = 2 * 10**8
EARLY_FLOPS = 3 * 10**8
LATE_FLOPS = 10**8
SCORE_FLOPS = 0


def params(mib):
    return pltpu.CompilerParams(vmem_limit_bytes=mib * MIB)


def cost(flops, nbytes):
    return pl.CostEstimate(flops=flops, bytes_accessed=nbytes, transcendentals=0)


def halves(x):
    high = x.astype(BF16)
    return high, (x - high.astype(F32)).astype(BF16)


def mm(a, b, dims=(((1,), (0,)), ((), ()))):
    return lax.dot_general(a, b, dims, preferred_element_type=F32)


def slot_mask(owners, relative, cap, lengths, owner, slots, tokens):
    docs = lengths.shape[1]
    row = lax.broadcasted_iota(jnp.int32, (docs, docs), 0)
    col = lax.broadcasted_iota(jnp.int32, (docs, docs), 1)
    len_row = lengths.astype(F32)
    place_row = lax.rem(owner - lax.axis_index("dp") + 2 * owners - 1, owners) if relative else owner
    own_row = place_row.astype(F32)

    def column(values):
        return jnp.sum(jnp.where(row == col, values, 0.0), axis=1, keepdims=True)

    ends = jnp.sum(jnp.where(row <= col, column(len_row), 0.0), axis=0, keepdims=True)
    rank = jnp.sum(
        jnp.where((row < col) & (column(own_row) == own_row), 1.0, 0.0), axis=0, keepdims=True
    )
    slot = lax.broadcasted_iota(jnp.int32, (slots, docs), 0).astype(F32)
    hot = slot == own_row * cap + rank
    first = jnp.sum(jnp.where(hot, ends - len_row, 0.0), axis=1, keepdims=True)
    last = jnp.sum(jnp.where(hot, ends, 0.0), axis=1, keepdims=True)
    token = lax.broadcasted_iota(jnp.int32, (slots, tokens), 1).astype(F32)
    return jnp.where((token >= first) & (token < last), 1.0, 0.0).astype(BF16)


def mask_kernel(owners, relative, cap, lengths_ref, owner_ref, mask_ref):
    mask_ref[...] = slot_mask(owners, relative, cap, lengths_ref[...], owner_ref[...], *mask_ref.shape)


def dispatch_mask(lengths, owner_row, owners, cap, tokens, relative):
    return pl.pallas_call(
        functools.partial(mask_kernel, owners, relative, cap),
        out_shape=jax.ShapeDtypeStruct((owners * cap, tokens), BF16),
        compiler_params=params(8),
        cost_estimate=cost(MASK_FLOPS, 0),
    )(lengths, owner_row)


def put_projection(out_ref, proj_ref, act_ref):
    half = act_ref.shape[0] // 2
    out_ref[:, :half] = mm(proj_ref[...], act_ref[:half, :], NT)
    out_ref[:, half:] = mm(act_ref[half:, :], proj_ref[...], NT).T


def x_kernel(act_ref, proj_ref, *refs):
    put_projection(refs[-1], proj_ref, act_ref)


def project_x(act, in_t, tokens):
    return pl.pallas_call(
        x_kernel,
        in_specs=[pl.BlockSpec(memory_space=pltpu.VMEM)] * 2
        + [pl.BlockSpec(memory_space=pl.ANY)] * len(tokens),
        out_shape=jax.ShapeDtypeStruct((in_t.shape[0], act.shape[0]), F32),
        compiler_params=params(8),
        cost_estimate=cost(X_FLOPS, 0),
    )(act, in_t, *tokens)


def g_kernel(width, grad_ref, proj_ref, keep_ref, send_ref, full):
    put_projection(full, proj_ref, grad_ref)
    me = lax.axis_index("tensor")
    count = full.shape[0] // width
    for apart in range(count):
        block = pl.ds(pl.multiple_of((me ^ apart) * width, width), width)
        ref, spot = (keep_ref, apart) if apart < count // 2 else (send_ref, apart - count // 2)
        ref[spot * width : (spot + 1) * width, :] = full[block, :]


def project_g(grad, out_t, width):
    tokens, rank = grad.shape[0], out_t.shape[0]
    part = jax.ShapeDtypeStruct((rank // 2, tokens), F32)
    return pl.pallas_call(
        functools.partial(g_kernel, width),
        out_shape=[part, part],
        scratch_shapes=[pltpu.VMEM((rank, tokens), F32)],
        compiler_params=params(24),
        cost_estimate=cost(0, 0),
    )(grad, out_t)


def stack(refs):
    return jnp.concatenate([r[...] for r in refs], axis=0)


def fold_kernel(rank, owned, came, keep_ref, *refs):
    first_ref, second_ref, kept_ref = refs[-3:]
    got = stack(refs[owned : owned + came])
    total = keep_ref[...] + got[rank:]
    kept = kept_ref.shape[0]
    kept_ref[...] = total[:kept]
    x = stack(refs[:owned])[:rank] + got[:rank]
    sent = jnp.concatenate([x, total[kept:]], axis=0)
    cut = first_ref.shape[0]
    first_ref[...] = sent[:cut]
    second_ref[...] = sent[cut:]


def fold(rank, keep, own, gots, pieces):
    tokens = keep.shape[1]
    kept = keep.shape[0] // 2
    cut = (rank + kept) // 16 * 8
    *sent, keep = pl.pallas_call(
        functools.partial(fold_kernel, rank, len(own), len(gots)),
        in_specs=[pl.BlockSpec(memory_space=pltpu.VMEM)] * (1 + len(own) + len(gots))
        + [pl.BlockSpec(memory_space=pl.ANY)] * len(pieces),
        out_shape=[
            jax.ShapeDtypeStruct((rows, tokens), F32) for rows in (cut, rank + kept - cut, kept)
        ],
        compiler_params=params(16),
        cost_estimate=cost(0, 0),
    )(keep, *own, *gots, *pieces)
    return keep, sent


def outer_kernel(first, owners, sent, g_ref, mask_ref, *refs):
    blocks = refs[-owners:]
    width = g_ref.shape[0]
    own, got = stack(refs[:sent]), stack(refs[sent : 2 * sent])
    rank = got.shape[0] - width
    x_full = own[:rank] + got[:rank]
    g_full = g_ref[...] + got[rank:]
    x_high, x_low = halves(x_full)
    x_both = jnp.concatenate(
        [
            jnp.concatenate([x_high, x_high], axis=1),
            jnp.concatenate([x_low, jnp.zeros_like(x_low)], axis=1),
        ],
        axis=0,
    )
    g_high = g_full.astype(BF16).astype(F32)
    g_low = g_full - g_high
    cap = blocks[0].shape[0]
    slots = owners * cap
    mask = mask_ref[first * cap : first * cap + slots, :]
    tokens = mask.shape[1]

    def masked(row):
        wide = jnp.broadcast_to(row, (ROWS, tokens)).astype(BF16)
        return [mask[i : i + ROWS] * wide for i in range(0, slots, ROWS)]

    group = min(width, GROUP)
    for i in range(0, width, group):
        rows = [
            jnp.concatenate([m for j in range(i, i + group) for m in masked(g[j : j + 1])], axis=0)
            for g in (g_high, g_low)
        ]
        both = mm(jnp.concatenate(rows, axis=1), x_both, NT)
        columns = []
        for j in range(group):
            part = both[j * slots : (j + 1) * slots]
            columns.append(part[:, :rank] + part[:, rank:])
        out = jnp.concatenate(columns, axis=1)
        for k, block in enumerate(blocks):
            block[:, i * rank : (i + group) * rank] = out[k * cap : (k + 1) * cap, :]


def outer(sent, gots, g, mask, cap, first, owners):
    width = g.shape[0]
    rank = sum(p.shape[0] for p in sent) - width
    return pl.pallas_call(
        functools.partial(outer_kernel, first, owners, len(sent)),
        out_shape=[jax.ShapeDtypeStruct((cap, width * rank), F32)] * owners,
        compiler_params=params(24),
        cost_estimate=cost(8 * owners * cap * width * mask.shape[1] * rank, 0),
    )(g, mask, *sent, *gots)


def token_kernel(*refs):
    refs[-1][...] = jnp.zeros_like(refs[-1])


def token(arrays, flops):
    return pl.pallas_call(
        token_kernel,
        in_specs=[pl.BlockSpec(memory_space=pl.ANY)] * len(arrays),
        out_shape=jax.ShapeDtypeStruct((8, 128), F32),
        compiler_params=params(4),
        cost_estimate=cost(flops, 0),
    )(*arrays)


def after_kernel(block_ref, *refs):
    refs[-1][...] = block_ref[...]


def after(block, pieces):
    return pl.pallas_call(
        after_kernel,
        in_specs=[pl.BlockSpec(memory_space=pltpu.VMEM)]
        + [pl.BlockSpec(memory_space=pl.ANY)] * len(pieces),
        out_shape=jax.ShapeDtypeStruct(block.shape, F32),
        compiler_params=params(4),
        cost_estimate=cost(0, 0),
    )(block, *pieces)


def pool_kernel(*refs):
    refs[-1][...] = jnp.concatenate(halves(stack(refs[:-1])), axis=0)


def pool_halves(pieces):
    rows, feats = sum(piece.shape[0] for piece in pieces), pieces[0].shape[1]
    return pl.pallas_call(
        pool_kernel,
        out_shape=jax.ShapeDtypeStruct((2 * rows, feats), BF16),
        compiler_params=params(16),
        cost_estimate=cost(0, 0),
    )(*pieces)


def scores_of(rows, ids, pool, gaps):
    me = lax.axis_index("dp")
    high, low = halves(rows)
    slots, split, queries = rows.shape[0], pool.shape[0] // 2, ids.shape[1]
    products = mm(jnp.concatenate([high, low], axis=0), pool, NT)
    part = products[:slots, :split] + products[:slots, split:] + products[slots:, :split]
    held = split // len(gaps)
    if split == LANES and queries == LANES and len(gaps) > 1:
        spot = lax.rem(ids, held)
        for place, gap in enumerate(gaps):
            spot = spot + jnp.where(lax.div(ids, held) == (me ^ gap), place * held, 0)
        return jnp.take_along_axis(part, jnp.broadcast_to(spot, part.shape), axis=1)
    row = lax.broadcasted_iota(jnp.int32, (held, queries), 0)
    places = [row + ((me ^ gap) * held if len(gaps) > 1 else 0) for gap in gaps]
    hot = (jnp.concatenate(places, axis=0) == ids).astype(F32).astype(BF16)
    top, rest = halves(part)
    last = (part - top.astype(F32) - rest.astype(F32)).astype(BF16)
    picked = mm(jnp.concatenate([top, rest, last], axis=0), hot)
    return picked[:slots] + picked[slots : 2 * slots] + picked[2 * slots :]


def early_kernel(gaps, ids_ref, pool_ref, *refs):
    refs[-1][...] = scores_of(stack(refs[:-1]), ids_ref[...], pool_ref[...], gaps)


def score_early(ids_row, pool, rows, gaps):
    slots = sum(row.shape[0] for row in rows)
    return pl.pallas_call(
        functools.partial(early_kernel, gaps),
        out_shape=jax.ShapeDtypeStruct((slots, ids_row.shape[1]), F32),
        compiler_params=params(16),
        cost_estimate=cost(SCORE_FLOPS, 0),
    )(ids_row, pool, *rows)


def score_kernel(count, gaps, relative, ids_ref, pool_ref, early_ref, *refs):
    rows, scores_ref = refs[:count], refs[-1]
    me = lax.axis_index("dp")
    cap = rows[0].shape[0]
    total = scores_of(stack(rows), ids_ref[...], pool_ref[...], gaps)
    done = early_ref.shape[0] // cap if relative else 0
    for k in range(done + count):
        part = early_ref if k < done else total
        at = (k if k < done else k - done) * cap
        source = lax.rem(me - k + done + count, done + count) if relative else k
        scores_ref[pl.ds(pl.multiple_of(source * cap, cap), cap), :] = part[at : at + cap, :]


def score(ids_row, pool, early, rows, gaps, relative, tokens):
    slots = sum(row.shape[0] for row in rows) + (early.shape[0] if relative else 0)
    queries = ids_row.shape[1]
    return pl.pallas_call(
        functools.partial(score_kernel, len(rows), gaps, relative),
        in_specs=[pl.BlockSpec(memory_space=pltpu.VMEM)] * (3 + len(rows))
        + [pl.BlockSpec(memory_space=pl.ANY)] * len(tokens),
        out_shape=jax.ShapeDtypeStruct((slots, queries), F32),
        compiler_params=params(24),
        cost_estimate=cost(0, 0),
    )(ids_row, pool, early, *rows, *tokens)


def place_kernel(*refs):
    rows, store_ref = refs[:-1], refs[-1]
    me = lax.axis_index("dp")
    cap = rows[0].shape[0]
    for k, row in enumerate(rows):
        source = lax.rem(me - k + len(rows), len(rows))
        store_ref[pl.ds(pl.multiple_of(source * cap, cap), cap), :] = row[...]


def place(rows):
    slots, feats = rows[0].shape[0] * len(rows), rows[0].shape[1]
    return pl.pallas_call(
        place_kernel,
        out_shape=jax.ShapeDtypeStruct((slots, feats), F32),
        compiler_params=params(16),
        cost_estimate=cost(0, 8 * slots * feats),
    )(*rows)


def swap(x, axis, gap):
    return lax.ppermute(x, axis, [(i, i ^ gap) for i in range(lax.axis_size(axis))])


def shift(x, axis, by):
    size = lax.axis_size(axis)
    return lax.ppermute(x, axis, [(i, (i + by) % size) for i in range(size)])


def gather_pieces(piece):
    pieces, gaps = [piece], [0]
    bit = lax.axis_size("dp") // 2
    while bit > 1:
        pieces, gaps = pieces + [swap(p, "dp", bit) for p in pieces], gaps + [g ^ bit for g in gaps]
        bit //= 2
    return pieces, gaps


def local(
    activations, out_grads, proj_in, proj_out, doc_lengths, doc_owner, query_grads, query_ids
):
    tensor_size = lax.axis_size("tensor")
    data_size = lax.axis_size("dp")
    tokens = activations.shape[0]
    rank = proj_in.shape[1]
    width = rank // tensor_size
    docs = doc_owner.shape[0]
    cap = max(2, 2 * docs // data_size)
    direct = data_size <= MOST_DIRECT

    if direct:
        pieces, gaps = gather_pieces(query_grads)
        mate = swap(query_grads, "dp", 1)
        passed = [swap(piece, "dp", 1) for piece in pieces[1:]]
    else:
        pieces, gaps = [lax.all_gather(query_grads, "dp", axis=0, tiled=True)], [0]

    mask = dispatch_mask(doc_lengths, doc_owner.T, data_size, cap, activations.shape[0], direct)
    x = project_x(activations, proj_in.T, [token([], FIRST_FLOPS)])
    bit = tensor_size // 2
    x_got = swap(x, "tensor", bit)
    keep, send = project_g(out_grads, proj_out.T, width)
    early = [mask] + ([token(pieces[1:], EARLY_FLOPS)] if direct else [])
    own, gots = [x], [x_got, swap(send, "tensor", bit)]
    while bit > 1:
        bit //= 2
        keep, own = fold(rank, keep, own, gots, early)
        gots = [swap(part, "tensor", bit) for part in own]
    ids_row = query_ids[None, :]
    if direct:
        split = max(1, data_size // 2)
        soon = [outer(own, gots, keep, mask, cap, k, 1)[0] for k in range(split)]
        rows = [shift(block, "dp", k) for k, block in enumerate(soon, 1)]
        *sent, kept = outer(own, gots, keep, mask, cap, split, data_size - split)
        sent[-1] = after(sent[-1], [mate, *passed])
        rows = [kept, *rows, *(shift(block, "dp", k) for k, block in enumerate(sent, 1 + split))]
        store = place(rows)
        late = [token(rows[2:-1], LATE_FLOPS)]
        pool = pool_halves([*pieces, mate, *passed])
        gaps = [*gaps, *(g ^ 1 for g in gaps)]
        early = score_early(ids_row, pool, rows[:2], gaps)
        scores = score(ids_row, pool, early, rows[2:], gaps, True, late)
    else:
        blocks = outer(own, gots, keep, mask, cap, 0, data_size)
        store = lax.all_to_all(jnp.stack(blocks), "dp", 0, 0, tiled=True).reshape(-1, width * rank)
        pool = pool_halves(pieces)
        scores = score(ids_row, pool, ids_row, [store], gaps, False, [])
    bit = 1
    while bit < tensor_size:
        scores = scores + swap(scores, "tensor", bit)
        bit *= 2
    return store, scores * (1.0 / (rank * rank))


def solution(mesh):
    return jax.shard_map(
        local,
        mesh=mesh,
        in_specs=(
            P(("groups", "dp"), "tensor"),
            P(("groups", "dp"), "tensor"),
            P("tensor", None),
            P("tensor", None),
            P(("groups", "dp"), None),
            P(("groups", "dp"), None),
            P(("groups", "dp"), "tensor"),
            P("groups"),
        ),
        out_specs=(P(("groups", "dp"), "tensor"), P(("groups", "dp"), None)),
        check_vma=False,
    )
```

```python
import functools

import jax
import jax.numpy as jnp
from jax import lax
from jax.experimental import pallas as pl
from jax.experimental.pallas import tpu as pltpu
from jax.sharding import PartitionSpec as P

F32 = jnp.float32
BF16 = jnp.bfloat16
MIB = 1024 * 1024
NT = (((1,), (1,)), ((), ()))
MOST_DIRECT = 8
GROUP = 16
ROWS = 16
LANES = 128
FIRST_FLOPS = 10 * 10**8
X_FLOPS = 6 * 10**8
MASK_FLOPS = 2 * 10**8
EARLY_FLOPS = 3 * 10**8
LATE_FLOPS = 10**8
SCORE_FLOPS = 0


def params(mib):
    return pltpu.CompilerParams(vmem_limit_bytes=mib * MIB)


def cost(flops, nbytes):
    return pl.CostEstimate(flops=flops, bytes_accessed=nbytes, transcendentals=0)


def halves(x):
    high = x.astype(BF16)
    return high, (x - high.astype(F32)).astype(BF16)


def mm(a, b, dims=(((1,), (0,)), ((), ()))):
    return lax.dot_general(a, b, dims, preferred_element_type=F32)


def slot_mask(owners, relative, cap, lengths, owner, slots, tokens):
    docs = lengths.shape[1]
    row = lax.broadcasted_iota(jnp.int32, (docs, docs), 0)
    col = lax.broadcasted_iota(jnp.int32, (docs, docs), 1)
    len_row = lengths.astype(F32)
    place_row = lax.rem(owner - lax.axis_index("dp") + 2 * owners - 1, owners) if relative else owner
    own_row = place_row.astype(F32)

    def column(values):
        return jnp.sum(jnp.where(row == col, values, 0.0), axis=1, keepdims=True)

    ends = jnp.sum(jnp.where(row <= col, column(len_row), 0.0), axis=0, keepdims=True)
    rank = jnp.sum(
        jnp.where((row < col) & (column(own_row) == own_row), 1.0, 0.0), axis=0, keepdims=True
    )
    slot = lax.broadcasted_iota(jnp.int32, (slots, docs), 0).astype(F32)
    hot = slot == own_row * cap + rank
    first = jnp.sum(jnp.where(hot, ends - len_row, 0.0), axis=1, keepdims=True)
    last = jnp.sum(jnp.where(hot, ends, 0.0), axis=1, keepdims=True)
    token = lax.broadcasted_iota(jnp.int32, (slots, tokens), 1).astype(F32)
    return jnp.where((token >= first) & (token < last), 1.0, 0.0).astype(BF16)


def mask_kernel(owners, relative, cap, lengths_ref, owner_ref, mask_ref):
    mask_ref[...] = slot_mask(owners, relative, cap, lengths_ref[...], owner_ref[...], *mask_ref.shape)


def dispatch_mask(lengths, owner_row, owners, cap, tokens, relative):
    return pl.pallas_call(
        functools.partial(mask_kernel, owners, relative, cap),
        out_shape=jax.ShapeDtypeStruct((owners * cap, tokens), BF16),
        compiler_params=params(8),
        cost_estimate=cost(MASK_FLOPS, 0),
    )(lengths, owner_row)


def put_projection(out_ref, proj_ref, act_ref):
    half = act_ref.shape[0] // 2
    out_ref[:, :half] = mm(proj_ref[...], act_ref[:half, :], NT)
    out_ref[:, half:] = mm(act_ref[half:, :], proj_ref[...], NT).T


def x_kernel(act_ref, proj_ref, *refs):
    put_projection(refs[-1], proj_ref, act_ref)


def project_x(act, in_t, tokens):
    return pl.pallas_call(
        x_kernel,
        in_specs=[pl.BlockSpec(memory_space=pltpu.VMEM)] * 2
        + [pl.BlockSpec(memory_space=pl.ANY)] * len(tokens),
        out_shape=jax.ShapeDtypeStruct((in_t.shape[0], act.shape[0]), F32),
        compiler_params=params(8),
        cost_estimate=cost(X_FLOPS, 0),
    )(act, in_t, *tokens)


def g_kernel(width, grad_ref, proj_ref, keep_ref, send_ref, full):
    put_projection(full, proj_ref, grad_ref)
    me = lax.axis_index("tensor")
    count = full.shape[0] // width
    for apart in range(count):
        block = pl.ds(pl.multiple_of((me ^ apart) * width, width), width)
        ref, spot = (keep_ref, apart) if apart < count // 2 else (send_ref, apart - count // 2)
        ref[spot * width : (spot + 1) * width, :] = full[block, :]


def project_g(grad, out_t, width):
    tokens, rank = grad.shape[0], out_t.shape[0]
    part = jax.ShapeDtypeStruct((rank // 2, tokens), F32)
    return pl.pallas_call(
        functools.partial(g_kernel, width),
        out_shape=[part, part],
        scratch_shapes=[pltpu.VMEM((rank, tokens), F32)],
        compiler_params=params(24),
        cost_estimate=cost(0, 0),
    )(grad, out_t)


def stack(refs):
    return jnp.concatenate([r[...] for r in refs], axis=0)


def fold_kernel(rank, owned, came, keep_ref, *refs):
    first_ref, second_ref, kept_ref = refs[-3:]
    got = stack(refs[owned : owned + came])
    total = keep_ref[...] + got[rank:]
    kept = kept_ref.shape[0]
    kept_ref[...] = total[:kept]
    x = stack(refs[:owned])[:rank] + got[:rank]
    sent = jnp.concatenate([x, total[kept:]], axis=0)
    cut = first_ref.shape[0]
    first_ref[...] = sent[:cut]
    second_ref[...] = sent[cut:]


def fold(rank, keep, own, gots, pieces):
    tokens = keep.shape[1]
    kept = keep.shape[0] // 2
    cut = (rank + kept) // 16 * 8
    *sent, keep = pl.pallas_call(
        functools.partial(fold_kernel, rank, len(own), len(gots)),
        in_specs=[pl.BlockSpec(memory_space=pltpu.VMEM)] * (1 + len(own) + len(gots))
        + [pl.BlockSpec(memory_space=pl.ANY)] * len(pieces),
        out_shape=[
            jax.ShapeDtypeStruct((rows, tokens), F32) for rows in (cut, rank + kept - cut, kept)
        ],
        compiler_params=params(16),
        cost_estimate=cost(0, 0),
    )(keep, *own, *gots, *pieces)
    return keep, sent


def outer_kernel(first, owners, sent, g_ref, mask_ref, *refs):
    blocks = refs[-owners:]
    width = g_ref.shape[0]
    own, got = stack(refs[:sent]), stack(refs[sent : 2 * sent])
    rank = got.shape[0] - width
    x_full = own[:rank] + got[:rank]
    g_full = g_ref[...] + got[rank:]
    x_high, x_low = halves(x_full)
    x_both = jnp.concatenate(
        [
            jnp.concatenate([x_high, x_high], axis=1),
            jnp.concatenate([x_low, jnp.zeros_like(x_low)], axis=1),
        ],
        axis=0,
    )
    g_high = g_full.astype(BF16).astype(F32)
    g_low = g_full - g_high
    cap = blocks[0].shape[0]
    slots = owners * cap
    mask = mask_ref[first * cap : first * cap + slots, :]
    tokens = mask.shape[1]

    def masked(row):
        wide = jnp.broadcast_to(row, (ROWS, tokens)).astype(BF16)
        return [mask[i : i + ROWS] * wide for i in range(0, slots, ROWS)]

    group = min(width, GROUP)
    for i in range(0, width, group):
        rows = [
            jnp.concatenate([m for j in range(i, i + group) for m in masked(g[j : j + 1])], axis=0)
            for g in (g_high, g_low)
        ]
        both = mm(jnp.concatenate(rows, axis=1), x_both, NT)
        columns = []
        for j in range(group):
            part = both[j * slots : (j + 1) * slots]
            columns.append(part[:, :rank] + part[:, rank:])
        out = jnp.concatenate(columns, axis=1)
        for k, block in enumerate(blocks):
            block[:, i * rank : (i + group) * rank] = out[k * cap : (k + 1) * cap, :]


def outer(sent, gots, g, mask, cap, first, owners):
    width = g.shape[0]
    rank = sum(p.shape[0] for p in sent) - width
    return pl.pallas_call(
        functools.partial(outer_kernel, first, owners, len(sent)),
        out_shape=[jax.ShapeDtypeStruct((cap, width * rank), F32)] * owners,
        compiler_params=params(24),
        cost_estimate=cost(8 * owners * cap * width * mask.shape[1] * rank, 0),
    )(g, mask, *sent, *gots)


def token_kernel(*refs):
    refs[-1][...] = jnp.zeros_like(refs[-1])


def token(arrays, flops):
    return pl.pallas_call(
        token_kernel,
        in_specs=[pl.BlockSpec(memory_space=pl.ANY)] * len(arrays),
        out_shape=jax.ShapeDtypeStruct((8, 128), F32),
        compiler_params=params(4),
        cost_estimate=cost(flops, 0),
    )(*arrays)


def after_kernel(block_ref, *refs):
    refs[-1][...] = block_ref[...]


def after(block, pieces):
    return pl.pallas_call(
        after_kernel,
        in_specs=[pl.BlockSpec(memory_space=pltpu.VMEM)]
        + [pl.BlockSpec(memory_space=pl.ANY)] * len(pieces),
        out_shape=jax.ShapeDtypeStruct(block.shape, F32),
        compiler_params=params(4),
        cost_estimate=cost(0, 0),
    )(block, *pieces)


def pool_kernel(*refs):
    refs[-1][...] = jnp.concatenate(halves(stack(refs[:-1])), axis=0)


def pool_halves(pieces):
    rows, feats = sum(piece.shape[0] for piece in pieces), pieces[0].shape[1]
    return pl.pallas_call(
        pool_kernel,
        out_shape=jax.ShapeDtypeStruct((2 * rows, feats), BF16),
        compiler_params=params(16),
        cost_estimate=cost(0, 0),
    )(*pieces)


def scores_of(rows, ids, pool, gaps):
    me = lax.axis_index("dp")
    high, low = halves(rows)
    slots, split, queries = rows.shape[0], pool.shape[0] // 2, ids.shape[1]
    products = mm(jnp.concatenate([high, low], axis=0), pool, NT)
    part = products[:slots, :split] + products[:slots, split:] + products[slots:, :split]
    held = split // len(gaps)
    if split == LANES and queries == LANES and len(gaps) > 1:
        spot = lax.rem(ids, held)
        for place, gap in enumerate(gaps):
            spot = spot + jnp.where(lax.div(ids, held) == (me ^ gap), place * held, 0)
        return jnp.take_along_axis(part, jnp.broadcast_to(spot, part.shape), axis=1)
    row = lax.broadcasted_iota(jnp.int32, (held, queries), 0)
    places = [row + ((me ^ gap) * held if len(gaps) > 1 else 0) for gap in gaps]
    hot = (jnp.concatenate(places, axis=0) == ids).astype(F32).astype(BF16)
    top, rest = halves(part)
    last = (part - top.astype(F32) - rest.astype(F32)).astype(BF16)
    picked = mm(jnp.concatenate([top, rest, last], axis=0), hot)
    return picked[:slots] + picked[slots : 2 * slots] + picked[2 * slots :]


def early_kernel(gaps, ids_ref, pool_ref, *refs):
    refs[-1][...] = scores_of(stack(refs[:-1]), ids_ref[...], pool_ref[...], gaps)


def score_early(ids_row, pool, rows, gaps):
    slots = sum(row.shape[0] for row in rows)
    return pl.pallas_call(
        functools.partial(early_kernel, gaps),
        out_shape=jax.ShapeDtypeStruct((slots, ids_row.shape[1]), F32),
        compiler_params=params(16),
        cost_estimate=cost(SCORE_FLOPS, 0),
    )(ids_row, pool, *rows)


def score_kernel(count, gaps, relative, ids_ref, pool_ref, early_ref, *refs):
    rows, scores_ref = refs[:count], refs[-1]
    me = lax.axis_index("dp")
    cap = rows[0].shape[0]
    total = scores_of(stack(rows), ids_ref[...], pool_ref[...], gaps)
    done = early_ref.shape[0] // cap if relative else 0
    for k in range(done + count):
        part = early_ref if k < done else total
        at = (k if k < done else k - done) * cap
        source = lax.rem(me - k + done + count, done + count) if relative else k
        scores_ref[pl.ds(pl.multiple_of(source * cap, cap), cap), :] = part[at : at + cap, :]


def score(ids_row, pool, early, rows, gaps, relative, tokens):
    slots = sum(row.shape[0] for row in rows) + (early.shape[0] if relative else 0)
    queries = ids_row.shape[1]
    return pl.pallas_call(
        functools.partial(score_kernel, len(rows), gaps, relative),
        in_specs=[pl.BlockSpec(memory_space=pltpu.VMEM)] * (3 + len(rows))
        + [pl.BlockSpec(memory_space=pl.ANY)] * len(tokens),
        out_shape=jax.ShapeDtypeStruct((slots, queries), F32),
        compiler_params=params(24),
        cost_estimate=cost(0, 0),
    )(ids_row, pool, early, *rows, *tokens)


def place_kernel(*refs):
    rows, store_ref = refs[:-1], refs[-1]
    me = lax.axis_index("dp")
    cap = rows[0].shape[0]
    for k, row in enumerate(rows):
        source = lax.rem(me - k + len(rows), len(rows))
        store_ref[pl.ds(pl.multiple_of(source * cap, cap), cap), :] = row[...]


def place(rows):
    slots, feats = rows[0].shape[0] * len(rows), rows[0].shape[1]
    return pl.pallas_call(
        place_kernel,
        out_shape=jax.ShapeDtypeStruct((slots, feats), F32),
        compiler_params=params(16),
        cost_estimate=cost(0, 8 * slots * feats),
    )(*rows)


def swap(x, axis, gap):
    return lax.ppermute(x, axis, [(i, i ^ gap) for i in range(lax.axis_size(axis))])


def shift(x, axis, by):
    size = lax.axis_size(axis)
    return lax.ppermute(x, axis, [(i, (i + by) % size) for i in range(size)])


def gather_pieces(piece):
    pieces, gaps = [piece], [0]
    bit = lax.axis_size("dp") // 2
    while bit > 1:
        pieces, gaps = pieces + [swap(p, "dp", bit) for p in pieces], gaps + [g ^ bit for g in gaps]
        bit //= 2
    return pieces, gaps


def local(
    activations, out_grads, proj_in, proj_out, doc_lengths, doc_owner, query_grads, query_ids
):
    tensor_size = lax.axis_size("tensor")
    data_size = lax.axis_size("dp")
    tokens = activations.shape[0]
    rank = proj_in.shape[1]
    width = rank // tensor_size
    docs = doc_owner.shape[0]
    cap = max(2, 2 * docs // data_size)
    direct = data_size <= MOST_DIRECT

    if direct:
        pieces, gaps = gather_pieces(query_grads)
        mate = swap(query_grads, "dp", 1)
        passed = [swap(piece, "dp", 1) for piece in pieces[1:]]
    else:
        pieces, gaps = [lax.all_gather(query_grads, "dp", axis=0, tiled=True)], [0]

    mask = dispatch_mask(doc_lengths, doc_owner.T, data_size, cap, activations.shape[0], direct)
    x = project_x(activations, proj_in.T, [token([], FIRST_FLOPS)])
    bit = tensor_size // 2
    x_got = swap(x, "tensor", bit)
    keep, send = project_g(out_grads, proj_out.T, width)
    early = [mask] + ([token(pieces[1:], EARLY_FLOPS)] if direct else [])
    own, gots = [x], [x_got, swap(send, "tensor", bit)]
    while bit > 1:
        bit //= 2
        keep, own = fold(rank, keep, own, gots, early)
        gots = [swap(part, "tensor", bit) for part in own]
    ids_row = query_ids[None, :]
    if direct:
        spans = [(0, 1), (1, data_size - 1), (data_size - 1, data_size)]
        calls = [outer(own, gots, keep, mask, cap, i, j - i) for i, j in spans if i < j]
        *sent, kept = [block for blocks in calls for block in blocks]
        sent[-1] = after(sent[-1], [mate, *passed])
        rows = [kept, *(shift(block, "dp", k) for k, block in enumerate(sent, 1))]
        store = place(rows)
        late = [token(rows[2:-1], LATE_FLOPS)]
        pool = pool_halves([*pieces, mate, *passed])
        gaps = [*gaps, *(g ^ 1 for g in gaps)]
        early = score_early(ids_row, pool, rows[:2], gaps)
        scores = score(ids_row, pool, early, rows[2:], gaps, True, late)
    else:
        blocks = outer(own, gots, keep, mask, cap, 0, data_size)
        store = lax.all_to_all(jnp.stack(blocks), "dp", 0, 0, tiled=True).reshape(-1, width * rank)
        pool = pool_halves(pieces)
        scores = score(ids_row, pool, ids_row, [store], gaps, False, [])
    bit = 1
    while bit < tensor_size:
        scores = scores + swap(scores, "tensor", bit)
        bit *= 2
    return store, scores * (1.0 / (rank * rank))


def solution(mesh):
    return jax.shard_map(
        local,
        mesh=mesh,
        in_specs=(
            P(("groups", "dp"), "tensor"),
            P(("groups", "dp"), "tensor"),
            P("tensor", None),
            P("tensor", None),
            P(("groups", "dp"), None),
            P(("groups", "dp"), None),
            P(("groups", "dp"), "tensor"),
            P("groups"),
        ),
        out_specs=(P(("groups", "dp"), "tensor"), P(("groups", "dp"), None)),
        check_vma=False,
    )
```

```python
import functools

import jax
import jax.numpy as jnp
from jax import lax
from jax.experimental import pallas as pl
from jax.experimental.pallas import tpu as pltpu
from jax.sharding import PartitionSpec as P

F32 = jnp.float32
BF16 = jnp.bfloat16
MIB = 1024 * 1024
NT = (((1,), (1,)), ((), ()))
MOST_DIRECT = 8
GROUP = 16
ROWS = 16
LANES = 128
FIRST_FLOPS = 10 * 10**8
X_FLOPS = 6 * 10**8
MASK_FLOPS = 2 * 10**8
EARLY_FLOPS = 3 * 10**8
LATE_FLOPS = 10**8
SCORE_FLOPS = 0


def params(mib):
    return pltpu.CompilerParams(vmem_limit_bytes=mib * MIB)


def cost(flops, nbytes):
    return pl.CostEstimate(flops=flops, bytes_accessed=nbytes, transcendentals=0)


def halves(x):
    high = x.astype(BF16)
    return high, (x - high.astype(F32)).astype(BF16)


def mm(a, b, dims=(((1,), (0,)), ((), ()))):
    return lax.dot_general(a, b, dims, preferred_element_type=F32)


def slot_mask(owners, relative, cap, lengths, owner, slots, tokens):
    docs = lengths.shape[1]
    row = lax.broadcasted_iota(jnp.int32, (docs, docs), 0)
    col = lax.broadcasted_iota(jnp.int32, (docs, docs), 1)
    len_row = lengths.astype(F32)
    place_row = lax.rem(owner - lax.axis_index("dp") + 2 * owners - 1, owners) if relative else owner
    own_row = place_row.astype(F32)

    def column(values):
        return jnp.sum(jnp.where(row == col, values, 0.0), axis=1, keepdims=True)

    ends = jnp.sum(jnp.where(row <= col, column(len_row), 0.0), axis=0, keepdims=True)
    rank = jnp.sum(
        jnp.where((row < col) & (column(own_row) == own_row), 1.0, 0.0), axis=0, keepdims=True
    )
    slot = lax.broadcasted_iota(jnp.int32, (slots, docs), 0).astype(F32)
    hot = slot == own_row * cap + rank
    first = jnp.sum(jnp.where(hot, ends - len_row, 0.0), axis=1, keepdims=True)
    last = jnp.sum(jnp.where(hot, ends, 0.0), axis=1, keepdims=True)
    token = lax.broadcasted_iota(jnp.int32, (slots, tokens), 1).astype(F32)
    return jnp.where((token >= first) & (token < last), 1.0, 0.0).astype(BF16)


def mask_kernel(owners, relative, cap, lengths_ref, owner_ref, mask_ref):
    mask_ref[...] = slot_mask(owners, relative, cap, lengths_ref[...], owner_ref[...], *mask_ref.shape)


def dispatch_mask(lengths, owner_row, owners, cap, tokens, relative):
    return pl.pallas_call(
        functools.partial(mask_kernel, owners, relative, cap),
        out_shape=jax.ShapeDtypeStruct((owners * cap, tokens), BF16),
        compiler_params=params(8),
        cost_estimate=cost(MASK_FLOPS, 0),
    )(lengths, owner_row)


def put_projection(out_ref, proj_ref, act_ref):
    half = act_ref.shape[0] // 2
    out_ref[:, :half] = mm(proj_ref[...], act_ref[:half, :], NT)
    out_ref[:, half:] = mm(act_ref[half:, :], proj_ref[...], NT).T


def x_kernel(act_ref, proj_ref, *refs):
    put_projection(refs[-1], proj_ref, act_ref)


def project_x(act, in_t, tokens):
    return pl.pallas_call(
        x_kernel,
        in_specs=[pl.BlockSpec(memory_space=pltpu.VMEM)] * 2
        + [pl.BlockSpec(memory_space=pl.ANY)] * len(tokens),
        out_shape=jax.ShapeDtypeStruct((in_t.shape[0], act.shape[0]), F32),
        compiler_params=params(8),
        cost_estimate=cost(X_FLOPS, 0),
    )(act, in_t, *tokens)


def g_kernel(width, grad_ref, proj_ref, keep_ref, send_ref, full):
    put_projection(full, proj_ref, grad_ref)
    me = lax.axis_index("tensor")
    count = full.shape[0] // width
    for apart in range(count):
        block = pl.ds(pl.multiple_of((me ^ apart) * width, width), width)
        ref, spot = (keep_ref, apart) if apart < count // 2 else (send_ref, apart - count // 2)
        ref[spot * width : (spot + 1) * width, :] = full[block, :]


def project_g(grad, out_t, width):
    tokens, rank = grad.shape[0], out_t.shape[0]
    part = jax.ShapeDtypeStruct((rank // 2, tokens), F32)
    return pl.pallas_call(
        functools.partial(g_kernel, width),
        out_shape=[part, part],
        scratch_shapes=[pltpu.VMEM((rank, tokens), F32)],
        compiler_params=params(24),
        cost_estimate=cost(0, 0),
    )(grad, out_t)


def stack(refs):
    return jnp.concatenate([r[...] for r in refs], axis=0)


def fold_kernel(rank, owned, came, keep_ref, *refs):
    first_ref, second_ref, kept_ref = refs[-3:]
    got = stack(refs[owned : owned + came])
    total = keep_ref[...] + got[rank:]
    kept = kept_ref.shape[0]
    kept_ref[...] = total[:kept]
    x = stack(refs[:owned])[:rank] + got[:rank]
    sent = jnp.concatenate([x, total[kept:]], axis=0)
    cut = first_ref.shape[0]
    first_ref[...] = sent[:cut]
    second_ref[...] = sent[cut:]


def fold(rank, keep, own, gots, pieces):
    tokens = keep.shape[1]
    kept = keep.shape[0] // 2
    cut = (rank + kept) // 16 * 8
    *sent, keep = pl.pallas_call(
        functools.partial(fold_kernel, rank, len(own), len(gots)),
        in_specs=[pl.BlockSpec(memory_space=pltpu.VMEM)] * (1 + len(own) + len(gots))
        + [pl.BlockSpec(memory_space=pl.ANY)] * len(pieces),
        out_shape=[
            jax.ShapeDtypeStruct((rows, tokens), F32) for rows in (cut, rank + kept - cut, kept)
        ],
        compiler_params=params(16),
        cost_estimate=cost(0, 0),
    )(keep, *own, *gots, *pieces)
    return keep, sent


def outer_kernel(first, owners, sent, g_ref, mask_ref, *refs):
    blocks = refs[-owners:]
    width = g_ref.shape[0]
    own, got = stack(refs[:sent]), stack(refs[sent : 2 * sent])
    rank = got.shape[0] - width
    x_full = own[:rank] + got[:rank]
    g_full = g_ref[...] + got[rank:]
    x_both = jnp.concatenate(halves(x_full), axis=0)
    g_high = g_full.astype(BF16).astype(F32)
    g_low = g_full - g_high
    cap = blocks[0].shape[0]
    slots = owners * cap
    mask = mask_ref[first * cap : first * cap + slots, :]
    tokens = mask.shape[1]

    def masked(row):
        wide = jnp.broadcast_to(row, (ROWS, tokens)).astype(BF16)
        return [mask[i : i + ROWS] * wide for i in range(0, slots, ROWS)]

    group = min(width, GROUP)
    for i in range(0, width, group):
        rows = [m for j in range(i, i + group) for g in (g_high, g_low) for m in masked(g[j : j + 1])]
        both = mm(jnp.concatenate(rows, axis=0), x_both, NT)
        columns = []
        for j in range(group):
            high = both[2 * j * slots : (2 * j + 1) * slots]
            low = both[(2 * j + 1) * slots : (2 * j + 2) * slots]
            columns.append(high[:, :rank] + high[:, rank:] + low[:, :rank])
        out = jnp.concatenate(columns, axis=1)
        for k, block in enumerate(blocks):
            block[:, i * rank : (i + group) * rank] = out[k * cap : (k + 1) * cap, :]


def outer(sent, gots, g, mask, cap, first, owners):
    width = g.shape[0]
    rank = sum(p.shape[0] for p in sent) - width
    return pl.pallas_call(
        functools.partial(outer_kernel, first, owners, len(sent)),
        out_shape=[jax.ShapeDtypeStruct((cap, width * rank), F32)] * owners,
        compiler_params=params(24),
        cost_estimate=cost(8 * owners * cap * width * mask.shape[1] * rank, 0),
    )(g, mask, *sent, *gots)


def token_kernel(*refs):
    refs[-1][...] = jnp.zeros_like(refs[-1])


def token(arrays, flops):
    return pl.pallas_call(
        token_kernel,
        in_specs=[pl.BlockSpec(memory_space=pl.ANY)] * len(arrays),
        out_shape=jax.ShapeDtypeStruct((8, 128), F32),
        compiler_params=params(4),
        cost_estimate=cost(flops, 0),
    )(*arrays)


def after_kernel(block_ref, *refs):
    refs[-1][...] = block_ref[...]


def after(block, pieces):
    return pl.pallas_call(
        after_kernel,
        in_specs=[pl.BlockSpec(memory_space=pltpu.VMEM)]
        + [pl.BlockSpec(memory_space=pl.ANY)] * len(pieces),
        out_shape=jax.ShapeDtypeStruct(block.shape, F32),
        compiler_params=params(4),
        cost_estimate=cost(0, 0),
    )(block, *pieces)


def pool_kernel(*refs):
    refs[-1][...] = jnp.concatenate(halves(stack(refs[:-1])), axis=0)


def pool_halves(pieces):
    rows, feats = sum(piece.shape[0] for piece in pieces), pieces[0].shape[1]
    return pl.pallas_call(
        pool_kernel,
        out_shape=jax.ShapeDtypeStruct((2 * rows, feats), BF16),
        compiler_params=params(16),
        cost_estimate=cost(0, 0),
    )(*pieces)


def scores_of(rows, ids, pool, gaps):
    me = lax.axis_index("dp")
    high, low = halves(rows)
    slots, split, queries = rows.shape[0], pool.shape[0] // 2, ids.shape[1]
    products = mm(jnp.concatenate([high, low], axis=0), pool, NT)
    part = products[:slots, :split] + products[:slots, split:] + products[slots:, :split]
    held = split // len(gaps)
    if split == LANES and queries == LANES and len(gaps) > 1:
        spot = lax.rem(ids, held)
        for place, gap in enumerate(gaps):
            spot = spot + jnp.where(lax.div(ids, held) == (me ^ gap), place * held, 0)
        return jnp.take_along_axis(part, jnp.broadcast_to(spot, part.shape), axis=1)
    row = lax.broadcasted_iota(jnp.int32, (held, queries), 0)
    places = [row + ((me ^ gap) * held if len(gaps) > 1 else 0) for gap in gaps]
    hot = (jnp.concatenate(places, axis=0) == ids).astype(F32).astype(BF16)
    top, rest = halves(part)
    last = (part - top.astype(F32) - rest.astype(F32)).astype(BF16)
    picked = mm(jnp.concatenate([top, rest, last], axis=0), hot)
    return picked[:slots] + picked[slots : 2 * slots] + picked[2 * slots :]


def early_kernel(gaps, ids_ref, pool_ref, *refs):
    refs[-1][...] = scores_of(stack(refs[:-1]), ids_ref[...], pool_ref[...], gaps)


def score_early(ids_row, pool, rows, gaps):
    slots = sum(row.shape[0] for row in rows)
    return pl.pallas_call(
        functools.partial(early_kernel, gaps),
        out_shape=jax.ShapeDtypeStruct((slots, ids_row.shape[1]), F32),
        compiler_params=params(16),
        cost_estimate=cost(SCORE_FLOPS, 0),
    )(ids_row, pool, *rows)


def score_kernel(count, gaps, relative, ids_ref, pool_ref, early_ref, *refs):
    rows, scores_ref = refs[:count], refs[-1]
    me = lax.axis_index("dp")
    cap = rows[0].shape[0]
    total = scores_of(stack(rows), ids_ref[...], pool_ref[...], gaps)
    done = early_ref.shape[0] // cap if relative else 0
    for k in range(done + count):
        part = early_ref if k < done else total
        at = (k if k < done else k - done) * cap
        source = lax.rem(me - k + done + count, done + count) if relative else k
        scores_ref[pl.ds(pl.multiple_of(source * cap, cap), cap), :] = part[at : at + cap, :]


def score(ids_row, pool, early, rows, gaps, relative, tokens):
    slots = sum(row.shape[0] for row in rows) + (early.shape[0] if relative else 0)
    queries = ids_row.shape[1]
    return pl.pallas_call(
        functools.partial(score_kernel, len(rows), gaps, relative),
        in_specs=[pl.BlockSpec(memory_space=pltpu.VMEM)] * (3 + len(rows))
        + [pl.BlockSpec(memory_space=pl.ANY)] * len(tokens),
        out_shape=jax.ShapeDtypeStruct((slots, queries), F32),
        compiler_params=params(24),
        cost_estimate=cost(0, 0),
    )(ids_row, pool, early, *rows, *tokens)


def place_kernel(*refs):
    rows, store_ref = refs[:-1], refs[-1]
    me = lax.axis_index("dp")
    cap = rows[0].shape[0]
    for k, row in enumerate(rows):
        source = lax.rem(me - k + len(rows), len(rows))
        store_ref[pl.ds(pl.multiple_of(source * cap, cap), cap), :] = row[...]


def place(rows):
    slots, feats = rows[0].shape[0] * len(rows), rows[0].shape[1]
    return pl.pallas_call(
        place_kernel,
        out_shape=jax.ShapeDtypeStruct((slots, feats), F32),
        compiler_params=params(16),
        cost_estimate=cost(0, 8 * slots * feats),
    )(*rows)


def swap(x, axis, gap):
    return lax.ppermute(x, axis, [(i, i ^ gap) for i in range(lax.axis_size(axis))])


def shift(x, axis, by):
    size = lax.axis_size(axis)
    return lax.ppermute(x, axis, [(i, (i + by) % size) for i in range(size)])


def gather_pieces(piece):
    pieces, gaps = [piece], [0]
    bit = lax.axis_size("dp") // 2
    while bit > 1:
        pieces, gaps = pieces + [swap(p, "dp", bit) for p in pieces], gaps + [g ^ bit for g in gaps]
        bit //= 2
    return pieces, gaps


def local(
    activations, out_grads, proj_in, proj_out, doc_lengths, doc_owner, query_grads, query_ids
):
    tensor_size = lax.axis_size("tensor")
    data_size = lax.axis_size("dp")
    tokens = activations.shape[0]
    rank = proj_in.shape[1]
    width = rank // tensor_size
    docs = doc_owner.shape[0]
    cap = max(2, 2 * docs // data_size)
    direct = data_size <= MOST_DIRECT

    if direct:
        pieces, gaps = gather_pieces(query_grads)
        mate = swap(query_grads, "dp", 1)
        passed = [swap(piece, "dp", 1) for piece in pieces[1:]]
    else:
        pieces, gaps = [lax.all_gather(query_grads, "dp", axis=0, tiled=True)], [0]

    mask = dispatch_mask(doc_lengths, doc_owner.T, data_size, cap, activations.shape[0], direct)
    x = project_x(activations, proj_in.T, [token([], FIRST_FLOPS)])
    bit = tensor_size // 2
    x_got = swap(x, "tensor", bit)
    keep, send = project_g(out_grads, proj_out.T, width)
    early = [mask] + ([token(pieces[1:], EARLY_FLOPS)] if direct else [])
    own, gots = [x], [x_got, swap(send, "tensor", bit)]
    while bit > 1:
        bit //= 2
        keep, own = fold(rank, keep, own, gots, early)
        gots = [swap(part, "tensor", bit) for part in own]
    ids_row = query_ids[None, :]
    if direct:
        calls = [outer(own, gots, keep, mask, cap, k, 1) for k in range(data_size)]
        *sent, kept = [block for blocks in calls for block in blocks]
        sent[-1] = after(sent[-1], [mate, *passed])
        rows = [kept, *(shift(block, "dp", k) for k, block in enumerate(sent, 1))]
        store = place(rows)
        late = [token(rows[2:-1], LATE_FLOPS)]
        pool = pool_halves([*pieces, mate, *passed])
        gaps = [*gaps, *(g ^ 1 for g in gaps)]
        early = score_early(ids_row, pool, rows[:2], gaps)
        scores = score(ids_row, pool, early, rows[2:], gaps, True, late)
    else:
        blocks = outer(own, gots, keep, mask, cap, 0, data_size)
        store = lax.all_to_all(jnp.stack(blocks), "dp", 0, 0, tiled=True).reshape(-1, width * rank)
        pool = pool_halves(pieces)
        scores = score(ids_row, pool, ids_row, [store], gaps, False, [])
    bit = 1
    while bit < tensor_size:
        scores = scores + swap(scores, "tensor", bit)
        bit *= 2
    return store, scores * (1.0 / (rank * rank))


def solution(mesh):
    return jax.shard_map(
        local,
        mesh=mesh,
        in_specs=(
            P(("groups", "dp"), "tensor"),
            P(("groups", "dp"), "tensor"),
            P("tensor", None),
            P("tensor", None),
            P(("groups", "dp"), None),
            P(("groups", "dp"), None),
            P(("groups", "dp"), "tensor"),
            P("groups"),
        ),
        out_specs=(P(("groups", "dp"), "tensor"), P(("groups", "dp"), None)),
        check_vma=False,
    )
```

```python
import functools

import jax
import jax.numpy as jnp
from jax import lax
from jax.experimental import pallas as pl
from jax.experimental.pallas import tpu as pltpu
from jax.sharding import PartitionSpec as P

F32 = jnp.float32
BF16 = jnp.bfloat16
MIB = 1024 * 1024
NT = (((1,), (1,)), ((), ()))
MOST_DIRECT = 8
GROUP = 16
ROWS = 16
LANES = 128
FIRST_FLOPS = 10 * 10**8
X_FLOPS = 6 * 10**8
MASK_FLOPS = 2 * 10**8
EARLY_FLOPS = 3 * 10**8
LATE_FLOPS = 10**8
SCORE_FLOPS = 0


def params(mib):
    return pltpu.CompilerParams(vmem_limit_bytes=mib * MIB)


def cost(flops, nbytes):
    return pl.CostEstimate(flops=flops, bytes_accessed=nbytes, transcendentals=0)


def halves(x):
    high = x.astype(BF16)
    return high, (x - high.astype(F32)).astype(BF16)


def mm(a, b, dims=(((1,), (0,)), ((), ()))):
    return lax.dot_general(a, b, dims, preferred_element_type=F32)


def slot_mask(owners, relative, cap, lengths, owner, slots, tokens):
    docs = lengths.shape[1]
    row = lax.broadcasted_iota(jnp.int32, (docs, docs), 0)
    col = lax.broadcasted_iota(jnp.int32, (docs, docs), 1)
    len_row = lengths.astype(F32)
    place_row = lax.rem(owner - lax.axis_index("dp") + 2 * owners - 1, owners) if relative else owner
    own_row = place_row.astype(F32)

    def column(values):
        return jnp.sum(jnp.where(row == col, values, 0.0), axis=1, keepdims=True)

    ends = jnp.sum(jnp.where(row <= col, column(len_row), 0.0), axis=0, keepdims=True)
    rank = jnp.sum(
        jnp.where((row < col) & (column(own_row) == own_row), 1.0, 0.0), axis=0, keepdims=True
    )
    slot = lax.broadcasted_iota(jnp.int32, (slots, docs), 0).astype(F32)
    hot = slot == own_row * cap + rank
    first = jnp.sum(jnp.where(hot, ends - len_row, 0.0), axis=1, keepdims=True)
    last = jnp.sum(jnp.where(hot, ends, 0.0), axis=1, keepdims=True)
    token = lax.broadcasted_iota(jnp.int32, (slots, tokens), 1).astype(F32)
    return jnp.where((token >= first) & (token < last), 1.0, 0.0).astype(BF16)


def mask_kernel(owners, relative, cap, lengths_ref, owner_ref, mask_ref):
    mask_ref[...] = slot_mask(owners, relative, cap, lengths_ref[...], owner_ref[...], *mask_ref.shape)


def dispatch_mask(lengths, owner_row, owners, cap, tokens, relative):
    return pl.pallas_call(
        functools.partial(mask_kernel, owners, relative, cap),
        out_shape=jax.ShapeDtypeStruct((owners * cap, tokens), BF16),
        compiler_params=params(8),
        cost_estimate=cost(MASK_FLOPS, 0),
    )(lengths, owner_row)


def put_projection(out_ref, proj_ref, act_ref):
    half = act_ref.shape[0] // 2
    out_ref[:, :half] = mm(proj_ref[...], act_ref[:half, :], NT)
    out_ref[:, half:] = mm(act_ref[half:, :], proj_ref[...], NT).T


def x_kernel(act_ref, proj_ref, *refs):
    put_projection(refs[-1], proj_ref, act_ref)


def project_x(act, in_t, tokens):
    return pl.pallas_call(
        x_kernel,
        in_specs=[pl.BlockSpec(memory_space=pltpu.VMEM)] * 2
        + [pl.BlockSpec(memory_space=pl.ANY)] * len(tokens),
        out_shape=jax.ShapeDtypeStruct((in_t.shape[0], act.shape[0]), F32),
        compiler_params=params(8),
        cost_estimate=cost(X_FLOPS, 0),
    )(act, in_t, *tokens)


def g_kernel(width, grad_ref, proj_ref, keep_ref, send_ref, full):
    put_projection(full, proj_ref, grad_ref)
    me = lax.axis_index("tensor")
    count = full.shape[0] // width
    for apart in range(count):
        block = pl.ds(pl.multiple_of((me ^ apart) * width, width), width)
        ref, spot = (keep_ref, apart) if apart < count // 2 else (send_ref, apart - count // 2)
        ref[spot * width : (spot + 1) * width, :] = full[block, :]


def project_g(grad, out_t, width):
    tokens, rank = grad.shape[0], out_t.shape[0]
    part = jax.ShapeDtypeStruct((rank // 2, tokens), F32)
    return pl.pallas_call(
        functools.partial(g_kernel, width),
        out_shape=[part, part],
        scratch_shapes=[pltpu.VMEM((rank, tokens), F32)],
        compiler_params=params(24),
        cost_estimate=cost(0, 0),
    )(grad, out_t)


def stack(refs):
    return jnp.concatenate([r[...] for r in refs], axis=0)


def fold_kernel(rank, owned, came, keep_ref, *refs):
    first_ref, second_ref, kept_ref = refs[-3:]
    got = stack(refs[owned : owned + came])
    total = keep_ref[...] + got[rank:]
    kept = kept_ref.shape[0]
    kept_ref[...] = total[:kept]
    x = stack(refs[:owned])[:rank] + got[:rank]
    sent = jnp.concatenate([x, total[kept:]], axis=0)
    cut = first_ref.shape[0]
    first_ref[...] = sent[:cut]
    second_ref[...] = sent[cut:]


def fold(rank, keep, own, gots, pieces):
    tokens = keep.shape[1]
    kept = keep.shape[0] // 2
    cut = (rank + kept) // 16 * 8
    *sent, keep = pl.pallas_call(
        functools.partial(fold_kernel, rank, len(own), len(gots)),
        in_specs=[pl.BlockSpec(memory_space=pltpu.VMEM)] * (1 + len(own) + len(gots))
        + [pl.BlockSpec(memory_space=pl.ANY)] * len(pieces),
        out_shape=[
            jax.ShapeDtypeStruct((rows, tokens), F32) for rows in (cut, rank + kept - cut, kept)
        ],
        compiler_params=params(16),
        cost_estimate=cost(0, 0),
    )(keep, *own, *gots, *pieces)
    return keep, sent


def outer_kernel(first, owners, sent, g_ref, mask_ref, *refs):
    blocks = refs[-owners:]
    width = g_ref.shape[0]
    own, got = stack(refs[:sent]), stack(refs[sent : 2 * sent])
    rank = got.shape[0] - width
    x_full = own[:rank] + got[:rank]
    g_full = g_ref[...] + got[rank:]
    x_high, x_low = halves(x_full)
    x_both = jnp.concatenate(
        [
            jnp.concatenate([x_high, x_high], axis=1),
            jnp.concatenate([x_low, jnp.zeros_like(x_low)], axis=1),
        ],
        axis=0,
    )
    g_high = g_full.astype(BF16).astype(F32)
    g_low = g_full - g_high
    cap = blocks[0].shape[0]
    slots = owners * cap
    mask = mask_ref[first * cap : first * cap + slots, :]
    tokens = mask.shape[1]

    def masked(row):
        wide = jnp.broadcast_to(row, (ROWS, tokens)).astype(BF16)
        return [mask[i : i + ROWS] * wide for i in range(0, slots, ROWS)]

    group = min(width, GROUP)
    for i in range(0, width, group):
        rows = [
            jnp.concatenate([m for j in range(i, i + group) for m in masked(g[j : j + 1])], axis=0)
            for g in (g_high, g_low)
        ]
        both = mm(jnp.concatenate(rows, axis=1), x_both, NT)
        columns = []
        for j in range(group):
            part = both[j * slots : (j + 1) * slots]
            columns.append(part[:, :rank] + part[:, rank:])
        out = jnp.concatenate(columns, axis=1)
        for k, block in enumerate(blocks):
            block[:, i * rank : (i + group) * rank] = out[k * cap : (k + 1) * cap, :]


def outer(sent, gots, g, mask, cap, first, owners):
    width = g.shape[0]
    rank = sum(p.shape[0] for p in sent) - width
    return pl.pallas_call(
        functools.partial(outer_kernel, first, owners, len(sent)),
        out_shape=[jax.ShapeDtypeStruct((cap, width * rank), F32)] * owners,
        compiler_params=params(24),
        cost_estimate=cost(8 * owners * cap * width * mask.shape[1] * rank, 0),
    )(g, mask, *sent, *gots)


def token_kernel(*refs):
    refs[-1][...] = jnp.zeros_like(refs[-1])


def token(arrays, flops):
    return pl.pallas_call(
        token_kernel,
        in_specs=[pl.BlockSpec(memory_space=pl.ANY)] * len(arrays),
        out_shape=jax.ShapeDtypeStruct((8, 128), F32),
        compiler_params=params(4),
        cost_estimate=cost(flops, 0),
    )(*arrays)


def after_kernel(block_ref, *refs):
    refs[-1][...] = block_ref[...]


def after(block, pieces):
    return pl.pallas_call(
        after_kernel,
        in_specs=[pl.BlockSpec(memory_space=pltpu.VMEM)]
        + [pl.BlockSpec(memory_space=pl.ANY)] * len(pieces),
        out_shape=jax.ShapeDtypeStruct(block.shape, F32),
        compiler_params=params(4),
        cost_estimate=cost(0, 0),
    )(block, *pieces)


def pool_kernel(*refs):
    refs[-1][...] = jnp.concatenate(halves(stack(refs[:-1])), axis=0)


def pool_halves(pieces):
    rows, feats = sum(piece.shape[0] for piece in pieces), pieces[0].shape[1]
    return pl.pallas_call(
        pool_kernel,
        out_shape=jax.ShapeDtypeStruct((2 * rows, feats), BF16),
        compiler_params=params(16),
        cost_estimate=cost(0, 0),
    )(*pieces)


def scores_of(rows, ids, pool, gaps):
    me = lax.axis_index("dp")
    high, low = halves(rows)
    slots, split, queries = rows.shape[0], pool.shape[0] // 2, ids.shape[1]
    products = mm(jnp.concatenate([high, low], axis=0), pool, NT)
    part = products[:slots, :split] + products[:slots, split:] + products[slots:, :split]
    held = split // len(gaps)
    if split == LANES and queries == LANES and len(gaps) > 1:
        spot = lax.rem(ids, held)
        for place, gap in enumerate(gaps):
            spot = spot + jnp.where(lax.div(ids, held) == (me ^ gap), place * held, 0)
        return jnp.take_along_axis(part, jnp.broadcast_to(spot, part.shape), axis=1)
    row = lax.broadcasted_iota(jnp.int32, (held, queries), 0)
    places = [row + ((me ^ gap) * held if len(gaps) > 1 else 0) for gap in gaps]
    hot = (jnp.concatenate(places, axis=0) == ids).astype(F32).astype(BF16)
    top, rest = halves(part)
    last = (part - top.astype(F32) - rest.astype(F32)).astype(BF16)
    picked = mm(jnp.concatenate([top, rest, last], axis=0), hot)
    return picked[:slots] + picked[slots : 2 * slots] + picked[2 * slots :]


def early_kernel(gaps, ids_ref, pool_ref, *refs):
    refs[-1][...] = scores_of(stack(refs[:-1]), ids_ref[...], pool_ref[...], gaps)


def score_early(ids_row, pool, rows, gaps):
    slots = sum(row.shape[0] for row in rows)
    return pl.pallas_call(
        functools.partial(early_kernel, gaps),
        out_shape=jax.ShapeDtypeStruct((slots, ids_row.shape[1]), F32),
        compiler_params=params(16),
        cost_estimate=cost(SCORE_FLOPS, 0),
    )(ids_row, pool, *rows)


def score_kernel(count, gaps, relative, ids_ref, pool_ref, early_ref, *refs):
    rows, scores_ref = refs[:count], refs[-1]
    me = lax.axis_index("dp")
    cap = rows[0].shape[0]
    total = scores_of(stack(rows), ids_ref[...], pool_ref[...], gaps)
    done = early_ref.shape[0] // cap if relative else 0
    for k in range(done + count):
        part = early_ref if k < done else total
        at = (k if k < done else k - done) * cap
        source = lax.rem(me - k + done + count, done + count) if relative else k
        scores_ref[pl.ds(pl.multiple_of(source * cap, cap), cap), :] = part[at : at + cap, :]


def score(ids_row, pool, early, rows, gaps, relative, tokens):
    slots = sum(row.shape[0] for row in rows) + (early.shape[0] if relative else 0)
    queries = ids_row.shape[1]
    return pl.pallas_call(
        functools.partial(score_kernel, len(rows), gaps, relative),
        in_specs=[pl.BlockSpec(memory_space=pltpu.VMEM)] * (3 + len(rows))
        + [pl.BlockSpec(memory_space=pl.ANY)] * len(tokens),
        out_shape=jax.ShapeDtypeStruct((slots, queries), F32),
        compiler_params=params(24),
        cost_estimate=cost(0, 0),
    )(ids_row, pool, early, *rows, *tokens)


def place_kernel(*refs):
    rows, store_ref = refs[:-1], refs[-1]
    me = lax.axis_index("dp")
    cap = rows[0].shape[0]
    for k, row in enumerate(rows):
        source = lax.rem(me - k + len(rows), len(rows))
        store_ref[pl.ds(pl.multiple_of(source * cap, cap), cap), :] = row[...]


def place(rows):
    slots, feats = rows[0].shape[0] * len(rows), rows[0].shape[1]
    return pl.pallas_call(
        place_kernel,
        out_shape=jax.ShapeDtypeStruct((slots, feats), F32),
        compiler_params=params(16),
        cost_estimate=cost(0, 8 * slots * feats),
    )(*rows)


def swap(x, axis, gap):
    return lax.ppermute(x, axis, [(i, i ^ gap) for i in range(lax.axis_size(axis))])


def shift(x, axis, by):
    size = lax.axis_size(axis)
    return lax.ppermute(x, axis, [(i, (i + by) % size) for i in range(size)])


def gather_pieces(piece):
    pieces, gaps = [piece], [0]
    bit = lax.axis_size("dp") // 2
    while bit > 1:
        pieces, gaps = pieces + [swap(p, "dp", bit) for p in pieces], gaps + [g ^ bit for g in gaps]
        bit //= 2
    return pieces, gaps


def local(
    activations, out_grads, proj_in, proj_out, doc_lengths, doc_owner, query_grads, query_ids
):
    tensor_size = lax.axis_size("tensor")
    data_size = lax.axis_size("dp")
    tokens = activations.shape[0]
    rank = proj_in.shape[1]
    width = rank // tensor_size
    docs = doc_owner.shape[0]
    cap = max(2, 2 * docs // data_size)
    direct = data_size <= MOST_DIRECT

    if direct:
        pieces, gaps = gather_pieces(query_grads)
        mate = swap(query_grads, "dp", 1)
        passed = [swap(piece, "dp", 1) for piece in pieces[1:]]
    else:
        pieces, gaps = [lax.all_gather(query_grads, "dp", axis=0, tiled=True)], [0]

    mask = dispatch_mask(doc_lengths, doc_owner.T, data_size, cap, activations.shape[0], direct)
    x = project_x(activations, proj_in.T, [token([], FIRST_FLOPS)])
    bit = tensor_size // 2
    x_got = swap(x, "tensor", bit)
    keep, send = project_g(out_grads, proj_out.T, width)
    early = [mask] + ([token(pieces[1:], EARLY_FLOPS)] if direct else [])
    own, gots = [x], [x_got, swap(send, "tensor", bit)]
    while bit > 1:
        bit //= 2
        keep, own = fold(rank, keep, own, gots, early)
        gots = [swap(part, "tensor", bit) for part in own]
    ids_row = query_ids[None, :]
    if direct:
        split = max(1, data_size // 2)
        soon = [outer(own, gots, keep, mask, cap, k, 1)[0] for k in range(split)]
        rows = [shift(block, "dp", k) for k, block in enumerate(soon, 1)]
        *sent, kept = outer(own, gots, keep, mask, cap, split, data_size - split)
        sent[-1] = after(sent[-1], [mate])
        rows = [kept, *rows, *(shift(block, "dp", k) for k, block in enumerate(sent, 1 + split))]
        store = place(rows)
        late = [token(rows[2:-1], LATE_FLOPS)]
        pool = pool_halves([*pieces, mate, *passed])
        gaps = [*gaps, *(g ^ 1 for g in gaps)]
        early = score_early(ids_row, pool, rows[:2], gaps)
        scores = score(ids_row, pool, early, rows[2:], gaps, True, late)
    else:
        blocks = outer(own, gots, keep, mask, cap, 0, data_size)
        store = lax.all_to_all(jnp.stack(blocks), "dp", 0, 0, tiled=True).reshape(-1, width * rank)
        pool = pool_halves(pieces)
        scores = score(ids_row, pool, ids_row, [store], gaps, False, [])
    bit = 1
    while bit < tensor_size:
        scores = scores + swap(scores, "tensor", bit)
        bit *= 2
    return store, scores * (1.0 / (rank * rank))


def solution(mesh):
    return jax.shard_map(
        local,
        mesh=mesh,
        in_specs=(
            P(("groups", "dp"), "tensor"),
            P(("groups", "dp"), "tensor"),
            P("tensor", None),
            P("tensor", None),
            P(("groups", "dp"), None),
            P(("groups", "dp"), None),
            P(("groups", "dp"), "tensor"),
            P("groups"),
        ),
        out_specs=(P(("groups", "dp"), "tensor"), P(("groups", "dp"), None)),
        check_vma=False,
    )
```

```python
import functools

import jax
import jax.numpy as jnp
from jax import lax
from jax.experimental import pallas as pl
from jax.experimental.pallas import tpu as pltpu
from jax.sharding import PartitionSpec as P

F32 = jnp.float32
BF16 = jnp.bfloat16
MIB = 1024 * 1024
NT = (((1,), (1,)), ((), ()))
MOST_DIRECT = 8
MOST_AT_ONCE = 4
GROUP = 16
ROWS = 16
LANES = 128
FIRST_FLOPS = 10 * 10**8
X_FLOPS = 6 * 10**8
MASK_FLOPS = 2 * 10**8
EARLY_FLOPS = 3 * 10**8
LATE_FLOPS = 10**8
SCORE_FLOPS = 0


def params(mib):
    return pltpu.CompilerParams(vmem_limit_bytes=mib * MIB)


def cost(flops, nbytes):
    return pl.CostEstimate(flops=flops, bytes_accessed=nbytes, transcendentals=0)


def halves(x):
    high = x.astype(BF16)
    return high, (x - high.astype(F32)).astype(BF16)


def mm(a, b, dims=(((1,), (0,)), ((), ()))):
    return lax.dot_general(a, b, dims, preferred_element_type=F32)


def slot_mask(owners, relative, cap, lengths, owner, slots, tokens):
    docs = lengths.shape[1]
    row = lax.broadcasted_iota(jnp.int32, (docs, docs), 0)
    col = lax.broadcasted_iota(jnp.int32, (docs, docs), 1)
    len_row = lengths.astype(F32)
    place_row = lax.rem(owner - lax.axis_index("dp") + 2 * owners - 1, owners) if relative else owner
    own_row = place_row.astype(F32)

    def column(values):
        return jnp.sum(jnp.where(row == col, values, 0.0), axis=1, keepdims=True)

    ends = jnp.sum(jnp.where(row <= col, column(len_row), 0.0), axis=0, keepdims=True)
    rank = jnp.sum(
        jnp.where((row < col) & (column(own_row) == own_row), 1.0, 0.0), axis=0, keepdims=True
    )
    slot = lax.broadcasted_iota(jnp.int32, (slots, docs), 0).astype(F32)
    hot = slot == own_row * cap + rank
    first = jnp.sum(jnp.where(hot, ends - len_row, 0.0), axis=1, keepdims=True)
    last = jnp.sum(jnp.where(hot, ends, 0.0), axis=1, keepdims=True)
    token = lax.broadcasted_iota(jnp.int32, (slots, tokens), 1).astype(F32)
    return jnp.where((token >= first) & (token < last), 1.0, 0.0).astype(BF16)


def mask_kernel(owners, relative, cap, lengths_ref, owner_ref, mask_ref):
    mask_ref[...] = slot_mask(owners, relative, cap, lengths_ref[...], owner_ref[...], *mask_ref.shape)


def dispatch_mask(lengths, owner_row, owners, cap, tokens, relative):
    return pl.pallas_call(
        functools.partial(mask_kernel, owners, relative, cap),
        out_shape=jax.ShapeDtypeStruct((owners * cap, tokens), BF16),
        compiler_params=params(8),
        cost_estimate=cost(MASK_FLOPS, 0),
    )(lengths, owner_row)


def put_projection(out_ref, proj_ref, act_ref):
    half = act_ref.shape[0] // 2
    out_ref[:, :half] = mm(proj_ref[...], act_ref[:half, :], NT)
    out_ref[:, half:] = mm(act_ref[half:, :], proj_ref[...], NT).T


def x_kernel(act_ref, proj_ref, *refs):
    put_projection(refs[-1], proj_ref, act_ref)


def project_x(act, in_t, tokens):
    return pl.pallas_call(
        x_kernel,
        in_specs=[pl.BlockSpec(memory_space=pltpu.VMEM)] * 2
        + [pl.BlockSpec(memory_space=pl.ANY)] * len(tokens),
        out_shape=jax.ShapeDtypeStruct((in_t.shape[0], act.shape[0]), F32),
        compiler_params=params(8),
        cost_estimate=cost(X_FLOPS, 0),
    )(act, in_t, *tokens)


def g_kernel(width, grad_ref, proj_ref, keep_ref, send_ref, full):
    put_projection(full, proj_ref, grad_ref)
    me = lax.axis_index("tensor")
    count = full.shape[0] // width
    for apart in range(count):
        block = pl.ds(pl.multiple_of((me ^ apart) * width, width), width)
        ref, spot = (keep_ref, apart) if apart < count // 2 else (send_ref, apart - count // 2)
        ref[spot * width : (spot + 1) * width, :] = full[block, :]


def project_g(grad, out_t, width):
    tokens, rank = grad.shape[0], out_t.shape[0]
    part = jax.ShapeDtypeStruct((rank // 2, tokens), F32)
    return pl.pallas_call(
        functools.partial(g_kernel, width),
        out_shape=[part, part],
        scratch_shapes=[pltpu.VMEM((rank, tokens), F32)],
        compiler_params=params(24),
        cost_estimate=cost(0, 0),
    )(grad, out_t)


def stack(refs):
    return jnp.concatenate([r[...] for r in refs], axis=0)


def fold_kernel(rank, owned, came, keep_ref, *refs):
    first_ref, second_ref, kept_ref = refs[-3:]
    got = stack(refs[owned : owned + came])
    total = keep_ref[...] + got[rank:]
    kept = kept_ref.shape[0]
    kept_ref[...] = total[:kept]
    x = stack(refs[:owned])[:rank] + got[:rank]
    sent = jnp.concatenate([x, total[kept:]], axis=0)
    cut = first_ref.shape[0]
    first_ref[...] = sent[:cut]
    second_ref[...] = sent[cut:]


def fold(rank, keep, own, gots, pieces):
    tokens = keep.shape[1]
    kept = keep.shape[0] // 2
    cut = (rank + kept) // 16 * 8
    *sent, keep = pl.pallas_call(
        functools.partial(fold_kernel, rank, len(own), len(gots)),
        in_specs=[pl.BlockSpec(memory_space=pltpu.VMEM)] * (1 + len(own) + len(gots))
        + [pl.BlockSpec(memory_space=pl.ANY)] * len(pieces),
        out_shape=[
            jax.ShapeDtypeStruct((rows, tokens), F32) for rows in (cut, rank + kept - cut, kept)
        ],
        compiler_params=params(16),
        cost_estimate=cost(0, 0),
    )(keep, *own, *gots, *pieces)
    return keep, sent


def outer_kernel(first, owners, sent, g_ref, mask_ref, *refs):
    blocks = refs[-owners:]
    width = g_ref.shape[0]
    own, got = stack(refs[:sent]), stack(refs[sent : 2 * sent])
    rank = got.shape[0] - width
    x_full = own[:rank] + got[:rank]
    g_full = g_ref[...] + got[rank:]
    x_high, x_low = halves(x_full)
    x_both = jnp.concatenate(
        [
            jnp.concatenate([x_high, x_high], axis=1),
            jnp.concatenate([x_low, jnp.zeros_like(x_low)], axis=1),
        ],
        axis=0,
    )
    g_high = g_full.astype(BF16).astype(F32)
    g_low = g_full - g_high
    cap = blocks[0].shape[0]
    slots = owners * cap
    mask = mask_ref[first * cap : first * cap + slots, :]
    tokens = mask.shape[1]

    def masked(row):
        wide = jnp.broadcast_to(row, (ROWS, tokens)).astype(BF16)
        return [mask[i : i + ROWS] * wide for i in range(0, slots, ROWS)]

    group = min(width, GROUP)
    for i in range(0, width, group):
        rows = [
            jnp.concatenate([m for j in range(i, i + group) for m in masked(g[j : j + 1])], axis=0)
            for g in (g_high, g_low)
        ]
        both = mm(jnp.concatenate(rows, axis=1), x_both, NT)
        columns = []
        for j in range(group):
            part = both[j * slots : (j + 1) * slots]
            columns.append(part[:, :rank] + part[:, rank:])
        out = jnp.concatenate(columns, axis=1)
        for k, block in enumerate(blocks):
            block[:, i * rank : (i + group) * rank] = out[k * cap : (k + 1) * cap, :]


def outer(sent, gots, g, mask, cap, first, owners):
    width = g.shape[0]
    rank = sum(p.shape[0] for p in sent) - width
    return pl.pallas_call(
        functools.partial(outer_kernel, first, owners, len(sent)),
        out_shape=[jax.ShapeDtypeStruct((cap, width * rank), F32)] * owners,
        compiler_params=params(24),
        cost_estimate=cost(8 * owners * cap * width * mask.shape[1] * rank, 0),
    )(g, mask, *sent, *gots)


def token_kernel(*refs):
    refs[-1][...] = jnp.zeros_like(refs[-1])


def token(arrays, flops):
    return pl.pallas_call(
        token_kernel,
        in_specs=[pl.BlockSpec(memory_space=pl.ANY)] * len(arrays),
        out_shape=jax.ShapeDtypeStruct((8, 128), F32),
        compiler_params=params(4),
        cost_estimate=cost(flops, 0),
    )(*arrays)


def after_kernel(block_ref, *refs):
    refs[-1][...] = block_ref[...]


def after(block, pieces):
    return pl.pallas_call(
        after_kernel,
        in_specs=[pl.BlockSpec(memory_space=pltpu.VMEM)]
        + [pl.BlockSpec(memory_space=pl.ANY)] * len(pieces),
        out_shape=jax.ShapeDtypeStruct(block.shape, F32),
        compiler_params=params(4),
        cost_estimate=cost(0, 0),
    )(block, *pieces)


def pool_kernel(*refs):
    refs[-1][...] = jnp.concatenate(halves(stack(refs[:-1])), axis=0)


def pool_halves(pieces):
    rows, feats = sum(piece.shape[0] for piece in pieces), pieces[0].shape[1]
    return pl.pallas_call(
        pool_kernel,
        out_shape=jax.ShapeDtypeStruct((2 * rows, feats), BF16),
        compiler_params=params(16),
        cost_estimate=cost(0, 0),
    )(*pieces)


def scores_of(rows, ids, pool, gaps):
    me = lax.axis_index("dp")
    high, low = halves(rows)
    slots, split, queries = rows.shape[0], pool.shape[0] // 2, ids.shape[1]
    products = mm(jnp.concatenate([high, low], axis=0), pool, NT)
    part = products[:slots, :split] + products[:slots, split:] + products[slots:, :split]
    held = split // len(gaps)
    if split == LANES and queries == LANES and len(gaps) > 1:
        spot = lax.rem(ids, held)
        for place, gap in enumerate(gaps):
            spot = spot + jnp.where(lax.div(ids, held) == (me ^ gap), place * held, 0)
        return jnp.take_along_axis(part, jnp.broadcast_to(spot, part.shape), axis=1)
    row = lax.broadcasted_iota(jnp.int32, (held, queries), 0)
    places = [row + ((me ^ gap) * held if len(gaps) > 1 else 0) for gap in gaps]
    hot = (jnp.concatenate(places, axis=0) == ids).astype(F32).astype(BF16)
    top, rest = halves(part)
    last = (part - top.astype(F32) - rest.astype(F32)).astype(BF16)
    picked = mm(jnp.concatenate([top, rest, last], axis=0), hot)
    return picked[:slots] + picked[slots : 2 * slots] + picked[2 * slots :]


def early_kernel(gaps, ids_ref, pool_ref, *refs):
    refs[-1][...] = scores_of(stack(refs[:-1]), ids_ref[...], pool_ref[...], gaps)


def score_early(ids_row, pool, rows, gaps):
    slots = sum(row.shape[0] for row in rows)
    return pl.pallas_call(
        functools.partial(early_kernel, gaps),
        out_shape=jax.ShapeDtypeStruct((slots, ids_row.shape[1]), F32),
        compiler_params=params(16),
        cost_estimate=cost(SCORE_FLOPS, 0),
    )(ids_row, pool, *rows)


def score_kernel(count, gaps, relative, ids_ref, pool_ref, early_ref, *refs):
    rows, scores_ref = refs[:count], refs[-1]
    me = lax.axis_index("dp")
    cap = rows[0].shape[0]
    total = scores_of(stack(rows), ids_ref[...], pool_ref[...], gaps)
    done = early_ref.shape[0] // cap if relative else 0
    for k in range(done + count):
        part = early_ref if k < done else total
        at = (k if k < done else k - done) * cap
        source = lax.rem(me - k + done + count, done + count) if relative else k
        scores_ref[pl.ds(pl.multiple_of(source * cap, cap), cap), :] = part[at : at + cap, :]


def score(ids_row, pool, early, rows, gaps, relative, tokens):
    slots = sum(row.shape[0] for row in rows) + (early.shape[0] if relative else 0)
    queries = ids_row.shape[1]
    return pl.pallas_call(
        functools.partial(score_kernel, len(rows), gaps, relative),
        in_specs=[pl.BlockSpec(memory_space=pltpu.VMEM)] * (3 + len(rows))
        + [pl.BlockSpec(memory_space=pl.ANY)] * len(tokens),
        out_shape=jax.ShapeDtypeStruct((slots, queries), F32),
        compiler_params=params(24),
        cost_estimate=cost(0, 0),
    )(ids_row, pool, early, *rows, *tokens)


def place_kernel(*refs):
    rows, store_ref = refs[:-1], refs[-1]
    me = lax.axis_index("dp")
    cap = rows[0].shape[0]
    for k, row in enumerate(rows):
        source = lax.rem(me - k + len(rows), len(rows))
        store_ref[pl.ds(pl.multiple_of(source * cap, cap), cap), :] = row[...]


def place(rows):
    slots, feats = rows[0].shape[0] * len(rows), rows[0].shape[1]
    return pl.pallas_call(
        place_kernel,
        out_shape=jax.ShapeDtypeStruct((slots, feats), F32),
        compiler_params=params(16),
        cost_estimate=cost(0, 8 * slots * feats),
    )(*rows)


def swap(x, axis, gap):
    return lax.ppermute(x, axis, [(i, i ^ gap) for i in range(lax.axis_size(axis))])


def shift(x, axis, by):
    size = lax.axis_size(axis)
    return lax.ppermute(x, axis, [(i, (i + by) % size) for i in range(size)])


def gather_pieces(piece):
    pieces, gaps = [piece], [0]
    bit = lax.axis_size("dp") // 2
    while bit > 1:
        pieces, gaps = pieces + [swap(p, "dp", bit) for p in pieces], gaps + [g ^ bit for g in gaps]
        bit //= 2
    return pieces, gaps


def local(
    activations, out_grads, proj_in, proj_out, doc_lengths, doc_owner, query_grads, query_ids
):
    tensor_size = lax.axis_size("tensor")
    data_size = lax.axis_size("dp")
    tokens = activations.shape[0]
    rank = proj_in.shape[1]
    width = rank // tensor_size
    docs = doc_owner.shape[0]
    cap = max(2, 2 * docs // data_size)
    direct = data_size <= MOST_DIRECT

    if direct:
        pieces, gaps = gather_pieces(query_grads)
        mate = swap(query_grads, "dp", 1)
        passed = [swap(piece, "dp", 1) for piece in pieces[1:]]
    else:
        pieces, gaps = [lax.all_gather(query_grads, "dp", axis=0, tiled=True)], [0]

    mask = dispatch_mask(doc_lengths, doc_owner.T, data_size, cap, activations.shape[0], direct)
    x = project_x(activations, proj_in.T, [token([], FIRST_FLOPS)])
    bit = tensor_size // 2
    x_got = swap(x, "tensor", bit)
    keep, send = project_g(out_grads, proj_out.T, width)
    early = [mask] + ([token(pieces[1:], EARLY_FLOPS)] if direct else [])
    own, gots = [x], [x_got, swap(send, "tensor", bit)]
    while bit > 1:
        bit //= 2
        keep, own = fold(rank, keep, own, gots, early)
        gots = [swap(part, "tensor", bit) for part in own]
    ids_row = query_ids[None, :]
    if direct:
        split = max(1, data_size // 2)
        soon = [outer(own, gots, keep, mask, cap, k, 1)[0] for k in range(split)]
        rows = [shift(block, "dp", k) for k, block in enumerate(soon, 1)]
        *sent, kept = outer(own, gots, keep, mask, cap, split, data_size - split)
        sent[-1] = after(sent[-1], [mate, *passed])
        rows = [kept, *rows, *(shift(block, "dp", k) for k, block in enumerate(sent, 1 + split))]
        store = place(rows)
        late = [token(rows[2:-1], LATE_FLOPS)]
        pool = pool_halves([*pieces, mate, *passed])
        gaps = [*gaps, *(g ^ 1 for g in gaps)]
        early = score_early(ids_row, pool, rows[:2], gaps)
        scores = score(ids_row, pool, early, rows[2:], gaps, True, late)
    else:
        blocks = outer(own, gots, keep, mask, cap, 0, data_size)
        store = lax.all_to_all(jnp.stack(blocks), "dp", 0, 0, tiled=True).reshape(-1, width * rank)
        pool = pool_halves(pieces)
        scores = score(ids_row, pool, ids_row, [store], gaps, False, [])
    if tensor_size <= MOST_AT_ONCE:
        gots = {gap: swap(scores, "tensor", gap) for gap in range(tensor_size - 1, 0, -1)}
        parts = [scores] + [gots[gap] for gap in range(1, tensor_size)]
        while len(parts) > 1:
            parts = [one + two for one, two in zip(parts[::2], parts[1::2])]
        scores = parts[0]
    else:
        bit = 1
        while bit < tensor_size:
            scores = scores + swap(scores, "tensor", bit)
            bit *= 2
    return store, scores * (1.0 / (rank * rank))


def solution(mesh):
    return jax.shard_map(
        local,
        mesh=mesh,
        in_specs=(
            P(("groups", "dp"), "tensor"),
            P(("groups", "dp"), "tensor"),
            P("tensor", None),
            P("tensor", None),
            P(("groups", "dp"), None),
            P(("groups", "dp"), None),
            P(("groups", "dp"), "tensor"),
            P("groups"),
        ),
        out_specs=(P(("groups", "dp"), "tensor"), P(("groups", "dp"), None)),
        check_vma=False,
    )
```

```python
import functools

import jax
import jax.numpy as jnp
from jax import lax
from jax.experimental import pallas as pl
from jax.experimental.pallas import tpu as pltpu
from jax.sharding import PartitionSpec as P

F32 = jnp.float32
BF16 = jnp.bfloat16
MIB = 1024 * 1024
NT = (((1,), (1,)), ((), ()))
MOST_DIRECT = 8
MOST_AT_ONCE = 4
GROUP = 8
ROWS = 16
LANES = 128
FIRST_FLOPS = 10 * 10**8
X_FLOPS = 6 * 10**8
MASK_FLOPS = 2 * 10**8
EARLY_FLOPS = 3 * 10**8
LATE_FLOPS = 10**8
SCORE_FLOPS = 0


def params(mib):
    return pltpu.CompilerParams(vmem_limit_bytes=mib * MIB)


def cost(flops, nbytes):
    return pl.CostEstimate(flops=flops, bytes_accessed=nbytes, transcendentals=0)


def halves(x):
    high = x.astype(BF16)
    return high, (x - high.astype(F32)).astype(BF16)


def mm(a, b, dims=(((1,), (0,)), ((), ()))):
    return lax.dot_general(a, b, dims, preferred_element_type=F32)


def slot_mask(owners, relative, cap, lengths, owner, slots, tokens):
    docs = lengths.shape[1]
    row = lax.broadcasted_iota(jnp.int32, (docs, docs), 0)
    col = lax.broadcasted_iota(jnp.int32, (docs, docs), 1)
    len_row = lengths.astype(F32)
    place_row = lax.rem(owner - lax.axis_index("dp") + 2 * owners - 1, owners) if relative else owner
    own_row = place_row.astype(F32)

    def column(values):
        return jnp.sum(jnp.where(row == col, values, 0.0), axis=1, keepdims=True)

    ends = jnp.sum(jnp.where(row <= col, column(len_row), 0.0), axis=0, keepdims=True)
    rank = jnp.sum(
        jnp.where((row < col) & (column(own_row) == own_row), 1.0, 0.0), axis=0, keepdims=True
    )
    slot = lax.broadcasted_iota(jnp.int32, (slots, docs), 0).astype(F32)
    hot = slot == own_row * cap + rank
    first = jnp.sum(jnp.where(hot, ends - len_row, 0.0), axis=1, keepdims=True)
    last = jnp.sum(jnp.where(hot, ends, 0.0), axis=1, keepdims=True)
    token = lax.broadcasted_iota(jnp.int32, (slots, tokens), 1).astype(F32)
    return jnp.where((token >= first) & (token < last), 1.0, 0.0).astype(BF16)


def mask_kernel(owners, relative, cap, lengths_ref, owner_ref, mask_ref):
    mask_ref[...] = slot_mask(owners, relative, cap, lengths_ref[...], owner_ref[...], *mask_ref.shape)


def dispatch_mask(lengths, owner_row, owners, cap, tokens, relative):
    return pl.pallas_call(
        functools.partial(mask_kernel, owners, relative, cap),
        out_shape=jax.ShapeDtypeStruct((owners * cap, tokens), BF16),
        compiler_params=params(8),
        cost_estimate=cost(MASK_FLOPS, 0),
    )(lengths, owner_row)


def put_projection(out_ref, proj_ref, act_ref):
    half = act_ref.shape[0] // 2
    out_ref[:, :half] = mm(proj_ref[...], act_ref[:half, :], NT)
    out_ref[:, half:] = mm(act_ref[half:, :], proj_ref[...], NT).T


def x_kernel(act_ref, proj_ref, *refs):
    put_projection(refs[-1], proj_ref, act_ref)


def project_x(act, in_t, tokens):
    return pl.pallas_call(
        x_kernel,
        in_specs=[pl.BlockSpec(memory_space=pltpu.VMEM)] * 2
        + [pl.BlockSpec(memory_space=pl.ANY)] * len(tokens),
        out_shape=jax.ShapeDtypeStruct((in_t.shape[0], act.shape[0]), F32),
        compiler_params=params(8),
        cost_estimate=cost(X_FLOPS, 0),
    )(act, in_t, *tokens)


def g_kernel(width, grad_ref, proj_ref, keep_ref, send_ref, full):
    put_projection(full, proj_ref, grad_ref)
    me = lax.axis_index("tensor")
    count = full.shape[0] // width
    for apart in range(count):
        block = pl.ds(pl.multiple_of((me ^ apart) * width, width), width)
        ref, spot = (keep_ref, apart) if apart < count // 2 else (send_ref, apart - count // 2)
        ref[spot * width : (spot + 1) * width, :] = full[block, :]


def project_g(grad, out_t, width):
    tokens, rank = grad.shape[0], out_t.shape[0]
    part = jax.ShapeDtypeStruct((rank // 2, tokens), F32)
    return pl.pallas_call(
        functools.partial(g_kernel, width),
        out_shape=[part, part],
        scratch_shapes=[pltpu.VMEM((rank, tokens), F32)],
        compiler_params=params(24),
        cost_estimate=cost(0, 0),
    )(grad, out_t)


def stack(refs):
    return jnp.concatenate([r[...] for r in refs], axis=0)


def fold_kernel(rank, owned, came, keep_ref, *refs):
    first_ref, second_ref, kept_ref = refs[-3:]
    got = stack(refs[owned : owned + came])
    total = keep_ref[...] + got[rank:]
    kept = kept_ref.shape[0]
    kept_ref[...] = total[:kept]
    x = stack(refs[:owned])[:rank] + got[:rank]
    sent = jnp.concatenate([x, total[kept:]], axis=0)
    cut = first_ref.shape[0]
    first_ref[...] = sent[:cut]
    second_ref[...] = sent[cut:]


def fold(rank, keep, own, gots, pieces):
    tokens = keep.shape[1]
    kept = keep.shape[0] // 2
    cut = (rank + kept) // 16 * 8
    *sent, keep = pl.pallas_call(
        functools.partial(fold_kernel, rank, len(own), len(gots)),
        in_specs=[pl.BlockSpec(memory_space=pltpu.VMEM)] * (1 + len(own) + len(gots))
        + [pl.BlockSpec(memory_space=pl.ANY)] * len(pieces),
        out_shape=[
            jax.ShapeDtypeStruct((rows, tokens), F32) for rows in (cut, rank + kept - cut, kept)
        ],
        compiler_params=params(16),
        cost_estimate=cost(0, 0),
    )(keep, *own, *gots, *pieces)
    return keep, sent


def outer_kernel(first, owners, sent, g_ref, mask_ref, *refs):
    blocks = refs[-owners:]
    width = g_ref.shape[0]
    own, got = stack(refs[:sent]), stack(refs[sent : 2 * sent])
    rank = got.shape[0] - width
    x_full = own[:rank] + got[:rank]
    g_full = g_ref[...] + got[rank:]
    x_high, x_low = halves(x_full)
    x_both = jnp.concatenate(
        [
            jnp.concatenate([x_high, x_high], axis=1),
            jnp.concatenate([x_low, jnp.zeros_like(x_low)], axis=1),
        ],
        axis=0,
    )
    g_high = g_full.astype(BF16).astype(F32)
    g_low = g_full - g_high
    cap = blocks[0].shape[0]
    slots = owners * cap
    mask = mask_ref[first * cap : first * cap + slots, :]
    tokens = mask.shape[1]

    def masked(row):
        wide = jnp.broadcast_to(row, (ROWS, tokens)).astype(BF16)
        return [mask[i : i + ROWS] * wide for i in range(0, slots, ROWS)]

    group = min(width, GROUP)
    for i in range(0, width, group):
        rows = [
            jnp.concatenate([m for j in range(i, i + group) for m in masked(g[j : j + 1])], axis=0)
            for g in (g_high, g_low)
        ]
        both = mm(jnp.concatenate(rows, axis=1), x_both, NT)
        columns = []
        for j in range(group):
            part = both[j * slots : (j + 1) * slots]
            columns.append(part[:, :rank] + part[:, rank:])
        out = jnp.concatenate(columns, axis=1)
        for k, block in enumerate(blocks):
            block[:, i * rank : (i + group) * rank] = out[k * cap : (k + 1) * cap, :]


def outer(sent, gots, g, mask, cap, first, owners):
    width = g.shape[0]
    rank = sum(p.shape[0] for p in sent) - width
    return pl.pallas_call(
        functools.partial(outer_kernel, first, owners, len(sent)),
        out_shape=[jax.ShapeDtypeStruct((cap, width * rank), F32)] * owners,
        compiler_params=params(24),
        cost_estimate=cost(8 * owners * cap * width * mask.shape[1] * rank, 0),
    )(g, mask, *sent, *gots)


def token_kernel(*refs):
    refs[-1][...] = jnp.zeros_like(refs[-1])


def token(arrays, flops):
    return pl.pallas_call(
        token_kernel,
        in_specs=[pl.BlockSpec(memory_space=pl.ANY)] * len(arrays),
        out_shape=jax.ShapeDtypeStruct((8, 128), F32),
        compiler_params=params(4),
        cost_estimate=cost(flops, 0),
    )(*arrays)


def after_kernel(block_ref, *refs):
    refs[-1][...] = block_ref[...]


def after(block, pieces):
    return pl.pallas_call(
        after_kernel,
        in_specs=[pl.BlockSpec(memory_space=pltpu.VMEM)]
        + [pl.BlockSpec(memory_space=pl.ANY)] * len(pieces),
        out_shape=jax.ShapeDtypeStruct(block.shape, F32),
        compiler_params=params(4),
        cost_estimate=cost(0, 0),
    )(block, *pieces)


def pool_kernel(*refs):
    refs[-1][...] = jnp.concatenate(halves(stack(refs[:-1])), axis=0)


def pool_halves(pieces):
    rows, feats = sum(piece.shape[0] for piece in pieces), pieces[0].shape[1]
    return pl.pallas_call(
        pool_kernel,
        out_shape=jax.ShapeDtypeStruct((2 * rows, feats), BF16),
        compiler_params=params(16),
        cost_estimate=cost(0, 0),
    )(*pieces)


def scores_of(rows, ids, pool, gaps):
    me = lax.axis_index("dp")
    high, low = halves(rows)
    slots, split, queries = rows.shape[0], pool.shape[0] // 2, ids.shape[1]
    products = mm(jnp.concatenate([high, low], axis=0), pool, NT)
    part = products[:slots, :split] + products[:slots, split:] + products[slots:, :split]
    held = split // len(gaps)
    if split == LANES and queries == LANES and len(gaps) > 1:
        spot = lax.rem(ids, held)
        for place, gap in enumerate(gaps):
            spot = spot + jnp.where(lax.div(ids, held) == (me ^ gap), place * held, 0)
        return jnp.take_along_axis(part, jnp.broadcast_to(spot, part.shape), axis=1)
    row = lax.broadcasted_iota(jnp.int32, (held, queries), 0)
    places = [row + ((me ^ gap) * held if len(gaps) > 1 else 0) for gap in gaps]
    hot = (jnp.concatenate(places, axis=0) == ids).astype(F32).astype(BF16)
    top, rest = halves(part)
    last = (part - top.astype(F32) - rest.astype(F32)).astype(BF16)
    picked = mm(jnp.concatenate([top, rest, last], axis=0), hot)
    return picked[:slots] + picked[slots : 2 * slots] + picked[2 * slots :]


def early_kernel(gaps, ids_ref, pool_ref, *refs):
    refs[-1][...] = scores_of(stack(refs[:-1]), ids_ref[...], pool_ref[...], gaps)


def score_early(ids_row, pool, rows, gaps):
    slots = sum(row.shape[0] for row in rows)
    return pl.pallas_call(
        functools.partial(early_kernel, gaps),
        out_shape=jax.ShapeDtypeStruct((slots, ids_row.shape[1]), F32),
        compiler_params=params(16),
        cost_estimate=cost(SCORE_FLOPS, 0),
    )(ids_row, pool, *rows)


def score_kernel(count, gaps, relative, ids_ref, pool_ref, early_ref, *refs):
    rows, scores_ref = refs[:count], refs[-1]
    me = lax.axis_index("dp")
    cap = rows[0].shape[0]
    total = scores_of(stack(rows), ids_ref[...], pool_ref[...], gaps)
    done = early_ref.shape[0] // cap if relative else 0
    for k in range(done + count):
        part = early_ref if k < done else total
        at = (k if k < done else k - done) * cap
        source = lax.rem(me - k + done + count, done + count) if relative else k
        scores_ref[pl.ds(pl.multiple_of(source * cap, cap), cap), :] = part[at : at + cap, :]


def score(ids_row, pool, early, rows, gaps, relative, tokens):
    slots = sum(row.shape[0] for row in rows) + (early.shape[0] if relative else 0)
    queries = ids_row.shape[1]
    return pl.pallas_call(
        functools.partial(score_kernel, len(rows), gaps, relative),
        in_specs=[pl.BlockSpec(memory_space=pltpu.VMEM)] * (3 + len(rows))
        + [pl.BlockSpec(memory_space=pl.ANY)] * len(tokens),
        out_shape=jax.ShapeDtypeStruct((slots, queries), F32),
        compiler_params=params(24),
        cost_estimate=cost(0, 0),
    )(ids_row, pool, early, *rows, *tokens)


def place_kernel(*refs):
    rows, store_ref = refs[:-1], refs[-1]
    me = lax.axis_index("dp")
    cap = rows[0].shape[0]
    for k, row in enumerate(rows):
        source = lax.rem(me - k + len(rows), len(rows))
        store_ref[pl.ds(pl.multiple_of(source * cap, cap), cap), :] = row[...]


def place(rows):
    slots, feats = rows[0].shape[0] * len(rows), rows[0].shape[1]
    return pl.pallas_call(
        place_kernel,
        out_shape=jax.ShapeDtypeStruct((slots, feats), F32),
        compiler_params=params(16),
        cost_estimate=cost(0, 8 * slots * feats),
    )(*rows)


def swap(x, axis, gap):
    return lax.ppermute(x, axis, [(i, i ^ gap) for i in range(lax.axis_size(axis))])


def shift(x, axis, by):
    size = lax.axis_size(axis)
    return lax.ppermute(x, axis, [(i, (i + by) % size) for i in range(size)])


def gather_pieces(piece):
    pieces, gaps = [piece], [0]
    bit = lax.axis_size("dp") // 2
    while bit > 1:
        pieces, gaps = pieces + [swap(p, "dp", bit) for p in pieces], gaps + [g ^ bit for g in gaps]
        bit //= 2
    return pieces, gaps


def local(
    activations, out_grads, proj_in, proj_out, doc_lengths, doc_owner, query_grads, query_ids
):
    tensor_size = lax.axis_size("tensor")
    data_size = lax.axis_size("dp")
    tokens = activations.shape[0]
    rank = proj_in.shape[1]
    width = rank // tensor_size
    docs = doc_owner.shape[0]
    cap = max(2, 2 * docs // data_size)
    direct = data_size <= MOST_DIRECT

    if direct:
        pieces, gaps = gather_pieces(query_grads)
        mate = swap(query_grads, "dp", 1)
        passed = [swap(piece, "dp", 1) for piece in pieces[1:]]
    else:
        pieces, gaps = [lax.all_gather(query_grads, "dp", axis=0, tiled=True)], [0]

    mask = dispatch_mask(doc_lengths, doc_owner.T, data_size, cap, activations.shape[0], direct)
    x = project_x(activations, proj_in.T, [token([], FIRST_FLOPS)])
    bit = tensor_size // 2
    x_got = swap(x, "tensor", bit)
    keep, send = project_g(out_grads, proj_out.T, width)
    early = [mask] + ([token(pieces[1:], EARLY_FLOPS)] if direct else [])
    own, gots = [x], [x_got, swap(send, "tensor", bit)]
    while bit > 1:
        bit //= 2
        keep, own = fold(rank, keep, own, gots, early)
        gots = [swap(part, "tensor", bit) for part in own]
    ids_row = query_ids[None, :]
    if direct:
        split = max(1, data_size // 2)
        soon = outer(own, gots, keep, mask, cap, 0, split)
        rows = [shift(block, "dp", k) for k, block in enumerate(soon, 1)]
        *sent, kept = outer(own, gots, keep, mask, cap, split, data_size - split)
        sent[-1] = after(sent[-1], [mate, *passed])
        rows = [kept, *rows, *(shift(block, "dp", k) for k, block in enumerate(sent, 1 + split))]
        store = place(rows)
        late = [token(rows[2:-1], LATE_FLOPS)]
        pool = pool_halves([*pieces, mate, *passed])
        gaps = [*gaps, *(g ^ 1 for g in gaps)]
        early = score_early(ids_row, pool, rows[:2], gaps)
        scores = score(ids_row, pool, early, rows[2:], gaps, True, late)
    else:
        blocks = outer(own, gots, keep, mask, cap, 0, data_size)
        store = lax.all_to_all(jnp.stack(blocks), "dp", 0, 0, tiled=True).reshape(-1, width * rank)
        pool = pool_halves(pieces)
        scores = score(ids_row, pool, ids_row, [store], gaps, False, [])
    if tensor_size <= MOST_AT_ONCE:
        gots = {gap: swap(scores, "tensor", gap) for gap in range(tensor_size - 1, 0, -1)}
        parts = [scores] + [gots[gap] for gap in range(1, tensor_size)]
        while len(parts) > 1:
            parts = [one + two for one, two in zip(parts[::2], parts[1::2])]
        scores = parts[0]
    else:
        bit = 1
        while bit < tensor_size:
            scores = scores + swap(scores, "tensor", bit)
            bit *= 2
    return store, scores * (1.0 / (rank * rank))


def solution(mesh):
    return jax.shard_map(
        local,
        mesh=mesh,
        in_specs=(
            P(("groups", "dp"), "tensor"),
            P(("groups", "dp"), "tensor"),
            P("tensor", None),
            P("tensor", None),
            P(("groups", "dp"), None),
            P(("groups", "dp"), None),
            P(("groups", "dp"), "tensor"),
            P("groups"),
        ),
        out_specs=(P(("groups", "dp"), "tensor"), P(("groups", "dp"), None)),
        check_vma=False,
    )
```
